32 devices in a mesh: sec: 2 (over core), dom: 8 (over z, y), lev: 2 (over x).
Axes of the slice: x: 2, y: 2, z: 4, core: 2. Of those that a mesh axis runs over, the one named last changes fastest.
Arguments:
- sections: float32 [2, 12, 90, 2048], P('sec', None, 'lev', 'dom'), may hold values from -6 to 6
- neighbours: int32 [3, 2048], P(None, 'dom'), may hold values from 0 to 767, as said below
- edge_weight: float32 [3, 2048], P(None, 'dom'), may hold values from 0.05 to 0.3
- field_diff: float32 [12], replicated, may hold values from 0.3 to 1
- vert_coef: float32 [90, 2048], P('lev', 'dom'), may hold values from 1 to 300
- relax_rate: float32 [12], replicated, may hold values from 0.05 to 0.5
- precip_mask: int32 [2, 2048], P(None, 'dom'), may hold values from 0 to 1, as said below
Outputs:
- final: float32 [2, 12, 90, 2048], P('sec', None, 'lev', 'dom')
The draws below stay inside these ranges and needn't reach their ends.
Inputs may be any that keep to these rules, and one draw needn't show every extreme that they name: neighbours[j, c] is a position p in the block of 256 cells holding c, extended by the last 256 cells of the block before and the first 256 of the block after (the cell order closes around the sphere); p names the cell given by cell_neighbour and differs from the position of c by 1 to 256. `precip_mask`: for every step and every block b below 4, the blocks of 256 cells numbered b and b + 4 hold together at most 256 precipitating columns; in every step one block precipitates in all its columns.
All inputs are finite; a program needn't handle non-finite values.
Results may differ from the reference program's by a relative error of at most 0.0031.
Values may be sent and summed in bfloat16 or wider, within the bound.
No kernel may reach another device: no remote copies, remote signals or barrier semaphores. Data moves between devices by JAX's collectives and lax.ppermute only.
A program may use at most 64 MiB of HBM per device.

```python
import math
import jax
import jax.numpy as jnp
from jax import lax

COL_DEV = 256
LEV = 90
NV = 12
HALO = 256
STEPS = 2
COLS = 2048


def draw_neighbours(key, part):
    grid_shape = (3, COLS)
    key_size, key_sign = jax.random.split(jax.random.fold_in(key, 11))
    magnitude = jax.random.randint(key_size, grid_shape, 1, HALO + 1)
    sign_pick = jax.random.randint(key_sign, grid_shape, 0, 2) * 2 - 1
    offset = magnitude * sign_pick
    local_cell = jnp.arange(COLS, dtype=jnp.int32) % COL_DEV
    row_index = jnp.arange(3, dtype=jnp.int32)[:, None]
    offset = jnp.where((row_index == 0) & (local_cell[None] == 0), -HALO, offset)
    offset = jnp.where((row_index == 0) & (local_cell[None] == COL_DEV - 1), HALO, offset)
    return (local_cell[None] + HALO + offset).astype(jnp.int32)


def draw_precip_mask(key, part):
    blocks = COLS // COL_DEV
    pairs = blocks // 2
    base = jax.random.fold_in(key, 23)
    key_list = [jax.random.fold_in(base, number) for number in range(7)]
    pair_shape = (STEPS, pairs)
    storm = jax.random.randint(key_list[0], pair_shape, 0, 3) == 0
    total = jnp.where(storm, COL_DEV, jax.random.randint(key_list[1], pair_shape, 0, COL_DEV // 2 + 1))
    light_share = jax.random.randint(key_list[2], pair_shape, 0, total + 1)
    heavy_share = jnp.where(storm, jax.random.randint(key_list[3], pair_shape, 3 * COL_DEV // 4, COL_DEV + 1), light_share)
    forced = jax.random.randint(key_list[4], (STEPS, 1), 0, pairs)
    is_forced = jnp.arange(pairs, dtype=jnp.int32)[None] == forced
    total = jnp.where(is_forced, COL_DEV, total)
    heavy_share = jnp.where(is_forced, COL_DEV, heavy_share)
    side = jax.random.randint(key_list[5], pair_shape, 0, 2) == 1
    first_count = jnp.where(side, heavy_share, total - heavy_share)
    second_count = total - first_count
    counts = jnp.concatenate([first_count, second_count], axis=1)
    scores = jax.random.randint(key_list[6], (STEPS, blocks, COL_DEV), 0, 2 ** 19) * COL_DEV + jnp.arange(COL_DEV, dtype=jnp.int32)
    ranking = jnp.argsort(jnp.argsort(scores, axis=-1), axis=-1)
    chosen = (ranking < counts[:, :, None]).astype(jnp.int32)
    return chosen.reshape(STEPS, COLS)


def levels(own_key, extent, pieces, least, top_value):
    def one(axis_at, shards_of):
        draws = jax.random.uniform(jax.random.fold_in(jax.random.fold_in(own_key, 6), axis_at), (shards_of,), jnp.float32, least / len(pieces), top_value / len(pieces))
        return jnp.repeat(jnp.exp(draws), extent[axis_at] // shards_of).reshape((-1,) + (1,) * (len(extent) - axis_at - 1))

    factor_of = one(*pieces[0])
    for cut in pieces[1:]:
        factor_of = factor_of * one(*cut)
    return factor_of


def noise(rng, shape, scale, most, cuts=(), kind=jnp.bfloat16):
    entries = jax.random.normal(rng, shape, jnp.float32) * scale
    if len(cuts) > 0:
        entries = levels(rng, shape, cuts, -0.22, 0.18) * entries
    return jnp.clip(entries, min=-most, max=most).astype(kind)


def setup_inputs(seed: int = 0) -> dict:
    streams_of = jax.random.split(jax.random.key(seed), 8)
    return {
        "sections": noise(streams_of[0], (2, NV, LEV, COLS), 1.0, 6.0, ((0, 2), (2, 2), (3, 8)), jnp.float32),
        "neighbours": draw_neighbours(jax.random.fold_in(streams_of[7], 71), 0),
        "edge_weight": jnp.clip(jnp.exp(math.log(0.3) - 1.7917595 * jax.random.uniform(streams_of[2], (3, COLS), jnp.float32) ** levels(streams_of[2], (3, COLS), ((1, 8),), -0.2, 0.2)), 0.05, 0.3),
        "field_diff": jnp.clip(jnp.exp(jax.random.uniform(streams_of[3], (NV,), jnp.float32, math.log(0.3), math.log(1.0))), 0.3, 1.0),
        "vert_coef": jnp.clip(jnp.exp(math.log(300.0) - 5.7037825 * jax.random.uniform(streams_of[4], (LEV, COLS), jnp.float32) ** levels(streams_of[4], (LEV, COLS), ((0, 2), (1, 8)), -0.2, 0.2)), 1.0, 300.0),
        "relax_rate": jnp.clip(jnp.exp(jax.random.uniform(streams_of[5], (NV,), jnp.float32, math.log(0.05), math.log(0.5))), 0.05, 0.5),
        "precip_mask": draw_precip_mask(jax.random.fold_in(streams_of[7], 71), 0),
    }


def column_coefficients(kappa):
    zero_row = jnp.zeros((1, kappa.shape[1]), jnp.float32)
    above = jnp.concatenate([zero_row, kappa[:-1]], axis=0)
    lower = -above
    diagonal = 1.0 + above + kappa
    upper = jnp.concatenate([-kappa[:-1], zero_row], axis=0)
    return lower, diagonal, upper


def thomas(lower, diagonal, upper, right):
    def forward(carry, row):
        prev_ratio, prev_value = carry
        lower_k, diag_k, upper_k, right_k = row
        denom = diag_k - lower_k * prev_ratio
        new_ratio = upper_k / denom
        new_value = (right_k - lower_k[None] * prev_value) / denom[None]
        return (new_ratio, new_value), (new_ratio, new_value)

    start = (jnp.zeros(right.shape[2:], jnp.float32), jnp.zeros(right.shape[1:], jnp.float32))
    _, (ratios, values) = lax.scan(forward, start, (lower, diagonal, upper, right))

    def backward(after, row):
        ratio_k, value_k = row
        result = value_k - ratio_k[None] * after
        return result, result

    _, solution = lax.scan(backward, jnp.zeros(right.shape[1:], jnp.float32), (ratios, values), reverse=True)
    return solution


def solve_column(right, kappa):
    lower, diagonal, upper = column_coefficients(kappa)
    return jnp.swapaxes(thomas(lower, diagonal, upper, jnp.swapaxes(right, 0, 1)), 0, 1)


def microphysics(moist):
    theta, vapour, cloud, rain = moist[0], moist[1], moist[2], moist[3]
    saturation = 0.6 * jnp.exp(0.25 * theta)
    condense = 0.5 * jnp.tanh(vapour - saturation)
    autoconv = 0.4 * cloud * cloud / (1.0 + cloud * cloud)
    evaporate = 0.3 * rain * rain / (1.0 + rain * rain) * jax.nn.sigmoid(saturation - vapour)
    return jnp.stack([2.5 * (condense - evaporate), evaporate - condense, condense - autoconv, autoconv - evaporate])


def reference(sections, neighbours, edge_weight, field_diff, vert_coef, relax_rate, precip_mask):
    cell = jnp.arange(COLS, dtype=jnp.int32)
    cell_neighbour = (((cell - cell % COL_DEV)[None] + neighbours - HALO) % COLS).astype(jnp.int32)
    state = sections[0]
    tend = sections[1]
    for step_index in range(STEPS):
        state_b = lax.optimization_barrier(state.astype(jnp.bfloat16))
        lagged_b = lax.optimization_barrier(tend.astype(jnp.bfloat16))
        total = jnp.zeros_like(state)
        for edge in range(3):
            total = total + edge_weight[edge] * (jnp.take(state, cell_neighbour[edge], axis=2) - state)
        smoothed = state + field_diff[:, None, None] * total
        solved = solve_column(smoothed[0:2], vert_coef)
        new_state = jnp.concatenate([solved, smoothed[2:]], axis=0) + lagged_b.astype(jnp.float32)
        physics_in = state_b.astype(jnp.float32)
        clear = -relax_rate[:, None, None] * physics_in
        micro = microphysics(physics_in[1:5])
        moist = jnp.where(precip_mask[step_index][None, None] == 1, clear[1:5] + micro, clear[1:5])
        tend = jnp.concatenate([clear[0:1], moist, clear[5:]], axis=0)
        state = new_state
    return jnp.stack([state, tend])
```

```python
import functools
import jax
import jax.numpy as jnp
from jax import lax
from jax.experimental import pallas as pl
from jax.experimental.pallas import tpu as pltpu
from jax.sharding import PartitionSpec as P

AXES = ("sec", "dom", "lev")
SOLVED = 2
EDGES = 3
LANES8 = 8
LANES = 128
VMEM = pl.BlockSpec(memory_space=pltpu.VMEM)
SMEM = pl.BlockSpec(memory_space=pltpu.SMEM)
F32 = jnp.float32
BF16 = jnp.bfloat16


def up(count, unit):
    return -(-count // unit) * unit


def route(array, dom_step, swap_lev, pairs):
    doms, levs = lax.axis_size("dom"), lax.axis_size("lev")
    place = lambda s, d, v: (s * doms + d) * levs + v
    table = [
        (place(a, d, v), place(b, (d + step) % doms, v ^ flip))
        for a, b, step, flip in [(a, b, dom_step, swap_lev) for a, b in pairs]
        for d in range(doms)
        for v in range(levs)
    ]
    return lax.ppermute(array, AXES, table)


def tendency_into(out_ref, state, mask, relax_ref):
    fields = out_ref.shape[0]
    rounded = lambda f: state(f).astype(BF16).astype(F32)
    theta, vapour, cloud, rain = rounded(1), rounded(2), rounded(3), rounded(4)
    saturation = 0.6 * jnp.exp(0.25 * theta)
    condense = 0.5 * jnp.tanh(vapour - saturation)
    autoconv = 0.4 * cloud * cloud / (1.0 + cloud * cloud)
    evaporate = 0.3 * rain * rain / (1.0 + rain * rain) * jax.nn.sigmoid(saturation - vapour)
    micro = {
        1: 2.5 * (condense - evaporate),
        2: evaporate - condense,
        3: condense - autoconv,
        4: autoconv - evaporate,
    }
    for f in range(fields):
        clear = -relax_ref[f] * rounded(f)
        if f in micro:
            clear = jnp.where(mask == 1, clear + micro[f], clear)
        out_ref[f] = clear.astype(out_ref.dtype)


def prepare_kernel(mine_ref, nbr_ref, weight_ref, mask_ref, relax_ref, gather_ref, lagged_ref):
    width = nbr_ref.shape[1]
    reach = gather_ref.shape[0]
    rows = 64
    for start in range(0, reach, rows):
        place = lax.broadcasted_iota(jnp.int32, (rows, width), 0) + start
        total = jnp.zeros((rows, width), F32)
        for edge in range(EDGES):
            total = total + jnp.where(place == nbr_ref[edge : edge + 1, :], weight_ref[edge : edge + 1, :], 0.0)
        high = total.astype(BF16)
        gather_ref[start : start + rows, 0:width] = high
        gather_ref[start : start + rows, width : 2 * width] = (total - high.astype(F32)).astype(BF16)

    @pl.when(lax.axis_index("sec") == 0)
    def _():
        tendency_into(lagged_ref, lambda f: mine_ref[0, f], mask_ref[0:1, :], relax_ref)


def shift(values, by):
    return pltpu.roll(values, by % LANES8, 0)


def put(ref, start, value):
    for h in range(ref.shape[0]):
        ref[h, start : start + value.shape[0], :] = value[:, h * LANES : (h + 1) * LANES]


def get(ref, start, count):
    return jnp.concatenate([ref[h, start : start + count, :] for h in range(ref.shape[0])], axis=1)


def get_strided(ref, start, steps):
    rows = pl.ds(start, LANES8, stride=steps)
    return jnp.concatenate([ref[h, rows, :] for h in range(ref.shape[0])], axis=1)


def put_strided(ref, start, steps, value):
    for h in range(ref.shape[0]):
        ref[h, pl.ds(start, LANES8, stride=steps), :] = value[:, h * LANES : (h + 1) * LANES]


def factor_kernel(own_ref, other_ref, low_ref, fore_ref, inv_ref, high_ref, back_ref, scan_ref, kappa, ratio, inverse):
    half, width = own_ref.shape
    depth = 2 * half
    steps = low_ref.shape[0]
    level = lax.axis_index("lev")
    ratio[...] = jnp.zeros(ratio.shape, F32)
    inverse[...] = jnp.zeros(inverse.shape, F32)

    @pl.when(level == 0)
    def _():
        kappa[0:half, :] = own_ref[...]
        kappa[half:depth, :] = other_ref[...].astype(F32)

    @pl.when(level == 1)
    def _():
        kappa[0:half, :] = other_ref[...].astype(F32)
        kappa[half:depth, :] = own_ref[...]

    excess = jnp.ones((1, width), F32)
    for k in range(depth):
        here = kappa[k : k + 1, :]
        inv = 1.0 / (excess + here)
        down = here * inv
        put(inverse, k, inv)
        if k < depth - 1:
            put(ratio, LANES8 + k, down)
        excess = 1.0 + down * excess

    index = lax.broadcasted_iota(jnp.int32, (LANES8, width), 0)
    running = None
    for t in range(steps):
        low = get_strided(ratio, LANES8 - 1 + t, steps)
        low_ref[t] = low
        running = low if running is None else running * low
        fore_ref[t] = running
        inv_ref[t] = get_strided(inverse, t, steps)
    one = jnp.where(index >= 1, running, 0.0)
    two = jnp.where(index >= 2, running * shift(running, 1), 0.0)
    four = jnp.where(index >= 4, two * shift(two, 2), 0.0)
    scan_ref[0], scan_ref[1], scan_ref[2] = one, two, four
    running = None
    for t in range(steps - 1, -1, -1):
        high = get_strided(ratio, LANES8 + t, steps)
        high_ref[t] = high
        running = high if running is None else running * high
        back_ref[t] = running
    one = jnp.where(index < LANES8 - 1, running, 0.0)
    two = jnp.where(index < LANES8 - 2, running * shift(running, -1), 0.0)
    four = jnp.where(index < LANES8 - 4, two * shift(two, -2), 0.0)
    scan_ref[3], scan_ref[4], scan_ref[5] = one, two, four


def solve(right, factors):
    low_ref, fore_ref, inv_ref, high_ref, back_ref, scan_ref = factors
    steps, _, width = low_ref.shape
    index = lax.broadcasted_iota(jnp.int32, (LANES8, width), 0)
    rows = []
    for t in range(steps):
        row = get_strided(right, t, steps)
        if t:
            row = row + low_ref[t] * rows[-1]
        rows.append(row)
    carry = rows[-1]
    for i, by in enumerate((1, 2, 4)):
        carry = carry + scan_ref[i] * shift(carry, by)
    carry = jnp.where(index >= 1, shift(carry, 1), 0.0)
    rows = [(rows[t] + fore_ref[t] * carry) * inv_ref[t] for t in range(steps)]
    for t in range(steps - 2, -1, -1):
        rows[t] = rows[t] + high_ref[t] * rows[t + 1]
    carry = rows[0]
    for i, by in enumerate((1, 2, 4)):
        carry = carry + scan_ref[3 + i] * shift(carry, -by)
    carry = jnp.where(index < LANES8 - 1, shift(carry, -1), 0.0)
    for t in range(steps):
        put_strided(right, t, steps, rows[t] + back_ref[t] * carry)


def dynamics(own, left, right, weight_ref, diff_ref, gather_ref, factors, wide, flux, columns, emit, half, fields):
    slots = fields + SOLVED
    stride = wide.shape[0] // slots
    width = weight_ref.shape[1]
    for f in range(slots):
        at = slice(f * stride, f * stride + half)
        mid = own(f)
        high = mid.astype(BF16)
        wide[at, 0:width] = left(f)
        wide[at, width : 2 * width] = high
        wide[at, 2 * width : 3 * width] = right(f)
        wide[at, 3 * width :] = (mid - high.astype(F32)).astype(BF16)
    both = jnp.dot(wide[:, 0 : 3 * width], gather_ref[...], preferred_element_type=F32)
    rest = jnp.dot(wide[:, 3 * width :], gather_ref[width : 2 * width, 0:width], preferred_element_type=F32)
    flux[...] = both[:, :width] + both[:, width:] + rest
    total = weight_ref[0:1, :] + weight_ref[1:2, :] + weight_ref[2:3, :]

    def smoothed(f):
        scale = diff_ref[f if f < fields else f - fields]
        mid = own(f)
        return mid + scale * (flux[f * stride : f * stride + half, :] - total * mid)

    level = lax.axis_index("lev")
    depth = 2 * half
    for f in range(SOLVED):
        put(columns.at[f], depth, jnp.zeros((columns.shape[2] - depth, width), F32))
        mine, theirs = smoothed(f), smoothed(fields + f)

        @pl.when(level == 0)
        def _():
            put(columns.at[f], 0, mine)
            put(columns.at[f], half, theirs)

        @pl.when(level == 1)
        def _():
            put(columns.at[f], 0, theirs)
            put(columns.at[f], half, mine)

    for f in range(SOLVED):
        solve(columns.at[f], factors)
    for f in range(SOLVED, fields):
        emit(f, smoothed(f))

    @pl.when(level == 0)
    def _():
        for f in range(SOLVED):
            emit(f, get(columns.at[f], 0, half))
            emit(fields + f, get(columns.at[f], half, half))

    @pl.when(level == 1)
    def _():
        for f in range(SOLVED):
            emit(f, get(columns.at[f], half, half))
            emit(fields + f, get(columns.at[f], 0, half))


def first_kernel(
    state_ref, left_ref, right_ref, dleft_ref, dright_ref, across_ref, mine_ref, lag_ref, weight_ref, diff_ref, gather_ref,
    *rest,
):
    factors, (full_ref, short_ref, wide, flux, columns) = rest[:6], rest[6:]
    fields, half = state_ref.shape[1], state_ref.shape[2]

    def emit(f, value):
        lagged = mine_ref[f] if f < fields else lag_ref[f - fields]
        value = value + lagged.astype(F32)
        full_ref[f] = value
        short_ref[f] = value.astype(BF16)

    @pl.when(lax.axis_index("sec") == 1)
    def _():
        dynamics(
            lambda f: state_ref[0, f] if f < fields else across_ref[f - fields].astype(F32),
            lambda f: left_ref[f] if f < fields else dleft_ref[f - fields],
            lambda f: right_ref[f] if f < fields else dright_ref[f - fields],
            weight_ref, diff_ref, gather_ref, factors, wide, flux, columns, emit, half, fields,
        )


def last_kernel(
    state_ref, left_ref, right_ref, full_ref, lagged_ref, mask_ref, relax_ref, weight_ref, diff_ref, gather_ref, *rest
):
    factors, (out_ref, wide, flux, columns) = rest[:6], rest[6:]
    fields, half = out_ref.shape[1], out_ref.shape[2]

    def emit(f, value):
        if f < fields:
            out_ref[0, f] = value + lagged_ref[f].astype(F32)

    @pl.when(lax.axis_index("sec") == 0)
    def _():
        dynamics(
            lambda f: state_ref[f], lambda f: left_ref[f], lambda f: right_ref[f],
            weight_ref, diff_ref, gather_ref, factors, wide, flux, columns, emit, half, fields,
        )

    @pl.when(lax.axis_index("sec") == 1)
    def _():
        tendency_into(out_ref.at[0], lambda f: full_ref[f], mask_ref[1:2, :], relax_ref)


def params(mib):
    return pltpu.CompilerParams(vmem_limit_bytes=mib << 20)


def shards(sections, neighbours, edge_weight, field_diff, vert_coef, relax_rate, precip_mask):
    _, fields, half, width = sections.shape
    shape = jax.ShapeDtypeStruct
    steps = up(up(2 * half, LANES8) // LANES8, 4)
    depth = steps * LANES8
    slots = fields + SOLVED
    reach = 3 * width

    short = sections[0].astype(BF16)
    solved_short = short[0:SOLVED]
    left = route(short, 1, 0, [(0, 1)])
    right = route(short, -1, 0, [(0, 1)])
    pack = jnp.concatenate([solved_short, vert_coef.astype(BF16)[None]], axis=0)
    across = route(pack, 0, 1, [(0, 1), (1, 0)])
    lag = route(solved_short, 0, 1, [(0, 0), (1, 1)])
    dleft = route(solved_short, 1, 1, [(0, 1)])
    dright = route(solved_short, -1, 1, [(0, 1)])
    state = route(sections, 0, 0, [(0, 1), (1, 0)])

    gather, lagged = pl.pallas_call(
        prepare_kernel,
        out_shape=[shape((reach, 2 * width), BF16), shape((fields, half, width), BF16)],
        in_specs=[VMEM] * 4 + [SMEM],
        out_specs=[VMEM] * 2,
        compiler_params=params(16),
    )(sections, neighbours, edge_weight, precip_mask, relax_rate)

    chunk = shape((steps, LANES8, width), F32)
    factors = pl.pallas_call(
        factor_kernel,
        out_shape=[chunk] * 5 + [shape((6, LANES8, width), F32)],
        in_specs=[VMEM] * 2,
        out_specs=[VMEM] * 6,
        scratch_shapes=[
            pltpu.VMEM((2 * half, width), F32),
            pltpu.VMEM((width // LANES, depth + 2 * LANES8, LANES), F32),
            pltpu.VMEM((width // LANES, depth, LANES), F32),
        ],
        compiler_params=params(16),
    )(vert_coef, across[SOLVED])

    scratch = [
        pltpu.VMEM((slots * up(half, 16), 4 * width), BF16),
        pltpu.VMEM((slots * up(half, 16), width), F32),
        pltpu.VMEM((SOLVED, width // LANES, depth, LANES), F32),
    ]
    full, brief = pl.pallas_call(
        first_kernel,
        out_shape=[shape((slots, half, width), F32), shape((slots, half, width), BF16)],
        in_specs=[VMEM] * 9 + [SMEM] + [VMEM] * 7,
        out_specs=[VMEM] * 2,
        scratch_shapes=scratch,
        compiler_params=params(32),
    )(state, left, right, dleft, dright, across, short, lag, edge_weight, field_diff, gather, *factors)

    left = route(brief, 1, 0, [(1, 0)])
    right = route(brief, -1, 0, [(1, 0)])
    state = route(full, 0, 0, [(1, 0), (0, 1)])
    return pl.pallas_call(
        last_kernel,
        out_shape=shape(sections.shape, F32),
        in_specs=[VMEM] * 6 + [SMEM, VMEM, SMEM] + [VMEM] * 7,
        out_specs=VMEM,
        scratch_shapes=scratch,
        compiler_params=params(32),
    )(state, left, right, full, lagged, precip_mask, relax_rate, edge_weight, field_diff, gather, *factors)


def solution(mesh):
    return jax.shard_map(
        shards,
        mesh=mesh,
        in_specs=(
            P("sec", None, "lev", "dom"),
            P(None, "dom"),
            P(None, "dom"),
            P(),
            P("lev", "dom"),
            P(),
            P(None, "dom"),
        ),
        out_specs=P("sec", None, "lev", "dom"),
        check_vma=False,
    )
```

```python
import functools
import jax
import jax.numpy as jnp
from jax import lax
from jax.experimental import pallas as pl
from jax.experimental.pallas import tpu as pltpu
from jax.sharding import PartitionSpec as P

AXES = ("sec", "dom", "lev")
SOLVED = 2
PART = 5
EDGES = 3
LANES8 = 8
LANES = 128
VMEM = pl.BlockSpec(memory_space=pltpu.VMEM)
SMEM = pl.BlockSpec(memory_space=pltpu.SMEM)
ANY = pl.BlockSpec(memory_space=pl.ANY)
F32 = jnp.float32
BF16 = jnp.bfloat16


def up(count, unit):
    return -(-count // unit) * unit


def route(array, *moves):
    doms, levs = lax.axis_size("dom"), lax.axis_size("lev")
    place = lambda s, d, v: (s * doms + d) * levs + v
    table = [
        (place(a, d, v), place(b, (d + blocks) % doms, v ^ flip))
        for a, b, blocks, flip in moves
        for d in range(doms)
        for v in range(levs)
    ]
    return lax.ppermute(array, AXES, table)


def strips(array):
    return array.reshape(-1, LANES)


def get_field(ref, f, half, parts):
    rows = [pl.ds(f * half * parts + h, half, stride=parts) for h in range(parts)]
    return jnp.concatenate([ref[r, :] for r in rows], axis=1)


def put_field(ref, f, half, parts, value):
    for h in range(parts):
        ref[pl.ds(f * half * parts + h, half, stride=parts), :] = value[:, h * LANES : (h + 1) * LANES]


def tendency(state, fields, mask, relax, emit):
    rounded = lambda f: state(f).astype(BF16).astype(F32)
    theta, vapour, cloud, rain = rounded(1), rounded(2), rounded(3), rounded(4)
    saturation = 0.6 * jnp.exp(0.25 * theta)
    condense = 0.5 * jnp.tanh(vapour - saturation)
    autoconv = 0.4 * cloud * cloud / (1.0 + cloud * cloud)
    evaporate = 0.3 * rain * rain / (1.0 + rain * rain) * jax.nn.sigmoid(saturation - vapour)
    micro = {
        1: 2.5 * (condense - evaporate),
        2: evaporate - condense,
        3: condense - autoconv,
        4: autoconv - evaporate,
    }
    for f in range(fields):
        clear = -relax(f) * rounded(f)
        if f in micro:
            clear = jnp.where(mask == 1, clear + micro[f], clear)
        emit(f, clear)


def edge_matrix(gather_ref, nbr_ref, weight_ref):
    width = nbr_ref.shape[1]
    reach = gather_ref.shape[0]
    rows = 64
    for start in range(0, reach, rows):
        place = lax.broadcasted_iota(jnp.int32, (rows, width), 0) + start
        total = jnp.zeros((rows, width), F32)
        for edge in range(EDGES):
            total = total + jnp.where(place == nbr_ref[edge : edge + 1, :], weight_ref[edge : edge + 1, :], 0.0)
        high = total.astype(BF16)
        gather_ref[start : start + rows, 0:width] = high
        gather_ref[start : start + rows, width : 2 * width] = (total - high.astype(F32)).astype(BF16)


def prepare_kernel(
    mine_ref, short_ref, kappa_ref, nbr_ref, weight_ref, mask_ref, relax_ref, diff_ref, after_ref,
    gather_ref, lagged_ref, rates_ref, pack_ref,
):
    fields, half, width = lagged_ref.shape
    for f in range(SOLVED):
        pack_ref[f] = short_ref[f]
    pack_ref[SOLVED] = kappa_ref[...].astype(BF16)
    edge_matrix(gather_ref, nbr_ref, weight_ref)
    for f in range(fields):
        rates_ref[f : f + 1, :] = jnp.full((1, width), diff_ref[f], F32)
        rates_ref[fields + f : fields + f + 1, :] = jnp.full((1, width), relax_ref[f], F32)

    @pl.when(lax.axis_index("sec") == 0)
    def _():
        def emit(f, value):
            lagged_ref[f] = value.astype(BF16)

        state = lambda f: get_field(mine_ref, f, half, width // LANES)
        tendency(state, fields, mask_ref[0:1, :], lambda f: relax_ref[f], emit)


def shift(values, by):
    return pltpu.roll(values, by % LANES8, 0)


def put(ref, start, value):
    for h in range(ref.shape[0]):
        ref[h, start : start + value.shape[0], :] = value[:, h * LANES : (h + 1) * LANES]


def get(ref, start, count):
    return jnp.concatenate([ref[h, start : start + count, :] for h in range(ref.shape[0])], axis=1)


def get_strided(ref, start, steps):
    rows = pl.ds(start, LANES8, stride=steps)
    return jnp.concatenate([ref[h, rows, :] for h in range(ref.shape[0])], axis=1)


def put_strided(ref, start, steps, value):
    for h in range(ref.shape[0]):
        ref[h, pl.ds(start, LANES8, stride=steps), :] = value[:, h * LANES : (h + 1) * LANES]


def factor_kernel(own_ref, pack_ref, low_ref, fore_ref, inv_ref, high_ref, back_ref, scan_ref, kappa, ratio, inverse):
    half, width = own_ref.shape
    depth = 2 * half
    steps = low_ref.shape[0]
    level = lax.axis_index("lev")
    ratio[...] = jnp.zeros(ratio.shape, F32)
    inverse[...] = jnp.zeros(inverse.shape, F32)

    @pl.when(level == 0)
    def _():
        kappa[0:half, :] = own_ref[...]
        kappa[half:depth, :] = pack_ref[SOLVED].astype(F32)

    @pl.when(level == 1)
    def _():
        kappa[0:half, :] = pack_ref[SOLVED].astype(F32)
        kappa[half:depth, :] = own_ref[...]

    excess = jnp.ones((1, width), F32)
    for k in range(depth):
        here = kappa[k : k + 1, :]
        inv = 1.0 / (excess + here)
        down = here * inv
        put(inverse, k, inv)
        if k < depth - 1:
            put(ratio, LANES8 + k, down)
        excess = 1.0 + down * excess

    index = lax.broadcasted_iota(jnp.int32, (LANES8, width), 0)
    running = None
    for t in range(steps):
        low = get_strided(ratio, LANES8 - 1 + t, steps)
        low_ref[t] = low
        running = low if running is None else running * low
        fore_ref[t] = running
        inv_ref[t] = get_strided(inverse, t, steps)
    one = jnp.where(index >= 1, running, 0.0)
    two = jnp.where(index >= 2, running * shift(running, 1), 0.0)
    four = jnp.where(index >= 4, two * shift(two, 2), 0.0)
    scan_ref[0], scan_ref[1], scan_ref[2] = one, two, four
    running = None
    for t in range(steps - 1, -1, -1):
        high = get_strided(ratio, LANES8 + t, steps)
        high_ref[t] = high
        running = high if running is None else running * high
        back_ref[t] = running
    one = jnp.where(index < LANES8 - 1, running, 0.0)
    two = jnp.where(index < LANES8 - 2, running * shift(running, -1), 0.0)
    four = jnp.where(index < LANES8 - 4, two * shift(two, -2), 0.0)
    scan_ref[3], scan_ref[4], scan_ref[5] = one, two, four


def solve(right, factors):
    low_ref, fore_ref, inv_ref, high_ref, back_ref, scan_ref = factors
    steps, _, width = low_ref.shape
    index = lax.broadcasted_iota(jnp.int32, (LANES8, width), 0)
    rows = []
    for t in range(steps):
        row = get_strided(right, t, steps)
        if t:
            row = row + low_ref[t] * rows[-1]
        rows.append(row)
    carry = rows[-1]
    for i, by in enumerate((1, 2, 4)):
        carry = carry + scan_ref[i] * shift(carry, by)
    carry = jnp.where(index >= 1, shift(carry, 1), 0.0)
    rows = [(rows[t] + fore_ref[t] * carry) * inv_ref[t] for t in range(steps)]
    for t in range(steps - 2, -1, -1):
        rows[t] = rows[t] + high_ref[t] * rows[t + 1]
    carry = rows[0]
    for i, by in enumerate((1, 2, 4)):
        carry = carry + scan_ref[3 + i] * shift(carry, -by)
    carry = jnp.where(index < LANES8 - 1, shift(carry, -1), 0.0)
    for t in range(steps):
        put_strided(right, t, steps, rows[t] + back_ref[t] * carry)


def dynamics(own, left, right, weight_ref, rates_ref, gather_ref, factors, wide, flux, columns, emit, half, fields):
    slots = fields + SOLVED
    stride = wide.shape[0] // slots
    width = weight_ref.shape[1]
    for f in range(slots):
        at = slice(f * stride, f * stride + half)
        mid = own(f)
        high = mid.astype(BF16)
        wide[at, 0:width] = left(f)
        wide[at, width : 2 * width] = high
        wide[at, 2 * width : 3 * width] = right(f)
        wide[at, 3 * width :] = (mid - high.astype(F32)).astype(BF16)
    both = jnp.dot(wide[:, 0 : 3 * width], gather_ref[...], preferred_element_type=F32)
    rest = jnp.dot(wide[:, 3 * width :], gather_ref[width : 2 * width, 0:width], preferred_element_type=F32)
    flux[...] = both[:, :width] + both[:, width:] + rest
    total = weight_ref[0:1, :] + weight_ref[1:2, :] + weight_ref[2:3, :]

    def smoothed(f):
        at = f % fields
        scale = rates_ref[at : at + 1, :]
        mid = own(f)
        return mid + scale * (flux[f * stride : f * stride + half, :] - total * mid)

    level = lax.axis_index("lev")
    depth = 2 * half
    for f in range(SOLVED):
        put(columns.at[f], depth, jnp.zeros((columns.shape[2] - depth, width), F32))
        mine, theirs = smoothed(f), smoothed(fields + f)

        @pl.when(level == 0)
        def _():
            put(columns.at[f], 0, mine)
            put(columns.at[f], half, theirs)

        @pl.when(level == 1)
        def _():
            put(columns.at[f], 0, theirs)
            put(columns.at[f], half, mine)

    for f in range(SOLVED):
        solve(columns.at[f], factors)
    for f in range(SOLVED, fields):
        emit(f, smoothed(f))

    @pl.when(level == 0)
    def _():
        for f in range(SOLVED):
            emit(f, get(columns.at[f], 0, half))
            emit(fields + f, get(columns.at[f], half, half))

    @pl.when(level == 1)
    def _():
        for f in range(SOLVED):
            emit(f, get(columns.at[f], half, half))
            emit(fields + f, get(columns.at[f], 0, half))


def first_kernel(
    state_ref, left_ref, right_ref, dleft_ref, dright_ref, across_ref, pack_ref, mine_ref, weight_ref, rates_ref, gather_ref, *rest
):
    factors, (*full_refs, short_ref, wide, flux, columns) = rest[:6], rest[6:]
    fields, half, width = mine_ref.shape

    def emit(f, value):
        lagged = mine_ref[f] if f < fields else pack_ref[f - fields]
        value = value + lagged.astype(F32)
        full_refs[f // PART][f % PART] = value
        short_ref[f] = value.astype(BF16)

    @pl.when(lax.axis_index("sec") == 1)
    def _():
        dynamics(
            lambda f: get_field(state_ref, f, half, width // LANES) if f < fields else across_ref[f - fields].astype(F32),
            lambda f: left_ref[f] if f < fields else dleft_ref[f - fields],
            lambda f: right_ref[f] if f < fields else dright_ref[f - fields],
            weight_ref, rates_ref, gather_ref, factors, wide, flux, columns, emit, half, fields,
        )


def last_kernel(
    left_ref, right_ref, brief_ref, lagged_ref, mask_ref, weight_ref, rates_ref, gather_ref, *rest
):
    count = -(-left_ref.shape[0] // PART)
    states, rest = rest[:count], rest[count:]
    factors, (out_ref, wide, flux, columns, held, sems) = rest[:6], rest[6:]
    fields, half, width = lagged_ref.shape
    parts = width // LANES

    def send(low, high, sem):
        rows = pl.ds(low * half * parts, (high - low) * half * parts)
        return pltpu.make_async_copy(held.at[rows], out_ref.at[rows], sems.at[sem])

    def emit(f, value):
        if f < fields:
            put_field(held, f, half, parts, value + lagged_ref[f].astype(F32))
            if f == fields - 1:
                send(SOLVED, fields, 0).start()

    @pl.when(lax.axis_index("sec") == 0)
    def _():
        dynamics(
            lambda f: states[f // PART][f % PART], lambda f: left_ref[f], lambda f: right_ref[f],
            weight_ref, rates_ref, gather_ref, factors, wide, flux, columns, emit, half, fields,
        )

    @pl.when(lax.axis_index("sec") == 1)
    def _():
        def keep(f, value):
            put_field(held, f, half, parts, value)

        relax = lambda f: rates_ref[fields + f : fields + f + 1, :]
        tendency(lambda f: brief_ref[f].astype(F32), fields, mask_ref[1:2, :], relax, keep)
        send(SOLVED, fields, 0).start()

    send(0, SOLVED, 1).start()
    send(SOLVED, fields, 0).wait()
    send(0, SOLVED, 1).wait()


def cost(us):
    return pl.CostEstimate(flops=0, transcendentals=0, bytes_accessed=int(us * 3e6))


def params(mib):
    return pltpu.CompilerParams(vmem_limit_bytes=mib << 20)


def shards(sections, neighbours, edge_weight, field_diff, vert_coef, relax_rate, precip_mask):
    _, fields, half, width = sections.shape
    shape = jax.ShapeDtypeStruct
    steps = up(up(2 * half, LANES8) // LANES8, 4)
    depth = steps * LANES8
    slots = fields + SOLVED
    reach = 3 * width

    mine = strips(sections)
    short = sections[0].astype(BF16)
    head = short[0:SOLVED]
    back = (1, 0, 0, 0)
    state = route(mine, (0, 1, 0, 0), (1, 0, 0, 0))
    left = route(short, (0, 1, 1, 0), back)
    right = route(short, (0, 1, -1, 0), back)
    dleft = route(head, (0, 1, 1, 1), back)
    dright = route(head, (0, 1, -1, 1), back)

    gather, lagged, rates, pack = pl.pallas_call(
        prepare_kernel,
        out_shape=[
            shape((reach, 2 * width), BF16),
            shape((fields, half, width), BF16),
            shape((2 * fields, width), F32),
            shape((SOLVED + 1, half, width), BF16),
        ],
        in_specs=[VMEM] * 6 + [SMEM] * 2 + [ANY],
        out_specs=[VMEM] * 4,
        compiler_params=params(8),
        cost_estimate=cost(0.01),
    )(mine, short, vert_coef, neighbours, edge_weight, precip_mask, relax_rate, field_diff, state)
    pack = route(pack, (0, 0, 0, 1), (1, 1, 0, 1))
    across = route(pack, (0, 1, 0, 0), (1, 0, 0, 0))

    chunk = shape((steps, LANES8, width), F32)
    factors = pl.pallas_call(
        factor_kernel,
        out_shape=[chunk] * 5 + [shape((6, LANES8, width), F32)],
        in_specs=[VMEM] * 2,
        out_specs=[VMEM] * 6,
        scratch_shapes=[
            pltpu.VMEM((2 * half, width), F32),
            pltpu.VMEM((width // LANES, depth + 2 * LANES8, LANES), F32),
            pltpu.VMEM((width // LANES, depth, LANES), F32),
        ],
        compiler_params=params(8),
        cost_estimate=cost(0.01),
    )(vert_coef, pack)

    scratch = [
        pltpu.VMEM((slots * up(half, 16), 4 * width), BF16),
        pltpu.VMEM((slots * up(half, 16), width), F32),
        pltpu.VMEM((SOLVED, width // LANES, depth, LANES), F32),
    ]
    *full, brief = pl.pallas_call(
        first_kernel,
        out_shape=[shape((min(PART, slots - f), half, width), F32) for f in range(0, slots, PART)]
        + [shape((slots, half, width), BF16)],
        in_specs=[VMEM] * 17,
        out_specs=[VMEM] * (1 + -(-slots // PART)),
        scratch_shapes=scratch,
        compiler_params=params(32),
    )(state, left, right, dleft, dright, across, pack, short, edge_weight, rates, gather, *factors)

    left = route(brief, (1, 0, 1, 0), (0, 1, 0, 0))
    right = route(brief, (1, 0, -1, 0))
    states = [route(part, (1, 0, 0, 0), (0, 1, 0, 0)) for part in full]
    out = pl.pallas_call(
        last_kernel,
        out_shape=shape(mine.shape, F32),
        in_specs=[VMEM] * (14 + len(states)),
        out_specs=ANY,
        scratch_shapes=scratch + [pltpu.VMEM(mine.shape, F32), pltpu.SemaphoreType.DMA((2,))],
        compiler_params=params(32),
    )(left, right, brief, lagged, precip_mask, edge_weight, rates, gather, *states, *factors)
    return out.reshape(sections.shape)


def solution(mesh):
    return jax.shard_map(
        shards,
        mesh=mesh,
        in_specs=(
            P("sec", None, "lev", "dom"),
            P(None, "dom"),
            P(None, "dom"),
            P(),
            P("lev", "dom"),
            P(),
            P(None, "dom"),
        ),
        out_specs=P("sec", None, "lev", "dom"),
        check_vma=False,
    )
```

```python
import jax
import jax.numpy as jnp
from jax import lax
from jax.experimental import pallas as pl
from jax.experimental.pallas import tpu as pltpu
from jax.sharding import PartitionSpec as P

AXES = ("sec", "dom", "lev")
SOLVED = 2
EDGES = 3
SUB = 8
LANES = 128
TILE = 16
CHUNK = 32
PIECES = 3
VMEM = pl.BlockSpec(memory_space=pltpu.VMEM)
SMEM = pl.BlockSpec(memory_space=pltpu.SMEM)
ANY = pl.BlockSpec(memory_space=pl.ANY)
F32 = jnp.float32
BF16 = jnp.bfloat16


def up(count, unit):
    return -(-count // unit) * unit


def spans(low, high, size):
    return [(r, min(r + size, high)) for r in range(low, high, size)]


def route(array, *moves):
    doms, levs = lax.axis_size("dom"), lax.axis_size("lev")
    place = lambda s, d, v: (s * doms + d) * levs + v
    table = [
        (place(a, d, v), place(b, (d + blocks) % doms, v ^ flip))
        for a, b, blocks, flip in moves
        for d in range(doms)
        for v in range(levs)
    ]
    return lax.ppermute(array, AXES, table)


def strips(array):
    return array.reshape(-1, LANES)


def get_rows(ref, low, high, parts):
    return jnp.concatenate([ref[pl.ds(low * parts + h, high - low, stride=parts), :] for h in range(parts)], axis=1)


def put_rows(ref, low, parts, value):
    for h in range(parts):
        ref[pl.ds(low * parts + h, value.shape[0], stride=parts), :] = value[:, h * LANES : (h + 1) * LANES]


def tendency(state, fields, mask, relax, emit):
    rounded = lambda f: state(f).astype(BF16).astype(F32)
    theta, vapour, cloud, rain = rounded(1), rounded(2), rounded(3), rounded(4)
    saturation = 0.6 * jnp.exp(0.25 * theta)
    condense = 0.5 * jnp.tanh(vapour - saturation)
    autoconv = 0.4 * cloud * cloud / (1.0 + cloud * cloud)
    evaporate = 0.3 * rain * rain / (1.0 + rain * rain) * jax.nn.sigmoid(saturation - vapour)
    micro = {
        1: 2.5 * (condense - evaporate),
        2: evaporate - condense,
        3: condense - autoconv,
        4: autoconv - evaporate,
    }
    for f in range(fields):
        clear = -relax(f) * rounded(f)
        if f in micro:
            clear = jnp.where(mask == 1, clear + micro[f], clear)
        emit(f, clear)


def shorten_kernel(mine_ref, short_ref, head_ref):
    own, width = short_ref.shape
    parts = width // LANES

    @pl.when(lax.axis_index("sec") == 0)
    def _():
        for low, high in spans(0, own, CHUNK):
            value = get_rows(mine_ref, low, high, parts).astype(BF16)
            short_ref[low:high, :] = value
            end = min(high, head_ref.shape[0])
            if low < end:
                head_ref[low:end, :] = value[: end - low]


def pack_kernel(head_ref, other_ref, kappa_ref, pack_ref):
    _, half, width = pack_ref.shape
    parts = width // LANES

    @pl.when(lax.axis_index("sec") == 0)
    def _():
        for f in range(SOLVED):
            pack_ref[f] = head_ref[f * half : (f + 1) * half, :]
            pack_ref[SOLVED + f] = get_rows(other_ref, f * half, (f + 1) * half, parts).astype(BF16)

    pack_ref[2 * SOLVED] = kappa_ref[...].astype(BF16)


def prepare_kernel(
    mine_ref, short_ref, nbr_ref, weight_ref, mask_ref, relax_ref, diff_ref, gather_ref, lagged_ref, rates_ref, keep_ref, take_ref, work,
    lagged,
):
    fields = rates_ref.shape[0]
    reach, width = gather_ref.shape[0], nbr_ref.shape[1]
    half = lagged_ref.shape[0] // fields
    base = up(fields * half, TILE)
    for low, high in spans(0, reach, 64):
        place = lax.broadcasted_iota(jnp.int32, (high - low, width), 0) + low
        total = jnp.zeros((high - low, width), F32)
        for edge in range(EDGES):
            total = total + jnp.where(place == nbr_ref[edge : edge + 1, :], weight_ref[edge : edge + 1, :], 0.0)
        first = total.astype(BF16)
        gather_ref[low:high, 0:width] = first
        gather_ref[low:high, width : 2 * width] = (total - first.astype(F32)).astype(BF16)
    total = weight_ref[0:1, :] + weight_ref[1:2, :] + weight_ref[2:3, :]
    keep_ref[...] = jnp.zeros(keep_ref.shape, F32)
    take_ref[...] = jnp.zeros(take_ref.shape, F32)
    for f in range(fields):
        rates_ref[f : f + 1, :] = jnp.full((1, width), relax_ref[f], F32)
    for f in range(fields + SOLVED):
        low = f * half if f < fields else base + (f - fields) * half
        scale = diff_ref[f % fields]
        keep_ref[low : low + half, :] = jnp.broadcast_to(1.0 - scale * total, (half, width))
        take_ref[low : low + half, :] = jnp.full((half, width), scale, F32)

    @pl.when(lax.axis_index("sec") == 0)
    def _():
        def emit(f, value):
            lagged[f * half : (f + 1) * half, :] = value

        for low, high in spans(0, fields * half, CHUNK):
            work[low:high, :] = short_ref[low:high, :].astype(F32)
        tendency(
            lambda f: work[f * half : (f + 1) * half, :], fields, mask_ref[0:1, :], lambda f: relax_ref[f], emit
        )
        for low, high in spans(0, fields * half, CHUNK):
            lagged_ref[low:high, :] = lagged[low:high, :].astype(BF16)

    @pl.when(lax.axis_index("sec") == 1)
    def _():
        for low, high in spans(0, fields * half, CHUNK):
            lagged_ref[low:high, :] = get_rows(mine_ref, low, high, width // LANES).astype(BF16)


def shift(values, by):
    return pltpu.roll(values, by % SUB, 0)


def put(ref, start, value):
    for h in range(ref.shape[0]):
        ref[h, start : start + value.shape[0], :] = value[:, h * LANES : (h + 1) * LANES]


def get(ref, start, count):
    return jnp.concatenate([ref[h, start : start + count, :] for h in range(ref.shape[0])], axis=1)


def get_strided(ref, start, steps):
    rows = pl.ds(start, SUB, stride=steps)
    return jnp.concatenate([ref[h, rows, :] for h in range(ref.shape[0])], axis=1)


def put_strided(ref, start, steps, value):
    for h in range(ref.shape[0]):
        ref[h, pl.ds(start, SUB, stride=steps), :] = value[:, h * LANES : (h + 1) * LANES]


def factor_kernel(own_ref, pack_ref, low_ref, fore_ref, inv_ref, high_ref, back_ref, scan_ref, kappa, ratio, inverse):
    half, width = own_ref.shape
    depth = 2 * half
    steps = low_ref.shape[0]
    level = lax.axis_index("lev")
    other = pack_ref[2 * SOLVED].astype(F32)
    ratio[...] = jnp.zeros(ratio.shape, F32)
    inverse[...] = jnp.zeros(inverse.shape, F32)

    @pl.when(level == 0)
    def _():
        kappa[0:half, :] = own_ref[...]
        kappa[half:depth, :] = other

    @pl.when(level == 1)
    def _():
        kappa[0:half, :] = other
        kappa[half:depth, :] = own_ref[...]

    excess = jnp.ones((1, width), F32)
    for k in range(depth):
        here = kappa[k : k + 1, :]
        inv = 1.0 / (excess + here)
        down = here * inv
        put(inverse, k, inv)
        if k < depth - 1:
            put(ratio, SUB + k, down)
        excess = 1.0 + down * excess

    index = lax.broadcasted_iota(jnp.int32, (SUB, width), 0)
    running = None
    for t in range(steps):
        low = get_strided(ratio, SUB - 1 + t, steps)
        low_ref[t] = low
        running = low if running is None else running * low
        fore_ref[t] = running
        inv_ref[t] = get_strided(inverse, t, steps)
    one = jnp.where(index >= 1, running, 0.0)
    two = jnp.where(index >= 2, running * shift(running, 1), 0.0)
    four = jnp.where(index >= 4, two * shift(two, 2), 0.0)
    scan_ref[0], scan_ref[1], scan_ref[2] = one, two, four
    running = None
    for t in range(steps - 1, -1, -1):
        high = get_strided(ratio, SUB + t, steps)
        high_ref[t] = high
        running = high if running is None else running * high
        back_ref[t] = running
    one = jnp.where(index < SUB - 1, running, 0.0)
    two = jnp.where(index < SUB - 2, running * shift(running, -1), 0.0)
    four = jnp.where(index < SUB - 4, two * shift(two, -2), 0.0)
    scan_ref[3], scan_ref[4], scan_ref[5] = one, two, four


def solve(right, factors):
    low_ref, fore_ref, inv_ref, high_ref, back_ref, scan_ref = factors
    steps, _, width = low_ref.shape
    index = lax.broadcasted_iota(jnp.int32, (SUB, width), 0)
    rows = []
    for t in range(steps):
        row = get_strided(right, t, steps)
        if t:
            row = row + low_ref[t] * rows[-1]
        rows.append(row)
    carry = rows[-1]
    for i, by in enumerate((1, 2, 4)):
        carry = carry + scan_ref[i] * shift(carry, by)
    carry = jnp.where(index >= 1, shift(carry, 1), 0.0)
    rows = [(rows[t] + fore_ref[t] * carry) * inv_ref[t] for t in range(steps)]
    for t in range(steps - 2, -1, -1):
        rows[t] = rows[t] + high_ref[t] * rows[t + 1]
    carry = rows[0]
    for i, by in enumerate((1, 2, 4)):
        carry = carry + scan_ref[3 + i] * shift(carry, -by)
    carry = jnp.where(index < SUB - 1, shift(carry, -1), 0.0)
    for t in range(steps):
        put_strided(right, t, steps, rows[t] + back_ref[t] * carry)


def gathered(left, middle, right, gather_ref):
    width = gather_ref.shape[1] // 2
    high = middle.astype(BF16)
    low = (middle - high.astype(F32)).astype(BF16)
    mul = lambda rows, side, cols: jnp.dot(
        rows, gather_ref[side * width : (side + 1) * width, cols], preferred_element_type=F32
    )
    both = mul(left, 0, slice(None)) + mul(high, 1, slice(None)) + mul(right, 2, slice(None))
    return both[:, :width] + both[:, width:] + mul(low, 1, slice(0, width))


def solve_rows(smooth, columns, factors, half, base):
    level = lax.axis_index("lev")
    depth = 2 * half
    width = smooth.shape[1]
    for f in range(SOLVED):
        put(columns.at[f], depth, jnp.zeros((columns.shape[2] - depth, width), F32))
        mine = smooth[f * half : (f + 1) * half, :]
        theirs = smooth[base + f * half : base + (f + 1) * half, :]

        @pl.when(level == 0)
        def _():
            put(columns.at[f], 0, mine)
            put(columns.at[f], half, theirs)

        @pl.when(level == 1)
        def _():
            put(columns.at[f], 0, theirs)
            put(columns.at[f], half, mine)

    for f in range(SOLVED):
        solve(columns.at[f], factors)


def first_kernel(
    state_ref, left_ref, right_ref, dleft_ref, dright_ref, pack_ref, lagged_ref, keep_ref, take_ref, gather_ref, *rest
):
    factors, (*full_refs, short_ref, smooth, columns) = rest[:6], rest[6:]
    _, half, width = pack_ref.shape
    own = lagged_ref.shape[0]
    total = short_ref.shape[0]
    base = up(own, TILE)
    parts = width // LANES
    piece = full_refs[0].shape[0]

    @pl.when(lax.axis_index("sec") == 1)
    def _():
        middle = get_rows(state_ref, 0, own, parts)
        smooth[0:own, :] = middle * keep_ref[0:own, :] + take_ref[0:own, :] * gathered(
            left_ref[...], middle, right_ref[...], gather_ref
        )
        for f in range(SOLVED):
            smooth[base + f * half : base + (f + 1) * half, :] = pack_ref[f].astype(F32)
        rows = slice(base, base + SOLVED * half)
        middle = smooth[rows, :]
        smooth[rows, :] = middle * keep_ref[rows, :] + take_ref[rows, :] * gathered(
            dleft_ref[...], middle, dright_ref[...], gather_ref
        )
        solve_rows(smooth, columns, factors, half, base)
        for f in range(SOLVED):
            lag = pack_ref[SOLVED + f].astype(F32)

            @pl.when(lax.axis_index("lev") == 0)
            def _():
                smooth[f * half : (f + 1) * half, :] = get(columns.at[f], 0, half)
                smooth[base + f * half : base + (f + 1) * half, :] = get(columns.at[f], half, half) + lag

            @pl.when(lax.axis_index("lev") == 1)
            def _():
                smooth[f * half : (f + 1) * half, :] = get(columns.at[f], half, half)
                smooth[base + f * half : base + (f + 1) * half, :] = get(columns.at[f], 0, half) + lag

        for low, high in spans(0, total, CHUNK):
            value = smooth[low:high, :]
            if low < own:
                stop = min(high, own)
                value = smooth[low:stop, :] + lagged_ref[low:stop, :].astype(F32)
                smooth[low:stop, :] = value
                value = smooth[low:high, :]
            short_ref[low:high, :] = value.astype(BF16)
            full_refs[low // piece][low % piece : low % piece + high - low, :] = value


def last_kernel(left_ref, right_ref, brief_ref, lagged_ref, mask_ref, rates_ref, keep_ref, take_ref, gather_ref, *rest):
    pieces, factors, (out_ref, smooth, columns, held, sems) = rest[:PIECES], rest[PIECES : PIECES + 6], rest[PIECES + 6 :]
    own, width = lagged_ref.shape
    fields = rates_ref.shape[0]
    half = own // fields
    base = up(own, TILE)
    total = left_ref.shape[0]
    parts = width // LANES
    first = up(SOLVED * half, CHUNK)
    piece = pieces[0].shape[0]

    def send(low, high, sem):
        rows = pl.ds(low * parts, (high - low) * parts)
        return pltpu.make_async_copy(held.at[rows], out_ref.at[rows], sems.at[sem])

    @pl.when(lax.axis_index("sec") == 0)
    def _():
        for i in range(PIECES):
            low, high = i * piece, min((i + 1) * piece, total)
            rows = slice(low, high)
            middle = pieces[i][...]
            smooth[rows, :] = middle * keep_ref[rows, :] + take_ref[rows, :] * gathered(
                left_ref[rows, :], middle, right_ref[rows, :], gather_ref
            )
        for low, high in spans(first, own, CHUNK):
            put_rows(held, low, parts, smooth[low:high, :] + lagged_ref[low:high, :].astype(F32))
        send(first, own, 0).start()
        solve_rows(smooth, columns, factors, half, base)
        for f in range(SOLVED):

            @pl.when(lax.axis_index("lev") == 0)
            def _():
                smooth[f * half : (f + 1) * half, :] = get(columns.at[f], 0, half)

            @pl.when(lax.axis_index("lev") == 1)
            def _():
                smooth[f * half : (f + 1) * half, :] = get(columns.at[f], half, half)

        for low, high in spans(0, first, CHUNK):
            put_rows(held, low, parts, smooth[low:high, :] + lagged_ref[low:high, :].astype(F32))

    @pl.when(lax.axis_index("sec") == 1)
    def _():
        for low, high in spans(0, base, CHUNK):
            smooth[low:high, :] = brief_ref[low:high, :].astype(F32)

        def keep(f, value):
            put_rows(held, f * half, parts, value)

        relax = lambda f: rates_ref[f : f + 1, :]
        tendency(lambda f: smooth[f * half : (f + 1) * half, :], fields, mask_ref[1:2, :], relax, keep)
        send(first, own, 0).start()

    send(0, first, 1).start()
    send(first, own, 0).wait()
    send(0, first, 1).wait()


def cost(us):
    return pl.CostEstimate(flops=0, transcendentals=0, bytes_accessed=int(us * 3e6))


def params(mib):
    return pltpu.CompilerParams(vmem_limit_bytes=mib << 20)


def shards(sections, neighbours, edge_weight, field_diff, vert_coef, relax_rate, precip_mask):
    _, fields, half, width = sections.shape
    shape = jax.ShapeDtypeStruct
    steps = up(up(2 * half, SUB) // SUB, 4)
    depth = steps * SUB
    own = fields * half
    total = up(own, TILE) + up(SOLVED * half, TILE)
    piece = up(-(-total // PIECES), CHUNK)

    mine = strips(sections)
    short, head = pl.pallas_call(
        shorten_kernel,
        out_shape=[shape((own, width), BF16), shape((SOLVED * half, width), BF16)],
        in_specs=[VMEM],
        out_specs=[VMEM] * 2,
        compiler_params=params(4),
        cost_estimate=cost(0.01),
    )(mine)
    back = (1, 0, 0, 0)
    state = route(mine, (0, 1, 0, 0), (1, 0, 0, 0))
    left = route(short, (0, 1, 1, 0), back)
    right = route(short, (0, 1, -1, 0), back)
    dleft = route(head, (0, 1, 1, 1), back)
    dright = route(head, (0, 1, -1, 1), back)

    pack = pl.pallas_call(
        pack_kernel,
        out_shape=shape((2 * SOLVED + 1, half, width), BF16),
        in_specs=[VMEM] * 3,
        out_specs=VMEM,
        compiler_params=params(4),
        cost_estimate=cost(0.01),
    )(head, state, vert_coef)
    pack = route(pack, (0, 1, 0, 1), (1, 0, 0, 1))

    gather, lagged, rates, keep, take = pl.pallas_call(
        prepare_kernel,
        out_shape=[
            shape((3 * width, 2 * width), BF16),
            shape((own, width), BF16),
            shape((fields, width), F32),
            shape((total, width), F32),
            shape((total, width), F32),
        ],
        in_specs=[VMEM] * 5 + [SMEM] * 2,
        out_specs=[VMEM] * 5,
        scratch_shapes=[pltpu.VMEM((own, width), F32)] * 2,
        compiler_params=params(8),
        cost_estimate=cost(0.01),
    )(mine, short, neighbours, edge_weight, precip_mask, relax_rate, field_diff)

    chunk = shape((steps, SUB, width), F32)
    factors = pl.pallas_call(
        factor_kernel,
        out_shape=[chunk] * 5 + [shape((6, SUB, width), F32)],
        in_specs=[VMEM] * 2,
        out_specs=[VMEM] * 6,
        scratch_shapes=[
            pltpu.VMEM((2 * half, width), F32),
            pltpu.VMEM((width // LANES, depth + 2 * SUB, LANES), F32),
            pltpu.VMEM((width // LANES, depth, LANES), F32),
        ],
        compiler_params=params(8),
        cost_estimate=cost(0.01),
    )(vert_coef, pack)

    scratch = [pltpu.VMEM((total, width), F32), pltpu.VMEM((SOLVED, width // LANES, depth, LANES), F32)]
    *full, brief = pl.pallas_call(
        first_kernel,
        out_shape=[shape((high - low, width), F32) for low, high in spans(0, total, piece)] + [shape((total, width), BF16)],
        in_specs=[VMEM] * 16,
        out_specs=[VMEM] * (PIECES + 1),
        scratch_shapes=scratch,
        compiler_params=params(24),
    )(state, left, right, dleft, dright, pack, lagged, keep, take, gather, *factors)

    left = route(brief, (1, 0, 1, 0), (0, 1, 0, 0))
    right = route(brief, (1, 0, -1, 0))
    pieces = [route(part, (1, 0, 0, 0), (0, 1, 0, 0)) for part in full]
    out = pl.pallas_call(
        last_kernel,
        out_shape=shape(mine.shape, F32),
        in_specs=[VMEM] * (15 + PIECES),
        out_specs=ANY,
        scratch_shapes=scratch + [pltpu.VMEM(mine.shape, F32), pltpu.SemaphoreType.DMA((2,))],
        compiler_params=params(24),
    )(left, right, brief, lagged, precip_mask, rates, keep, take, gather, *pieces, *factors)
    return out.reshape(sections.shape)


def solution(mesh):
    return jax.shard_map(
        shards,
        mesh=mesh,
        in_specs=(
            P("sec", None, "lev", "dom"),
            P(None, "dom"),
            P(None, "dom"),
            P(),
            P("lev", "dom"),
            P(),
            P(None, "dom"),
        ),
        out_specs=P("sec", None, "lev", "dom"),
        check_vma=False,
    )
```

```python
import functools
import jax
import jax.numpy as jnp
from jax import lax
from jax.experimental import pallas as pl
from jax.experimental.pallas import tpu as pltpu
from jax.sharding import PartitionSpec as P

AXES = ("sec", "dom", "lev")
SOLVED = 2
EDGES = 3
SUB = 8
LANES = 128
TILE = 16
CHUNK = 32
PIECES = 3
VMEM = pl.BlockSpec(memory_space=pltpu.VMEM)
SMEM = pl.BlockSpec(memory_space=pltpu.SMEM)
ANY = pl.BlockSpec(memory_space=pl.ANY)
F32 = jnp.float32
BF16 = jnp.bfloat16


def up(count, unit):
    return -(-count // unit) * unit


def spans(low, high, size):
    return [(r, min(r + size, high)) for r in range(low, high, size)]


def route(array, *moves):
    doms, levs = lax.axis_size("dom"), lax.axis_size("lev")
    place = lambda s, d, v: (s * doms + d) * levs + v
    table = [
        (place(a, d, v), place(b, to_block(d) % doms, v ^ flip))
        for a, b, to_block, flip in moves
        for d in range(doms)
        for v in range(levs)
    ]
    return lax.ppermute(array, AXES, table)


def same(block):
    return block


def near(block):
    return block ^ 1


def far(block):
    return block - 1 if block % 2 == 0 else block + 1


def strips(array):
    return array.reshape(-1, LANES)


def get_rows(ref, low, high, parts):
    return jnp.concatenate([ref[pl.ds(low * parts + h, high - low, stride=parts), :] for h in range(parts)], axis=1)


def put_rows(ref, low, parts, value):
    for h in range(parts):
        ref[pl.ds(low * parts + h, value.shape[0], stride=parts), :] = value[:, h * LANES : (h + 1) * LANES]


def tendency(state, fields, mask, relax, emit):
    rounded = lambda f: state(f).astype(BF16).astype(F32)
    theta, vapour, cloud, rain = rounded(1), rounded(2), rounded(3), rounded(4)
    saturation = 0.6 * jnp.exp(0.25 * theta)
    condense = 0.5 * jnp.tanh(vapour - saturation)
    autoconv = 0.4 * cloud * cloud / (1.0 + cloud * cloud)
    evaporate = 0.3 * rain * rain / (1.0 + rain * rain) * jax.nn.sigmoid(saturation - vapour)
    micro = {
        1: 2.5 * (condense - evaporate),
        2: evaporate - condense,
        3: condense - autoconv,
        4: autoconv - evaporate,
    }
    for f in range(fields):
        clear = -relax(f) * rounded(f)
        if f in micro:
            clear = jnp.where(mask == 1, clear + micro[f], clear)
        emit(f, clear)


def shorten_kernel(mine_ref, short_ref, head_ref):
    own, width = short_ref.shape
    parts = width // LANES

    @pl.when(lax.axis_index("sec") == 0)
    def _():
        for low, high in spans(0, own, CHUNK):
            value = get_rows(mine_ref, low, high, parts).astype(BF16)
            short_ref[low:high, :] = value
            end = min(high, head_ref.shape[0])
            if low < end:
                head_ref[low:end, :] = value[: end - low]


def pack_kernel(head_ref, other_ref, kappa_ref, pack_ref):
    _, half, width = pack_ref.shape
    parts = width // LANES

    @pl.when(lax.axis_index("sec") == 0)
    def _():
        for f in range(SOLVED):
            pack_ref[f] = head_ref[f * half : (f + 1) * half, :]
            pack_ref[SOLVED + f] = get_rows(other_ref, f * half, (f + 1) * half, parts).astype(BF16)

    pack_ref[2 * SOLVED] = kappa_ref[...].astype(BF16)


def prepare_kernel(
    mine_ref, short_ref, nbr_ref, weight_ref, mask_ref, relax_ref, diff_ref, gather_ref, lagged_ref, rates_ref, keep_ref, take_ref, work,
    lagged,
):
    fields = rates_ref.shape[0]
    reach, width = gather_ref.shape[0], nbr_ref.shape[1]
    half = lagged_ref.shape[0] // fields
    base = up(fields * half, TILE)
    odd = lax.axis_index("dom") % 2
    sides = (2 * width * (1 - odd), width, 2 * width * odd)
    for low, high in spans(0, reach, 64):
        place = lax.broadcasted_iota(jnp.int32, (high - low, width), 0) + (low % width + sides[low // width])
        total = jnp.zeros((high - low, width), F32)
        for edge in range(EDGES):
            total = total + jnp.where(place == nbr_ref[edge : edge + 1, :], weight_ref[edge : edge + 1, :], 0.0)
        first = total.astype(BF16)
        gather_ref[low:high, 0:width] = first
        gather_ref[low:high, width : 2 * width] = (total - first.astype(F32)).astype(BF16)
    total = weight_ref[0:1, :] + weight_ref[1:2, :] + weight_ref[2:3, :]
    keep_ref[...] = jnp.zeros(keep_ref.shape, F32)
    take_ref[...] = jnp.zeros(take_ref.shape, F32)
    for f in range(fields):
        rates_ref[f : f + 1, :] = jnp.full((1, width), relax_ref[f], F32)
    for f in range(fields + SOLVED):
        low = f * half if f < fields else base + (f - fields) * half
        scale = diff_ref[f % fields]
        keep_ref[low : low + half, :] = jnp.broadcast_to(1.0 - scale * total, (half, width))
        take_ref[low : low + half, :] = jnp.full((half, width), scale, F32)

    @pl.when(lax.axis_index("sec") == 0)
    def _():
        def emit(f, value):
            lagged[f * half : (f + 1) * half, :] = value

        for low, high in spans(0, fields * half, CHUNK):
            work[low:high, :] = short_ref[low:high, :].astype(F32)
        tendency(
            lambda f: work[f * half : (f + 1) * half, :], fields, mask_ref[0:1, :], lambda f: relax_ref[f], emit
        )
        for low, high in spans(0, fields * half, CHUNK):
            lagged_ref[low:high, :] = lagged[low:high, :].astype(BF16)

    @pl.when(lax.axis_index("sec") == 1)
    def _():
        for low, high in spans(0, fields * half, CHUNK):
            lagged_ref[low:high, :] = get_rows(mine_ref, low, high, width // LANES).astype(BF16)


def shift(values, by):
    return pltpu.roll(values, by % SUB, 0)


def put(ref, start, value):
    for h in range(ref.shape[0]):
        ref[h, start : start + value.shape[0], :] = value[:, h * LANES : (h + 1) * LANES]


def get(ref, start, count):
    return jnp.concatenate([ref[h, start : start + count, :] for h in range(ref.shape[0])], axis=1)


def get_strided(ref, start, steps):
    rows = pl.ds(start, SUB, stride=steps)
    return jnp.concatenate([ref[h, rows, :] for h in range(ref.shape[0])], axis=1)


def put_strided(ref, start, steps, value):
    for h in range(ref.shape[0]):
        ref[h, pl.ds(start, SUB, stride=steps), :] = value[:, h * LANES : (h + 1) * LANES]


def factor_kernel(
    core, at, own_ref, other_ref, low_ref, fore_ref, inv_ref, high_ref, back_ref, scan_ref, kappa, ratio, inverse
):
    @pl.when(lax.axis_index("sec") == core)
    def _():
        factor(
            own_ref, other_ref[at].astype(F32), low_ref, fore_ref, inv_ref, high_ref, back_ref, scan_ref, kappa, ratio, inverse
        )


def factor(own_ref, other, low_ref, fore_ref, inv_ref, high_ref, back_ref, scan_ref, kappa, ratio, inverse):
    half, width = own_ref.shape
    depth = 2 * half
    steps = low_ref.shape[0]
    level = lax.axis_index("lev")
    ratio[...] = jnp.zeros(ratio.shape, F32)
    inverse[...] = jnp.zeros(inverse.shape, F32)

    @pl.when(level == 0)
    def _():
        kappa[0:half, :] = own_ref[...]
        kappa[half:depth, :] = other

    @pl.when(level == 1)
    def _():
        kappa[0:half, :] = other
        kappa[half:depth, :] = own_ref[...]

    excess = jnp.ones((1, width), F32)
    for k in range(depth):
        here = kappa[k : k + 1, :]
        inv = 1.0 / (excess + here)
        down = here * inv
        put(inverse, k, inv)
        if k < depth - 1:
            put(ratio, SUB + k, down)
        excess = 1.0 + down * excess

    index = lax.broadcasted_iota(jnp.int32, (SUB, width), 0)
    running = None
    for t in range(steps):
        low = get_strided(ratio, SUB - 1 + t, steps)
        low_ref[t] = low
        running = low if running is None else running * low
        fore_ref[t] = running
        inv_ref[t] = get_strided(inverse, t, steps)
    one = jnp.where(index >= 1, running, 0.0)
    two = jnp.where(index >= 2, running * shift(running, 1), 0.0)
    four = jnp.where(index >= 4, two * shift(two, 2), 0.0)
    scan_ref[0], scan_ref[1], scan_ref[2] = one, two, four
    running = None
    for t in range(steps - 1, -1, -1):
        high = get_strided(ratio, SUB + t, steps)
        high_ref[t] = high
        running = high if running is None else running * high
        back_ref[t] = running
    one = jnp.where(index < SUB - 1, running, 0.0)
    two = jnp.where(index < SUB - 2, running * shift(running, -1), 0.0)
    four = jnp.where(index < SUB - 4, two * shift(two, -2), 0.0)
    scan_ref[3], scan_ref[4], scan_ref[5] = one, two, four


def solve(right, factors):
    low_ref, fore_ref, inv_ref, high_ref, back_ref, scan_ref = factors
    steps, _, width = low_ref.shape
    index = lax.broadcasted_iota(jnp.int32, (SUB, width), 0)
    rows = []
    for t in range(steps):
        row = get_strided(right, t, steps)
        if t:
            row = row + low_ref[t] * rows[-1]
        rows.append(row)
    carry = rows[-1]
    for i, by in enumerate((1, 2, 4)):
        carry = carry + scan_ref[i] * shift(carry, by)
    carry = jnp.where(index >= 1, shift(carry, 1), 0.0)
    rows = [(rows[t] + fore_ref[t] * carry) * inv_ref[t] for t in range(steps)]
    for t in range(steps - 2, -1, -1):
        rows[t] = rows[t] + high_ref[t] * rows[t + 1]
    carry = rows[0]
    for i, by in enumerate((1, 2, 4)):
        carry = carry + scan_ref[3 + i] * shift(carry, -by)
    carry = jnp.where(index < SUB - 1, shift(carry, -1), 0.0)
    for t in range(steps):
        put_strided(right, t, steps, rows[t] + back_ref[t] * carry)


def gathered(near_rows, middle, far_rows, gather_ref):
    width = gather_ref.shape[1] // 2
    high = middle.astype(BF16)
    low = (middle - high.astype(F32)).astype(BF16)
    mul = lambda rows, side, cols: jnp.dot(
        rows, gather_ref[side * width : (side + 1) * width, cols], preferred_element_type=F32
    )
    both = mul(near_rows, 0, slice(None)) + mul(high, 1, slice(None)) + mul(far_rows, 2, slice(None))
    return both[:, :width] + both[:, width:] + mul(low, 1, slice(0, width))


def solve_rows(smooth, columns, factors, half, base):
    level = lax.axis_index("lev")
    depth = 2 * half
    width = smooth.shape[1]
    for f in range(SOLVED):
        put(columns.at[f], depth, jnp.zeros((columns.shape[2] - depth, width), F32))
        mine = smooth[f * half : (f + 1) * half, :]
        theirs = smooth[base + f * half : base + (f + 1) * half, :]

        @pl.when(level == 0)
        def _():
            put(columns.at[f], 0, mine)
            put(columns.at[f], half, theirs)

        @pl.when(level == 1)
        def _():
            put(columns.at[f], 0, theirs)
            put(columns.at[f], half, mine)

    for f in range(SOLVED):
        solve(columns.at[f], factors)


def first_kernel(
    state_ref, far_ref, near_ref, dfar_ref, dnear_ref, pack_ref, lagged_ref, keep_ref, take_ref, gather_ref, *rest
):
    factors, (*full_refs, short_ref, smooth, columns) = rest[:6], rest[6:]
    _, half, width = pack_ref.shape
    own = lagged_ref.shape[0]
    total = short_ref.shape[0]
    base = up(own, TILE)
    parts = width // LANES
    piece = full_refs[0].shape[0]

    def store(low, value):
        for i, (start, stop) in enumerate(spans(0, piece * PIECES, piece)):
            a, b = max(low, start), min(low + value.shape[0], stop)
            if a < b:
                full_refs[i][a - start : b - start, :] = value[a - low : b - low]

    @pl.when(lax.axis_index("sec") == 1)
    def _():
        middle = get_rows(state_ref, 0, own, parts)
        smooth[0:own, :] = middle * keep_ref[0:own, :] + take_ref[0:own, :] * gathered(
            near_ref[...], middle, far_ref[...], gather_ref
        )
        for f in range(SOLVED):
            smooth[base + f * half : base + (f + 1) * half, :] = pack_ref[f].astype(F32)
        rows = slice(base, base + SOLVED * half)
        middle = smooth[rows, :]
        smooth[rows, :] = middle * keep_ref[rows, :] + take_ref[rows, :] * gathered(
            dnear_ref[...], middle, dfar_ref[...], gather_ref
        )
        solve_rows(smooth, columns, factors, half, base)
        for f in range(SOLVED):
            lag = pack_ref[SOLVED + f].astype(F32)

            @pl.when(lax.axis_index("lev") == 0)
            def _():
                smooth[f * half : (f + 1) * half, :] = get(columns.at[f], 0, half)
                smooth[base + f * half : base + (f + 1) * half, :] = get(columns.at[f], half, half) + lag

            @pl.when(lax.axis_index("lev") == 1)
            def _():
                smooth[f * half : (f + 1) * half, :] = get(columns.at[f], half, half)
                smooth[base + f * half : base + (f + 1) * half, :] = get(columns.at[f], 0, half) + lag

        for low, high in spans(0, total, CHUNK):
            value = smooth[low:high, :]
            if low < own:
                stop = min(high, own)
                value = smooth[low:stop, :] + lagged_ref[low:stop, :].astype(F32)
                smooth[low:stop, :] = value
                value = smooth[low:high, :]
            short_ref[low:high, :] = value.astype(BF16)
            store(low, value)
        store(total, pack_ref[2 * SOLVED].astype(F32))


def last_kernel(near_ref, far_ref, brief_ref, lagged_ref, mask_ref, rates_ref, keep_ref, take_ref, gather_ref, *rest):
    pieces, factors, (out_ref, smooth, columns, held, sems) = rest[:PIECES], rest[PIECES : PIECES + 6], rest[PIECES + 6 :]
    own, width = lagged_ref.shape
    fields = rates_ref.shape[0]
    half = own // fields
    base = up(own, TILE)
    total = near_ref.shape[0]
    parts = width // LANES
    first = up(SOLVED * half, CHUNK)
    piece = pieces[0].shape[0]

    def send(low, high, sem):
        rows = pl.ds(low * parts, (high - low) * parts)
        return pltpu.make_async_copy(held.at[rows], out_ref.at[rows], sems.at[sem])

    @pl.when(lax.axis_index("sec") == 0)
    def _():
        for i in range(PIECES):
            low, high = i * piece, min((i + 1) * piece, total)
            rows = slice(low, high)
            middle = pieces[i][0 : high - low, :]
            smooth[rows, :] = middle * keep_ref[rows, :] + take_ref[rows, :] * gathered(
                near_ref[rows, :], middle, far_ref[rows, :], gather_ref
            )
        for low, high in spans(first, own, CHUNK):
            put_rows(held, low, parts, smooth[low:high, :] + lagged_ref[low:high, :].astype(F32))
        send(first, own, 0).start()
        solve_rows(smooth, columns, factors, half, base)
        for f in range(SOLVED):

            @pl.when(lax.axis_index("lev") == 0)
            def _():
                smooth[f * half : (f + 1) * half, :] = get(columns.at[f], 0, half)

            @pl.when(lax.axis_index("lev") == 1)
            def _():
                smooth[f * half : (f + 1) * half, :] = get(columns.at[f], half, half)

        for low, high in spans(0, first, CHUNK):
            put_rows(held, low, parts, smooth[low:high, :] + lagged_ref[low:high, :].astype(F32))

    @pl.when(lax.axis_index("sec") == 1)
    def _():
        for low, high in spans(0, base, CHUNK):
            smooth[low:high, :] = brief_ref[low:high, :].astype(F32)

        def keep(f, value):
            put_rows(held, f * half, parts, value)

        relax = lambda f: rates_ref[f : f + 1, :]
        tendency(lambda f: smooth[f * half : (f + 1) * half, :], fields, mask_ref[1:2, :], relax, keep)
        send(first, own, 0).start()

    send(0, first, 1).start()
    send(first, own, 0).wait()
    send(0, first, 1).wait()


def cost(us):
    return pl.CostEstimate(flops=int(us * 1e9), transcendentals=0, bytes_accessed=0)


def params(mib):
    return pltpu.CompilerParams(vmem_limit_bytes=mib << 20)


def shards(sections, neighbours, edge_weight, field_diff, vert_coef, relax_rate, precip_mask):
    _, fields, half, width = sections.shape
    shape = jax.ShapeDtypeStruct
    steps = up(up(2 * half, SUB) // SUB, 4)
    depth = steps * SUB
    own = fields * half
    total = up(own, TILE) + up(SOLVED * half, TILE)
    piece = up(-(-(total + half) // PIECES), SUB)

    mine = strips(sections)
    short, head = pl.pallas_call(
        shorten_kernel,
        out_shape=[shape((own, width), BF16), shape((SOLVED * half, width), BF16)],
        in_specs=[VMEM],
        out_specs=[VMEM] * 2,
        compiler_params=params(4),
        cost_estimate=cost(0.01),
    )(mine)
    back = (1, 0, same, 0)
    state = route(mine, (0, 1, same, 0), back)
    near_rows = route(short, (0, 1, near, 0), back)
    far_rows = route(short, (0, 1, far, 0), back)
    dnear = route(head, (0, 1, near, 1), back)
    dfar = route(head, (0, 1, far, 1), back)

    pack = pl.pallas_call(
        pack_kernel,
        out_shape=shape((2 * SOLVED + 1, half, width), BF16),
        in_specs=[VMEM] * 3,
        out_specs=VMEM,
        compiler_params=params(4),
        cost_estimate=cost(0.01),
    )(head, state, vert_coef)
    pack = route(pack, (0, 1, same, 1), back)

    gather, lagged, rates, keep, take = pl.pallas_call(
        prepare_kernel,
        out_shape=[
            shape((3 * width, 2 * width), BF16),
            shape((own, width), BF16),
            shape((fields, width), F32),
            shape((total, width), F32),
            shape((total, width), F32),
        ],
        in_specs=[VMEM] * 5 + [SMEM] * 2,
        out_specs=[VMEM] * 5,
        scratch_shapes=[pltpu.VMEM((own, width), F32)] * 2,
        compiler_params=params(8),
        cost_estimate=cost(0.01),
    )(mine, short, neighbours, edge_weight, precip_mask, relax_rate, field_diff)

    chunk = shape((steps, SUB, width), F32)
    def factors_of(core, at, other, us):
        return pl.pallas_call(
            functools.partial(factor_kernel, core, at),
            out_shape=[chunk] * 5 + [shape((6, SUB, width), F32)],
            in_specs=[VMEM] * 2,
            out_specs=[VMEM] * 6,
            scratch_shapes=[
                pltpu.VMEM((2 * half, width), F32),
                pltpu.VMEM((width // LANES, depth + 2 * SUB, LANES), F32),
                pltpu.VMEM((width // LANES, depth, LANES), F32),
            ],
            compiler_params=params(8),
            cost_estimate=cost(us),
        )(vert_coef, other)

    factors = factors_of(1, 2 * SOLVED, pack, 0.01)

    scratch = [pltpu.VMEM((total, width), F32), pltpu.VMEM((SOLVED, width // LANES, depth, LANES), F32)]
    *full, brief = pl.pallas_call(
        first_kernel,
        out_shape=[shape((piece, width), F32)] * PIECES + [shape((total, width), BF16)],
        in_specs=[VMEM] * 16,
        out_specs=[VMEM] * (PIECES + 1),
        scratch_shapes=scratch,
        compiler_params=params(24),
    )(state, far_rows, near_rows, dfar, dnear, pack, lagged, keep, take, gather, *factors)

    near_rows = route(brief, (1, 0, near, 0), (0, 1, same, 0))
    far_rows = route(brief, (1, 0, far, 0))
    pieces = [route(part, back, (0, 1, same, 0)) for part in full]
    last, low = divmod(total, piece)
    factors = factors_of(0, slice(low, low + half), pieces[last], 0)
    out = pl.pallas_call(
        last_kernel,
        out_shape=shape(mine.shape, F32),
        in_specs=[VMEM] * (15 + PIECES),
        out_specs=ANY,
        scratch_shapes=scratch + [pltpu.VMEM(mine.shape, F32), pltpu.SemaphoreType.DMA((2,))],
        compiler_params=params(24),
    )(near_rows, far_rows, brief, lagged, precip_mask, rates, keep, take, gather, *pieces, *factors)
    return out.reshape(sections.shape)


def solution(mesh):
    return jax.shard_map(
        shards,
        mesh=mesh,
        in_specs=(
            P("sec", None, "lev", "dom"),
            P(None, "dom"),
            P(None, "dom"),
            P(),
            P("lev", "dom"),
            P(),
            P(None, "dom"),
        ),
        out_specs=P("sec", None, "lev", "dom"),
        check_vma=False,
    )
```

```python
import functools
import jax
import jax.numpy as jnp
from jax import lax
from jax.experimental import pallas as pl
from jax.experimental.pallas import tpu as pltpu
from jax.sharding import PartitionSpec as P

AXES = ("sec", "dom", "lev")
SOLVED = 2
EDGES = 3
SUB = 8
LANES = 128
TILE = 16
CHUNK = 32
PIECES = 3
VMEM = pl.BlockSpec(memory_space=pltpu.VMEM)
SMEM = pl.BlockSpec(memory_space=pltpu.SMEM)
ANY = pl.BlockSpec(memory_space=pl.ANY)
F32 = jnp.float32
BF16 = jnp.bfloat16


def up(count, unit):
    return -(-count // unit) * unit


def spans(low, high, size):
    return [(r, min(r + size, high)) for r in range(low, high, size)]


def route(array, *moves):
    doms, levs = lax.axis_size("dom"), lax.axis_size("lev")
    place = lambda s, d, v: (s * doms + d) * levs + v
    table = [
        (place(a, d, v), place(b, to_block(d) % doms, v ^ flip))
        for a, b, to_block, flip in moves
        for d in range(doms)
        for v in range(levs)
    ]
    return lax.ppermute(array, AXES, table)


def same(block):
    return block


def near(block):
    return block ^ 1


def far(block):
    return block - 1 if block % 2 == 0 else block + 1


def strips(array):
    return array.reshape(-1, LANES)


def get_rows(ref, low, high, parts):
    return jnp.concatenate([ref[pl.ds(low * parts + h, high - low, stride=parts), :] for h in range(parts)], axis=1)


def put_rows(ref, low, parts, value):
    for h in range(parts):
        ref[pl.ds(low * parts + h, value.shape[0], stride=parts), :] = value[:, h * LANES : (h + 1) * LANES]


def tendency(state, fields, mask, relax, emit):
    rounded = lambda f: state(f).astype(BF16).astype(F32)
    theta, vapour, cloud, rain = rounded(1), rounded(2), rounded(3), rounded(4)
    saturation = 0.6 * jnp.exp(0.25 * theta)
    condense = 0.5 * jnp.tanh(vapour - saturation)
    autoconv = 0.4 * cloud * cloud / (1.0 + cloud * cloud)
    evaporate = 0.3 * rain * rain / (1.0 + rain * rain) * jax.nn.sigmoid(saturation - vapour)
    micro = {
        1: 2.5 * (condense - evaporate),
        2: evaporate - condense,
        3: condense - autoconv,
        4: autoconv - evaporate,
    }
    for f in range(fields):
        clear = -relax(f) * rounded(f)
        if f in micro:
            clear = jnp.where(mask == 1, clear + micro[f], clear)
        emit(f, clear)


def shorten_kernel(mine_ref, short_ref, head_ref, wide, sems):
    own, width = short_ref.shape
    parts = width // LANES
    pieces = spans(0, own, up(-(-own // 4), TILE))
    copies = []
    for i, (low, high) in enumerate(pieces):
        rows = pl.ds(low * parts, (high - low) * parts)
        copies.append(pltpu.make_async_copy(mine_ref.at[rows], wide.at[rows], sems.at[i]))
        copies[-1].start()
    for copy, (start, stop) in zip(copies, pieces):
        copy.wait()
        for low, high in spans(start, stop, CHUNK):
            value = get_rows(wide, low, high, parts).astype(BF16)
            short_ref[low:high, :] = value
            end = min(high, head_ref.shape[0])
            if low < end:
                head_ref[low:end, :] = value[: end - low]


def nothing_kernel(short_ref, head_ref):
    head_ref[...] = jnp.zeros(head_ref.shape, BF16)


def pack_kernel(head_ref, other_ref, kappa_ref, pack_ref):
    _, half, width = pack_ref.shape
    parts = width // LANES

    @pl.when(lax.axis_index("sec") == 0)
    def _():
        for f in range(SOLVED):
            pack_ref[f] = head_ref[f * half : (f + 1) * half, :]
            pack_ref[SOLVED + f] = get_rows(other_ref, f * half, (f + 1) * half, parts).astype(BF16)

    pack_ref[2 * SOLVED] = kappa_ref[...].astype(BF16)


def prepare_kernel(
    mine_ref, short_ref, nbr_ref, weight_ref, mask_ref, relax_ref, diff_ref, gather_ref, lagged_ref, rates_ref, keep_ref, take_ref, work,
    lagged,
):
    fields = rates_ref.shape[0]
    width = nbr_ref.shape[1]
    half = lagged_ref.shape[0] // fields
    base = up(fields * half, TILE)
    odd = lax.axis_index("dom") % 2
    sides = (2 * width * (1 - odd), 2 * width * odd, width)
    for side, start in enumerate(sides):
        for low, high in spans(0, width, 64):
            place = lax.broadcasted_iota(jnp.int32, (high - low, width), 0) + (low + start)
            total = jnp.zeros((high - low, width), F32)
            for edge in range(EDGES):
                total = total + jnp.where(place == nbr_ref[edge : edge + 1, :], weight_ref[edge : edge + 1, :], 0.0)
            first = total.astype(BF16)
            at = 2 * side * width + low
            gather_ref[at : at + high - low, :] = first
            gather_ref[at + width : at + width + high - low, :] = (total - first.astype(F32)).astype(BF16)
            if side == 2:
                gather_ref[at + 2 * width : at + 2 * width + high - low, :] = first
    total = weight_ref[0:1, :] + weight_ref[1:2, :] + weight_ref[2:3, :]
    keep_ref[...] = jnp.zeros(keep_ref.shape, F32)
    take_ref[...] = jnp.zeros(take_ref.shape, F32)
    for f in range(fields):
        rates_ref[f : f + 1, :] = jnp.full((1, width), relax_ref[f], F32)
    for f in range(fields + SOLVED):
        low = f * half if f < fields else base + (f - fields) * half
        scale = diff_ref[f % fields]
        keep_ref[low : low + half, :] = jnp.broadcast_to(1.0 - scale * total, (half, width))
        take_ref[low : low + half, :] = jnp.full((half, width), scale, F32)

    @pl.when(lax.axis_index("sec") == 0)
    def _():
        def emit(f, value):
            lagged[f * half : (f + 1) * half, :] = value

        for low, high in spans(0, fields * half, CHUNK):
            work[low:high, :] = short_ref[low:high, :].astype(F32)
        tendency(
            lambda f: work[f * half : (f + 1) * half, :], fields, mask_ref[0:1, :], lambda f: relax_ref[f], emit
        )
        for low, high in spans(0, fields * half, CHUNK):
            lagged_ref[low:high, :] = lagged[low:high, :].astype(BF16)

    @pl.when(lax.axis_index("sec") == 1)
    def _():
        for low, high in spans(0, fields * half, CHUNK):
            lagged_ref[low:high, :] = get_rows(mine_ref, low, high, width // LANES).astype(BF16)


def shift(values, by):
    return pltpu.roll(values, by % SUB, 0)


def put(ref, start, value):
    for h in range(ref.shape[0]):
        ref[h, start : start + value.shape[0], :] = value[:, h * LANES : (h + 1) * LANES]


def get(ref, start, count):
    return jnp.concatenate([ref[h, start : start + count, :] for h in range(ref.shape[0])], axis=1)


def get_strided(ref, start, steps):
    rows = pl.ds(start, SUB, stride=steps)
    return jnp.concatenate([ref[h, rows, :] for h in range(ref.shape[0])], axis=1)


def put_strided(ref, start, steps, value):
    for h in range(ref.shape[0]):
        ref[h, pl.ds(start, SUB, stride=steps), :] = value[:, h * LANES : (h + 1) * LANES]


def ready_first_kernel(kappa_ref, pack_ref, state_ref, lagged_ref, keep_ref, take_ref, gather_ref, *rest):
    factors, (start_ref, middle, *work) = rest[:6], rest[6:]
    _, half, width = pack_ref.shape
    own = lagged_ref.shape[0]
    base = up(own, TILE)

    @pl.when(lax.axis_index("sec") == 1)
    def _():
        factor(kappa_ref, pack_ref[2 * SOLVED].astype(F32), *factors, *work)
        middle[0:own, :] = get_rows(state_ref, 0, own, width // LANES)
        for f in range(SOLVED):
            middle[base + f * half : base + (f + 1) * half, :] = pack_ref[f].astype(F32)
        own_share(start_ref, middle, lagged_ref, keep_ref, take_ref, gather_ref, half)


def ready_last_kernel(at, kappa_ref, lagged_ref, keep_ref, take_ref, gather_ref, *rest):
    pieces, factors, (start_ref, middle, *work) = rest[:PIECES], rest[PIECES : PIECES + 6], rest[PIECES + 6 :]
    half = kappa_ref.shape[0]
    piece = pieces[0].shape[0]

    @pl.when(lax.axis_index("sec") == 0)
    def _():
        factor(kappa_ref, pieces[at // piece][at % piece : at % piece + half, :], *factors, *work)
        for i in range(PIECES):
            low, high = i * piece, min((i + 1) * piece, middle.shape[0])
            middle[low:high, :] = pieces[i][0 : high - low, :]
        own_share(start_ref, middle, lagged_ref, keep_ref, take_ref, gather_ref, half)


def own_share(start_ref, middle, lagged_ref, keep_ref, take_ref, gather_ref, half):
    width = middle.shape[1]
    solved, own = SOLVED * half, lagged_ref.shape[0]
    values = middle[...]
    high = values.astype(BF16)
    low = (values - high.astype(F32)).astype(BF16)
    share = jnp.dot(
        jnp.concatenate([high, high, low], axis=1), gather_ref[4 * width : 7 * width, :], preferred_element_type=F32
    )
    start_ref[...] = values * keep_ref[...] + take_ref[...] * share
    for low, high in spans(solved // CHUNK * CHUNK, own, CHUNK):
        lag = lagged_ref[low:high, :].astype(F32)
        if low < solved:
            lag = jnp.where(lax.broadcasted_iota(jnp.int32, lag.shape, 0) >= solved - low, lag, 0.0)
        start_ref[low:high, :] += lag


def sides_share(near_rows, far_rows, gather_ref):
    width = near_rows.shape[1]
    rows = jnp.concatenate([near_rows, near_rows, far_rows, far_rows], axis=1)
    return jnp.dot(rows, gather_ref[0 : 4 * width, :], preferred_element_type=F32)


def factor(own_ref, other, low_ref, fore_ref, inv_ref, high_ref, back_ref, scan_ref, kappa, ratio, inverse):
    half, width = own_ref.shape
    depth = 2 * half
    steps = low_ref.shape[0]
    level = lax.axis_index("lev")
    ratio[...] = jnp.zeros(ratio.shape, F32)
    inverse[...] = jnp.zeros(inverse.shape, F32)

    @pl.when(level == 0)
    def _():
        kappa[0:half, :] = own_ref[...]
        kappa[half:depth, :] = other

    @pl.when(level == 1)
    def _():
        kappa[0:half, :] = other
        kappa[half:depth, :] = own_ref[...]

    excess = jnp.ones((1, width), F32)
    for k in range(depth):
        here = kappa[k : k + 1, :]
        inv = 1.0 / (excess + here)
        down = here * inv
        put(inverse, k, inv)
        if k < depth - 1:
            put(ratio, SUB + k, down)
        excess = 1.0 + down * excess

    index = lax.broadcasted_iota(jnp.int32, (SUB, width), 0)
    running = None
    for t in range(steps):
        low = get_strided(ratio, SUB - 1 + t, steps)
        low_ref[t] = low
        running = low if running is None else running * low
        fore_ref[t] = running
        inv_ref[t] = get_strided(inverse, t, steps)
    one = jnp.where(index >= 1, running, 0.0)
    two = jnp.where(index >= 2, running * shift(running, 1), 0.0)
    four = jnp.where(index >= 4, two * shift(two, 2), 0.0)
    scan_ref[0], scan_ref[1], scan_ref[2] = one, two, four
    running = None
    for t in range(steps - 1, -1, -1):
        high = get_strided(ratio, SUB + t, steps)
        high_ref[t] = high
        running = high if running is None else running * high
        back_ref[t] = running
    one = jnp.where(index < SUB - 1, running, 0.0)
    two = jnp.where(index < SUB - 2, running * shift(running, -1), 0.0)
    four = jnp.where(index < SUB - 4, two * shift(two, -2), 0.0)
    scan_ref[3], scan_ref[4], scan_ref[5] = one, two, four


def solve(right, factors):
    low_ref, fore_ref, inv_ref, high_ref, back_ref, scan_ref = factors
    steps, _, width = low_ref.shape
    index = lax.broadcasted_iota(jnp.int32, (SUB, width), 0)
    rows = []
    for t in range(steps):
        row = get_strided(right, t, steps)
        if t:
            row = row + low_ref[t] * rows[-1]
        rows.append(row)
    carry = rows[-1]
    for i, by in enumerate((1, 2, 4)):
        carry = carry + scan_ref[i] * shift(carry, by)
    carry = jnp.where(index >= 1, shift(carry, 1), 0.0)
    rows = [(rows[t] + fore_ref[t] * carry) * inv_ref[t] for t in range(steps)]
    for t in range(steps - 2, -1, -1):
        rows[t] = rows[t] + high_ref[t] * rows[t + 1]
    carry = rows[0]
    for i, by in enumerate((1, 2, 4)):
        carry = carry + scan_ref[3 + i] * shift(carry, -by)
    carry = jnp.where(index < SUB - 1, shift(carry, -1), 0.0)
    for t in range(steps):
        put_strided(right, t, steps, rows[t] + back_ref[t] * carry)


def solve_rows(own, other, columns, factors):
    upper = lax.axis_index("lev") == 0
    half, width = own[0].shape
    depth = 2 * half
    for f in range(SOLVED):
        put(columns.at[f], depth, jnp.zeros((columns.shape[2] - depth, width), F32))
        put(columns.at[f], 0, jnp.where(upper, own[f], other[f]))
        put(columns.at[f], half, jnp.where(upper, other[f], own[f]))
    for f in range(SOLVED):
        solve(columns.at[f], factors)
    halves = [(get(columns.at[f], 0, half), get(columns.at[f], half, half)) for f in range(SOLVED)]
    return [jnp.where(upper, a, b) for a, b in halves], [jnp.where(upper, b, a) for a, b in halves]


def first_kernel(
    far_ref, near_ref, dfar_ref, dnear_ref, pack_ref, start_ref, lagged_ref, take_ref, gather_ref, *rest
):
    factors, (*full_refs, short_ref, smooth, columns) = rest[:6], rest[6:]
    _, half, width = pack_ref.shape
    own = lagged_ref.shape[0]
    total = short_ref.shape[0]
    base = up(own, TILE)
    first = up(SOLVED * half, CHUNK)
    piece = full_refs[0].shape[0]

    def store(low, value):
        for i, (start, stop) in enumerate(spans(0, piece * PIECES, piece)):
            a, b = max(low, start), min(low + value.shape[0], stop)
            if a < b:
                full_refs[i][a - start : b - start, :] = value[a - low : b - low]

    def emit(low, value):
        short_ref[low : low + value.shape[0], :] = value.astype(BF16)
        store(low, value)

    @pl.when(lax.axis_index("sec") == 1)
    def _():
        others = slice(base, base + SOLVED * half)
        smooth[others, :] = start_ref[others, :] + take_ref[others, :] * sides_share(
            dnear_ref[...], dfar_ref[...], gather_ref
        )
        rows = slice(0, first)
        smooth[rows, :] = start_ref[rows, :] + take_ref[rows, :] * sides_share(
            near_ref[rows, :], far_ref[rows, :], gather_ref
        )
        part = lambda low: [smooth[low + f * half : low + (f + 1) * half, :] for f in range(SOLVED)]
        mine, theirs = solve_rows(part(0), part(base), columns, factors)
        rows = slice(first, own)
        value = start_ref[rows, :] + take_ref[rows, :] * sides_share(near_ref[rows, :], far_ref[rows, :], gather_ref)
        for low, high in spans(first, own, CHUNK):
            emit(low, value[low - first : high - first])
        for f in range(SOLVED):
            smooth[f * half : (f + 1) * half, :] = mine[f]
            smooth[base + f * half : base + (f + 1) * half, :] = theirs[f] + pack_ref[SOLVED + f].astype(F32)
        for low, high in spans(0, first, CHUNK):
            lag = lagged_ref[low:high, :].astype(F32)
            if high > SOLVED * half:
                lag = jnp.where(lax.broadcasted_iota(jnp.int32, lag.shape, 0) < SOLVED * half - low, lag, 0.0)
            emit(low, smooth[low:high, :] + lag)
        for low, high in spans(base, total, CHUNK):
            emit(low, smooth[low:high, :])
        store(total, pack_ref[2 * SOLVED].astype(F32))


def last_kernel(near_ref, far_ref, brief_ref, start_ref, lagged_ref, mask_ref, rates_ref, take_ref, gather_ref, *rest):
    factors, (out_ref, smooth, columns, held, sems) = rest[:6], rest[6:]
    own, width = lagged_ref.shape
    fields = rates_ref.shape[0]
    half = own // fields
    base = up(own, TILE)
    total = near_ref.shape[0]
    parts = width // LANES
    first = up(SOLVED * half, CHUNK)

    def send(low, high, sem):
        rows = pl.ds(low * parts, (high - low) * parts)
        return pltpu.make_async_copy(held.at[rows], out_ref.at[rows], sems.at[sem])

    @pl.when(lax.axis_index("sec") == 0)
    def _():
        def smoothed(low, high):
            rows = slice(low, high)
            share = sides_share(near_ref[rows, :], far_ref[rows, :], gather_ref)
            return start_ref[rows, :] + take_ref[rows, :] * share

        smooth[0:first, :] = smoothed(0, first)
        smooth[base:total, :] = smoothed(base, total)
        part = lambda low: [smooth[low + f * half : low + (f + 1) * half, :] for f in range(SOLVED)]
        mine, _ = solve_rows(part(0), part(base), columns, factors)
        put_rows(held, first, parts, smoothed(first, own))
        send(first, own, 0).start()
        for f in range(SOLVED):
            smooth[f * half : (f + 1) * half, :] = mine[f]
        for low, high in spans(0, first, CHUNK):
            lag = lagged_ref[low:high, :].astype(F32)
            if high > SOLVED * half:
                lag = jnp.where(lax.broadcasted_iota(jnp.int32, lag.shape, 0) < SOLVED * half - low, lag, 0.0)
            put_rows(held, low, parts, smooth[low:high, :] + lag)

    @pl.when(lax.axis_index("sec") == 1)
    def _():
        for low, high in spans(0, base, CHUNK):
            smooth[low:high, :] = brief_ref[low:high, :].astype(F32)

        def keep(f, value):
            put_rows(held, f * half, parts, value)

        relax = lambda f: rates_ref[f : f + 1, :]
        tendency(lambda f: smooth[f * half : (f + 1) * half, :], fields, mask_ref[1:2, :], relax, keep)
        send(first, own, 0).start()

    send(0, first, 1).start()
    send(first, own, 0).wait()
    send(0, first, 1).wait()


def cost(us):
    return pl.CostEstimate(flops=int(us * 1e9), transcendentals=0, bytes_accessed=0)


def params(mib):
    return pltpu.CompilerParams(vmem_limit_bytes=mib << 20)


def shards(sections, neighbours, edge_weight, field_diff, vert_coef, relax_rate, precip_mask):
    _, fields, half, width = sections.shape
    shape = jax.ShapeDtypeStruct
    steps = up(up(2 * half, SUB) // SUB, 4)
    depth = steps * SUB
    own = fields * half
    total = up(own, TILE) + up(SOLVED * half, TILE)
    piece = up(-(-(total + half) // PIECES), SUB)

    mine = strips(sections)
    shorts = [shape((own, width), BF16), shape((SOLVED * half, width), BF16)]
    short, head = lax.cond(
        lax.axis_index("sec") == 0,
        pl.pallas_call(
            shorten_kernel,
            out_shape=shorts,
            in_specs=[ANY],
            out_specs=[VMEM] * 2,
            scratch_shapes=[pltpu.VMEM(mine.shape, F32), pltpu.SemaphoreType.DMA((4,))],
            compiler_params=params(4),
            cost_estimate=cost(3),
        ),
        lambda _: pl.pallas_call(
            nothing_kernel, out_shape=shorts, out_specs=[VMEM] * 2, compiler_params=params(4), cost_estimate=cost(3)
        )(),
        mine,
    )
    back = (1, 0, same, 0)
    state = route(mine, (0, 1, same, 0), back)
    near_rows = route(short, (0, 1, near, 0), back)
    far_rows = route(short, (0, 1, far, 0), back)
    dnear = route(head, (0, 1, near, 1), back)
    dfar = route(head, (0, 1, far, 1), back)

    pack = pl.pallas_call(
        pack_kernel,
        out_shape=shape((2 * SOLVED + 1, half, width), BF16),
        in_specs=[VMEM] * 3,
        out_specs=VMEM,
        compiler_params=params(4),
        cost_estimate=cost(0.01),
    )(head, state, vert_coef)
    pack = route(pack, (0, 1, same, 1), back)

    gather, lagged, rates, keep, take = pl.pallas_call(
        prepare_kernel,
        out_shape=[
            shape((7 * width, width), BF16),
            shape((own, width), BF16),
            shape((fields, width), F32),
            shape((total, width), F32),
            shape((total, width), F32),
        ],
        in_specs=[VMEM] * 5 + [SMEM] * 2,
        out_specs=[VMEM] * 5,
        scratch_shapes=[pltpu.VMEM((own, width), F32)] * 2,
        compiler_params=params(8),
        cost_estimate=cost(0.01),
    )(mine, short, neighbours, edge_weight, precip_mask, relax_rate, field_diff)

    chunk = shape((steps, SUB, width), F32)

    def ready(kernel, *operands):
        start, *factors = pl.pallas_call(
            kernel,
            out_shape=[chunk] * 5 + [shape((6, SUB, width), F32), shape((total, width), F32)],
            in_specs=[VMEM] * len(operands),
            out_specs=[VMEM] * 7,
            scratch_shapes=[
                pltpu.VMEM((total, width), F32),
                pltpu.VMEM((2 * half, width), F32),
                pltpu.VMEM((width // LANES, depth + 2 * SUB, LANES), F32),
                pltpu.VMEM((width // LANES, depth, LANES), F32),
            ],
            compiler_params=params(16),
            cost_estimate=cost(0),
        )(*operands)[::-1]
        return start, factors[::-1]

    start, factors = ready(ready_first_kernel, vert_coef, pack, state, lagged, keep, take, gather)

    scratch = [pltpu.VMEM((total, width), F32), pltpu.VMEM((SOLVED, width // LANES, depth, LANES), F32)]
    *full, brief = pl.pallas_call(
        first_kernel,
        out_shape=[shape((piece, width), F32)] * PIECES + [shape((total, width), BF16)],
        in_specs=[VMEM] * 15,
        out_specs=[VMEM] * (PIECES + 1),
        scratch_shapes=scratch,
        compiler_params=params(24),
    )(far_rows, near_rows, dfar, dnear, pack, start, lagged, take, gather, *factors)

    near_rows = route(brief, (1, 0, near, 0), (0, 1, same, 0))
    far_rows = route(brief, (1, 0, far, 0))
    pieces = [route(part, back, (0, 1, same, 0)) for part in full]
    start, factors = ready(
        functools.partial(ready_last_kernel, total), vert_coef, lagged, keep, take, gather, *pieces
    )
    out = pl.pallas_call(
        last_kernel,
        out_shape=shape(mine.shape, F32),
        in_specs=[VMEM] * 15,
        out_specs=ANY,
        scratch_shapes=scratch + [pltpu.VMEM(mine.shape, F32), pltpu.SemaphoreType.DMA((2,))],
        compiler_params=params(24),
    )(near_rows, far_rows, brief, start, lagged, precip_mask, rates, take, gather, *factors)
    return out.reshape(sections.shape)


def solution(mesh):
    return jax.shard_map(
        shards,
        mesh=mesh,
        in_specs=(
            P("sec", None, "lev", "dom"),
            P(None, "dom"),
            P(None, "dom"),
            P(),
            P("lev", "dom"),
            P(),
            P(None, "dom"),
        ),
        out_specs=P("sec", None, "lev", "dom"),
        check_vma=False,
    )
```

```python
import functools
import jax
import jax.numpy as jnp
from jax import lax
from jax.experimental import pallas as pl
from jax.experimental.pallas import tpu as pltpu
from jax.sharding import PartitionSpec as P

AXES = ("sec", "dom", "lev")
SOLVED = 2
EDGES = 3
SUB = 8
LANES = 128
TILE = 16
CHUNK = 32
PIECES = 3
VMEM = pl.BlockSpec(memory_space=pltpu.VMEM)
SMEM = pl.BlockSpec(memory_space=pltpu.SMEM)
ANY = pl.BlockSpec(memory_space=pl.ANY)
F32 = jnp.float32
BF16 = jnp.bfloat16


def up(count, unit):
    return -(-count // unit) * unit


def spans(low, high, size):
    return [(r, min(r + size, high)) for r in range(low, high, size)]


def route(array, *moves):
    doms, levs = lax.axis_size("dom"), lax.axis_size("lev")
    place = lambda s, d, v: (s * doms + d) * levs + v
    table = [
        (place(a, d, v), place(b, to_block(d) % doms, v ^ flip))
        for a, b, to_block, flip in moves
        for d in range(doms)
        for v in range(levs)
    ]
    return lax.ppermute(array, AXES, table)


def same(block):
    return block


def near(block):
    return block ^ 1


def far(block):
    return block - 1 if block % 2 == 0 else block + 1


def strips(array):
    return array.reshape(-1, LANES)


def get_rows(ref, low, high, parts):
    return jnp.concatenate([ref[pl.ds(low * parts + h, high - low, stride=parts), :] for h in range(parts)], axis=1)


def put_rows(ref, low, parts, value):
    for h in range(parts):
        ref[pl.ds(low * parts + h, value.shape[0], stride=parts), :] = value[:, h * LANES : (h + 1) * LANES]


def tendency(state, fields, mask, relax, emit):
    rounded = lambda f: state(f).astype(BF16).astype(F32)
    theta, vapour, cloud, rain = rounded(1), rounded(2), rounded(3), rounded(4)
    saturation = 0.6 * jnp.exp(0.25 * theta)
    condense = 0.5 * jnp.tanh(vapour - saturation)
    autoconv = 0.4 * cloud * cloud / (1.0 + cloud * cloud)
    evaporate = 0.3 * rain * rain / (1.0 + rain * rain) * jax.nn.sigmoid(saturation - vapour)
    micro = {
        1: 2.5 * (condense - evaporate),
        2: evaporate - condense,
        3: condense - autoconv,
        4: autoconv - evaporate,
    }
    for f in range(fields):
        clear = -relax(f) * rounded(f)
        if f in micro:
            clear = jnp.where(mask == 1, clear + micro[f], clear)
        emit(f, clear)


def shorten_kernel(mine_ref, short_ref, head_ref, wide, sems):
    own, width = short_ref.shape
    parts = width // LANES
    pieces = spans(0, own, up(-(-own // 2), TILE))
    copies = []
    for i, (low, high) in enumerate(pieces):
        rows = pl.ds(low * parts, (high - low) * parts)
        copies.append(pltpu.make_async_copy(mine_ref.at[rows], wide.at[rows], sems.at[i]))
        copies[-1].start()
    for copy, (start, stop) in zip(copies, pieces):
        copy.wait()
        for low, high in spans(start, stop, CHUNK):
            value = get_rows(wide, low, high, parts).astype(BF16)
            short_ref[low:high, :] = value
            end = min(high, head_ref.shape[0])
            if low < end:
                head_ref[low:end, :] = value[: end - low]


def nothing_kernel(short_ref, head_ref):
    head_ref[...] = jnp.zeros(head_ref.shape, BF16)


def pack_kernel(head_ref, other_ref, kappa_ref, pack_ref):
    _, half, width = pack_ref.shape
    parts = width // LANES

    @pl.when(lax.axis_index("sec") == 0)
    def _():
        for f in range(SOLVED):
            pack_ref[f] = head_ref[f * half : (f + 1) * half, :]
            pack_ref[SOLVED + f] = get_rows(other_ref, f * half, (f + 1) * half, parts).astype(BF16)

    pack_ref[2 * SOLVED] = kappa_ref[...].astype(BF16)


def prepare_kernel(
    mine_ref, short_ref, nbr_ref, weight_ref, mask_ref, relax_ref, diff_ref, gather_ref, lagged_ref, rates_ref, keep_ref, take_ref, work,
    lagged,
):
    fields = rates_ref.shape[0]
    width = nbr_ref.shape[1]
    half = lagged_ref.shape[0] // fields
    base = up(fields * half, TILE)
    odd = lax.axis_index("dom") % 2
    sides = (2 * width * (1 - odd), 2 * width * odd, width)
    for side, start in enumerate(sides):
        for low, high in spans(0, width, 64):
            place = lax.broadcasted_iota(jnp.int32, (high - low, width), 0) + (low + start)
            total = jnp.zeros((high - low, width), F32)
            for edge in range(EDGES):
                total = total + jnp.where(place == nbr_ref[edge : edge + 1, :], weight_ref[edge : edge + 1, :], 0.0)
            first = total.astype(BF16)
            at = 2 * side * width + low
            gather_ref[at : at + high - low, :] = first
            gather_ref[at + width : at + width + high - low, :] = (total - first.astype(F32)).astype(BF16)
            if side == 2:
                gather_ref[at + 2 * width : at + 2 * width + high - low, :] = first
    total = weight_ref[0:1, :] + weight_ref[1:2, :] + weight_ref[2:3, :]
    keep_ref[...] = jnp.zeros(keep_ref.shape, F32)
    take_ref[...] = jnp.zeros(take_ref.shape, F32)
    for f in range(fields):
        rates_ref[f : f + 1, :] = jnp.full((1, width), relax_ref[f], F32)
    for f in range(fields + SOLVED):
        low = f * half if f < fields else base + (f - fields) * half
        scale = diff_ref[f % fields]
        keep_ref[low : low + half, :] = jnp.broadcast_to(1.0 - scale * total, (half, width))
        take_ref[low : low + half, :] = jnp.full((half, width), scale, F32)

    @pl.when(lax.axis_index("sec") == 0)
    def _():
        def emit(f, value):
            lagged[f * half : (f + 1) * half, :] = value

        for low, high in spans(0, fields * half, CHUNK):
            work[low:high, :] = short_ref[low:high, :].astype(F32)
        tendency(
            lambda f: work[f * half : (f + 1) * half, :], fields, mask_ref[0:1, :], lambda f: relax_ref[f], emit
        )
        for low, high in spans(0, fields * half, CHUNK):
            lagged_ref[low:high, :] = lagged[low:high, :].astype(BF16)

    @pl.when(lax.axis_index("sec") == 1)
    def _():
        for low, high in spans(0, fields * half, CHUNK):
            lagged_ref[low:high, :] = get_rows(mine_ref, low, high, width // LANES).astype(BF16)


def shift(values, by):
    return pltpu.roll(values, by % SUB, 0)


def put(ref, start, value):
    for h in range(ref.shape[0]):
        ref[h, start : start + value.shape[0], :] = value[:, h * LANES : (h + 1) * LANES]


def get(ref, start, count):
    return jnp.concatenate([ref[h, start : start + count, :] for h in range(ref.shape[0])], axis=1)


def get_strided(ref, start, steps):
    rows = pl.ds(start, SUB, stride=steps)
    return jnp.concatenate([ref[h, rows, :] for h in range(ref.shape[0])], axis=1)


def put_strided(ref, start, steps, value):
    for h in range(ref.shape[0]):
        ref[h, pl.ds(start, SUB, stride=steps), :] = value[:, h * LANES : (h + 1) * LANES]


def ready_first_kernel(kappa_ref, pack_ref, state_ref, lagged_ref, keep_ref, take_ref, gather_ref, *rest):
    factors, (start_ref, middle, *work) = rest[:6], rest[6:]
    _, half, width = pack_ref.shape
    own = lagged_ref.shape[0]
    base = up(own, TILE)

    @pl.when(lax.axis_index("sec") == 1)
    def _():
        factor(kappa_ref, pack_ref[2 * SOLVED].astype(F32), *factors, *work)
        middle[0:own, :] = get_rows(state_ref, 0, own, width // LANES)
        for f in range(SOLVED):
            middle[base + f * half : base + (f + 1) * half, :] = pack_ref[f].astype(F32)
        own_share(start_ref, middle, lagged_ref, keep_ref, take_ref, gather_ref, half)


def ready_last_kernel(at, kappa_ref, lagged_ref, keep_ref, take_ref, gather_ref, *rest):
    pieces, factors, (start_ref, middle, *work) = rest[:PIECES], rest[PIECES : PIECES + 6], rest[PIECES + 6 :]
    half = kappa_ref.shape[0]
    piece = pieces[0].shape[0]

    @pl.when(lax.axis_index("sec") == 0)
    def _():
        factor(kappa_ref, pieces[at // piece][at % piece : at % piece + half, :], *factors, *work)
        for i in range(PIECES):
            low, high = i * piece, min((i + 1) * piece, middle.shape[0])
            middle[low:high, :] = pieces[i][0 : high - low, :]
        own_share(start_ref, middle, lagged_ref, keep_ref, take_ref, gather_ref, half)


def own_share(start_ref, middle, lagged_ref, keep_ref, take_ref, gather_ref, half):
    width = middle.shape[1]
    solved, own = SOLVED * half, lagged_ref.shape[0]
    values = middle[...]
    high = values.astype(BF16)
    low = (values - high.astype(F32)).astype(BF16)
    share = jnp.dot(
        jnp.concatenate([high, high, low], axis=1), gather_ref[4 * width : 7 * width, :], preferred_element_type=F32
    )
    start_ref[...] = values * keep_ref[...] + take_ref[...] * share
    for low, high in spans(solved // CHUNK * CHUNK, own, CHUNK):
        lag = lagged_ref[low:high, :].astype(F32)
        if low < solved:
            lag = jnp.where(lax.broadcasted_iota(jnp.int32, lag.shape, 0) >= solved - low, lag, 0.0)
        start_ref[low:high, :] += lag


def side_share(rows, gather_ref, side):
    width = rows.shape[1]
    return jnp.dot(
        jnp.concatenate([rows, rows], axis=1),
        gather_ref[2 * side * width : 2 * (side + 1) * width, :],
        preferred_element_type=F32,
    )


def sides_share(near_rows, far_rows, gather_ref):
    width = near_rows.shape[1]
    rows = jnp.concatenate([near_rows, near_rows, far_rows, far_rows], axis=1)
    return jnp.dot(rows, gather_ref[0 : 4 * width, :], preferred_element_type=F32)


def factor(own_ref, other, low_ref, fore_ref, inv_ref, high_ref, back_ref, scan_ref, kappa, ratio, inverse):
    half, width = own_ref.shape
    depth = 2 * half
    steps = low_ref.shape[0]
    level = lax.axis_index("lev")
    ratio[...] = jnp.zeros(ratio.shape, F32)
    inverse[...] = jnp.zeros(inverse.shape, F32)

    @pl.when(level == 0)
    def _():
        kappa[0:half, :] = own_ref[...]
        kappa[half:depth, :] = other

    @pl.when(level == 1)
    def _():
        kappa[0:half, :] = other
        kappa[half:depth, :] = own_ref[...]

    excess = jnp.ones((1, width), F32)
    for k in range(depth):
        here = kappa[k : k + 1, :]
        inv = 1.0 / (excess + here)
        down = here * inv
        put(inverse, k, inv)
        if k < depth - 1:
            put(ratio, SUB + k, down)
        excess = 1.0 + down * excess

    index = lax.broadcasted_iota(jnp.int32, (SUB, width), 0)
    running = None
    for t in range(steps):
        low = get_strided(ratio, SUB - 1 + t, steps)
        low_ref[t] = low
        running = low if running is None else running * low
        fore_ref[t] = running
        inv_ref[t] = get_strided(inverse, t, steps)
    one = jnp.where(index >= 1, running, 0.0)
    two = jnp.where(index >= 2, running * shift(running, 1), 0.0)
    four = jnp.where(index >= 4, two * shift(two, 2), 0.0)
    scan_ref[0], scan_ref[1], scan_ref[2] = one, two, four
    running = None
    for t in range(steps - 1, -1, -1):
        high = get_strided(ratio, SUB + t, steps)
        high_ref[t] = high
        running = high if running is None else running * high
        back_ref[t] = running
    one = jnp.where(index < SUB - 1, running, 0.0)
    two = jnp.where(index < SUB - 2, running * shift(running, -1), 0.0)
    four = jnp.where(index < SUB - 4, two * shift(two, -2), 0.0)
    scan_ref[3], scan_ref[4], scan_ref[5] = one, two, four


def solve(right, factors):
    low_ref, fore_ref, inv_ref, high_ref, back_ref, scan_ref = factors
    steps, _, width = low_ref.shape
    index = lax.broadcasted_iota(jnp.int32, (SUB, width), 0)
    rows = []
    for t in range(steps):
        row = get_strided(right, t, steps)
        if t:
            row = row + low_ref[t] * rows[-1]
        rows.append(row)
    carry = rows[-1]
    for i, by in enumerate((1, 2, 4)):
        carry = carry + scan_ref[i] * shift(carry, by)
    carry = jnp.where(index >= 1, shift(carry, 1), 0.0)
    rows = [(rows[t] + fore_ref[t] * carry) * inv_ref[t] for t in range(steps)]
    for t in range(steps - 2, -1, -1):
        rows[t] = rows[t] + high_ref[t] * rows[t + 1]
    carry = rows[0]
    for i, by in enumerate((1, 2, 4)):
        carry = carry + scan_ref[3 + i] * shift(carry, -by)
    carry = jnp.where(index < SUB - 1, shift(carry, -1), 0.0)
    for t in range(steps):
        put_strided(right, t, steps, rows[t] + back_ref[t] * carry)


def solve_rows(own, other, columns, factors):
    upper = lax.axis_index("lev") == 0
    half, width = own[0].shape
    depth = 2 * half
    for f in range(SOLVED):
        put(columns.at[f], depth, jnp.zeros((columns.shape[2] - depth, width), F32))
        put(columns.at[f], 0, jnp.where(upper, own[f], other[f]))
        put(columns.at[f], half, jnp.where(upper, other[f], own[f]))
    for f in range(SOLVED):
        solve(columns.at[f], factors)
    halves = [(get(columns.at[f], 0, half), get(columns.at[f], half, half)) for f in range(SOLVED)]
    return [jnp.where(upper, a, b) for a, b in halves], [jnp.where(upper, b, a) for a, b in halves]


def near_kernel(core, near_ref, start_ref, take_ref, gather_ref, out_ref):
    rows = slice(0, near_ref.shape[0])

    @pl.when(lax.axis_index("sec") == core)
    def _():
        out_ref[rows, :] = start_ref[rows, :] + take_ref[rows, :] * side_share(near_ref[...], gather_ref, 0)
        if near_ref.shape[0] < out_ref.shape[0]:
            rest = slice(up(near_ref.shape[0], TILE), out_ref.shape[0])
            out_ref[rest, :] = start_ref[rest, :]


def first_kernel(
    dfar_ref, dnear_ref, far_ref, pack_ref, start_ref, lagged_ref, take_ref, gather_ref, *rest
):
    factors, (*full_refs, short_ref, smooth, columns) = rest[:6], rest[6:]
    _, half, width = pack_ref.shape
    own = lagged_ref.shape[0]
    total = short_ref.shape[0]
    base = up(own, TILE)
    first = up(SOLVED * half, CHUNK)
    piece = full_refs[0].shape[0]

    def store(low, value):
        for i, (start, stop) in enumerate(spans(0, piece * PIECES, piece)):
            a, b = max(low, start), min(low + value.shape[0], stop)
            if a < b:
                full_refs[i][a - start : b - start, :] = value[a - low : b - low]

    def emit(low, value):
        short_ref[low : low + value.shape[0], :] = value.astype(BF16)
        store(low, value)

    @pl.when(lax.axis_index("sec") == 1)
    def _():
        others = slice(base, base + SOLVED * half)
        smooth[others, :] = start_ref[others, :] + take_ref[others, :] * sides_share(
            dnear_ref[...], dfar_ref[...], gather_ref
        )
        rows = slice(0, first)
        smooth[rows, :] = start_ref[rows, :] + take_ref[rows, :] * side_share(far_ref[rows, :], gather_ref, 1)
        part = lambda low: [smooth[low + f * half : low + (f + 1) * half, :] for f in range(SOLVED)]
        mine, theirs = solve_rows(part(0), part(base), columns, factors)
        rows = slice(first, own)
        value = start_ref[rows, :] + take_ref[rows, :] * side_share(far_ref[rows, :], gather_ref, 1)
        for low, high in spans(first, own, CHUNK):
            emit(low, value[low - first : high - first])
        for f in range(SOLVED):
            smooth[f * half : (f + 1) * half, :] = mine[f]
            smooth[base + f * half : base + (f + 1) * half, :] = theirs[f] + pack_ref[SOLVED + f].astype(F32)
        for low, high in spans(0, first, CHUNK):
            lag = lagged_ref[low:high, :].astype(F32)
            if high > SOLVED * half:
                lag = jnp.where(lax.broadcasted_iota(jnp.int32, lag.shape, 0) < SOLVED * half - low, lag, 0.0)
            emit(low, smooth[low:high, :] + lag)
        for low, high in spans(base, total, CHUNK):
            emit(low, smooth[low:high, :])
        store(total, pack_ref[2 * SOLVED].astype(F32))


def last_kernel(far_ref, brief_ref, start_ref, lagged_ref, mask_ref, rates_ref, take_ref, gather_ref, *rest):
    factors, (out_ref, smooth, columns, held, sems) = rest[:6], rest[6:]
    own, width = lagged_ref.shape
    fields = rates_ref.shape[0]
    half = own // fields
    base = up(own, TILE)
    total = far_ref.shape[0]
    parts = width // LANES
    first = up(SOLVED * half, CHUNK)

    def send(low, high, sem):
        rows = pl.ds(low * parts, (high - low) * parts)
        return pltpu.make_async_copy(held.at[rows], out_ref.at[rows], sems.at[sem])

    @pl.when(lax.axis_index("sec") == 0)
    def _():
        def smoothed(low, high):
            rows = slice(low, high)
            return start_ref[rows, :] + take_ref[rows, :] * side_share(far_ref[rows, :], gather_ref, 1)

        smooth[0:first, :] = smoothed(0, first)
        smooth[base:total, :] = smoothed(base, total)
        part = lambda low: [smooth[low + f * half : low + (f + 1) * half, :] for f in range(SOLVED)]
        mine, _ = solve_rows(part(0), part(base), columns, factors)
        put_rows(held, first, parts, smoothed(first, own))
        send(first, own, 0).start()
        for f in range(SOLVED):
            smooth[f * half : (f + 1) * half, :] = mine[f]
        for low, high in spans(0, first, CHUNK):
            lag = lagged_ref[low:high, :].astype(F32)
            if high > SOLVED * half:
                lag = jnp.where(lax.broadcasted_iota(jnp.int32, lag.shape, 0) < SOLVED * half - low, lag, 0.0)
            put_rows(held, low, parts, smooth[low:high, :] + lag)

    @pl.when(lax.axis_index("sec") == 1)
    def _():
        for low, high in spans(0, base, CHUNK):
            smooth[low:high, :] = brief_ref[low:high, :].astype(F32)

        def keep(f, value):
            put_rows(held, f * half, parts, value)

        relax = lambda f: rates_ref[f : f + 1, :]
        tendency(lambda f: smooth[f * half : (f + 1) * half, :], fields, mask_ref[1:2, :], relax, keep)
        send(first, own, 0).start()

    send(0, first, 1).start()
    send(first, own, 0).wait()
    send(0, first, 1).wait()


def cost(us):
    return pl.CostEstimate(flops=int(us * 1e9), transcendentals=0, bytes_accessed=0)


def params(mib):
    return pltpu.CompilerParams(vmem_limit_bytes=mib << 20)


def shards(sections, neighbours, edge_weight, field_diff, vert_coef, relax_rate, precip_mask):
    _, fields, half, width = sections.shape
    shape = jax.ShapeDtypeStruct
    steps = up(up(2 * half, SUB) // SUB, 4)
    depth = steps * SUB
    own = fields * half
    total = up(own, TILE) + up(SOLVED * half, TILE)
    piece = up(-(-(total + half) // PIECES), SUB)

    mine = strips(sections)
    shorts = [shape((own, width), BF16), shape((SOLVED * half, width), BF16)]
    short, head = lax.cond(
        lax.axis_index("sec") == 0,
        pl.pallas_call(
            shorten_kernel,
            out_shape=shorts,
            in_specs=[ANY],
            out_specs=[VMEM] * 2,
            scratch_shapes=[pltpu.VMEM(mine.shape, F32), pltpu.SemaphoreType.DMA((2,))],
            compiler_params=params(4),
            cost_estimate=cost(3),
        ),
        lambda _: pl.pallas_call(
            nothing_kernel, out_shape=shorts, out_specs=[VMEM] * 2, compiler_params=params(4), cost_estimate=cost(3)
        )(),
        mine,
    )
    back = (1, 0, same, 0)
    state = route(mine, (0, 1, same, 0), back)
    near_rows = route(short, (0, 1, near, 0), back)
    far_rows = route(short, (0, 1, far, 0), back)
    dnear = route(head, (0, 1, near, 1), back)
    dfar = route(head, (0, 1, far, 1), back)

    pack = pl.pallas_call(
        pack_kernel,
        out_shape=shape((2 * SOLVED + 1, half, width), BF16),
        in_specs=[VMEM] * 3,
        out_specs=VMEM,
        compiler_params=params(4),
        cost_estimate=cost(0.01),
    )(head, state, vert_coef)
    pack = route(pack, (0, 1, same, 1), back)

    gather, lagged, rates, keep, take = pl.pallas_call(
        prepare_kernel,
        out_shape=[
            shape((7 * width, width), BF16),
            shape((own, width), BF16),
            shape((fields, width), F32),
            shape((total, width), F32),
            shape((total, width), F32),
        ],
        in_specs=[VMEM] * 5 + [SMEM] * 2,
        out_specs=[VMEM] * 5,
        scratch_shapes=[pltpu.VMEM((own, width), F32)] * 2,
        compiler_params=params(8),
        cost_estimate=cost(0.01),
    )(mine, short, neighbours, edge_weight, precip_mask, relax_rate, field_diff)

    chunk = shape((steps, SUB, width), F32)

    def ready(kernel, *operands):
        start, *factors = pl.pallas_call(
            kernel,
            out_shape=[chunk] * 5 + [shape((6, SUB, width), F32), shape((total, width), F32)],
            in_specs=[VMEM] * len(operands),
            out_specs=[VMEM] * 7,
            scratch_shapes=[
                pltpu.VMEM((total, width), F32),
                pltpu.VMEM((2 * half, width), F32),
                pltpu.VMEM((width // LANES, depth + 2 * SUB, LANES), F32),
                pltpu.VMEM((width // LANES, depth, LANES), F32),
            ],
            compiler_params=params(16),
            cost_estimate=cost(0),
        )(*operands)[::-1]
        return start, factors[::-1]

    def with_near(core, rows, start):
        return pl.pallas_call(
            functools.partial(near_kernel, core),
            out_shape=shape((total, width), F32),
            in_specs=[VMEM] * 4,
            out_specs=VMEM,
            compiler_params=params(8),
            cost_estimate=cost(0),
        )(rows, start, take, gather)

    start, factors = ready(ready_first_kernel, vert_coef, pack, state, lagged, keep, take, gather)

    start = with_near(1, near_rows, start)

    scratch = [pltpu.VMEM((total, width), F32), pltpu.VMEM((SOLVED, width // LANES, depth, LANES), F32)]
    *full, brief = pl.pallas_call(
        first_kernel,
        out_shape=[shape((piece, width), F32)] * PIECES + [shape((total, width), BF16)],
        in_specs=[VMEM] * 14,
        out_specs=[VMEM] * (PIECES + 1),
        scratch_shapes=scratch,
        compiler_params=params(24),
    )(dfar, dnear, far_rows, pack, start, lagged, take, gather, *factors)

    near_rows = route(brief, (1, 0, near, 0))
    far_rows = route(brief, (1, 0, far, 0), (0, 1, same, 0))
    pieces = [route(part, back, (0, 1, same, 0)) for part in full]
    start, factors = ready(
        functools.partial(ready_last_kernel, total), vert_coef, lagged, keep, take, gather, *pieces
    )
    start = with_near(0, near_rows, start)
    out = pl.pallas_call(
        last_kernel,
        out_shape=shape(mine.shape, F32),
        in_specs=[VMEM] * 14,
        out_specs=ANY,
        scratch_shapes=scratch + [pltpu.VMEM(mine.shape, F32), pltpu.SemaphoreType.DMA((2,))],
        compiler_params=params(24),
    )(far_rows, brief, start, lagged, precip_mask, rates, take, gather, *factors)
    return out.reshape(sections.shape)


def solution(mesh):
    return jax.shard_map(
        shards,
        mesh=mesh,
        in_specs=(
            P("sec", None, "lev", "dom"),
            P(None, "dom"),
            P(None, "dom"),
            P(),
            P("lev", "dom"),
            P(),
            P(None, "dom"),
        ),
        out_specs=P("sec", None, "lev", "dom"),
        check_vma=False,
    )
```

```python
import functools
import jax
import jax.numpy as jnp
from jax import lax
from jax.experimental import pallas as pl
from jax.experimental.pallas import tpu as pltpu
from jax.sharding import PartitionSpec as P

AXES = ("sec", "dom", "lev")
SOLVED = 2
EDGES = 3
SUB = 8
LANES = 128
TILE = 16
CHUNK = 32
PIECES = 3
VMEM = pl.BlockSpec(memory_space=pltpu.VMEM)
SMEM = pl.BlockSpec(memory_space=pltpu.SMEM)
ANY = pl.BlockSpec(memory_space=pl.ANY)
F32 = jnp.float32
BF16 = jnp.bfloat16


def up(count, unit):
    return -(-count // unit) * unit


def spans(low, high, size):
    return [(r, min(r + size, high)) for r in range(low, high, size)]


def route(array, *moves):
    doms, levs = lax.axis_size("dom"), lax.axis_size("lev")
    place = lambda s, d, v: (s * doms + d) * levs + v
    table = [
        (place(a, d, v), place(b, to_block(d) % doms, v ^ flip))
        for a, b, to_block, flip in moves
        for d in range(doms)
        for v in range(levs)
    ]
    return lax.ppermute(array, AXES, table)


def same(block):
    return block


def near(block):
    return block ^ 1


def far(block):
    return block - 1 if block % 2 == 0 else block + 1


def strips(array):
    return array.reshape(-1, LANES)


def get_rows(ref, low, high, parts):
    return jnp.concatenate([ref[pl.ds(low * parts + h, high - low, stride=parts), :] for h in range(parts)], axis=1)


def put_rows(ref, low, parts, value):
    for h in range(parts):
        ref[pl.ds(low * parts + h, value.shape[0], stride=parts), :] = value[:, h * LANES : (h + 1) * LANES]


def tendency(state, fields, mask, relax, emit):
    rounded = lambda f: state(f).astype(BF16).astype(F32)
    theta, vapour, cloud, rain = rounded(1), rounded(2), rounded(3), rounded(4)
    saturation = 0.6 * jnp.exp(0.25 * theta)
    condense = 0.5 * jnp.tanh(vapour - saturation)
    autoconv = 0.4 * cloud * cloud / (1.0 + cloud * cloud)
    evaporate = 0.3 * rain * rain / (1.0 + rain * rain) * jax.nn.sigmoid(saturation - vapour)
    micro = {
        1: 2.5 * (condense - evaporate),
        2: evaporate - condense,
        3: condense - autoconv,
        4: autoconv - evaporate,
    }
    for f in range(fields):
        clear = -relax(f) * rounded(f)
        if f in micro:
            clear = jnp.where(mask == 1, clear + micro[f], clear)
        emit(f, clear)


def shorten_kernel(mine_ref, short_ref, head_ref, wide, sems):
    own, width = short_ref.shape
    parts = width // LANES
    pieces = spans(0, own, up(-(-own // 2), TILE))
    copies = []
    for i, (low, high) in enumerate(pieces):
        rows = pl.ds(low * parts, (high - low) * parts)
        copies.append(pltpu.make_async_copy(mine_ref.at[rows], wide.at[rows], sems.at[i]))
        copies[-1].start()
    for copy, (start, stop) in zip(copies, pieces):
        copy.wait()
        for low, high in spans(start, stop, CHUNK):
            value = get_rows(wide, low, high, parts).astype(BF16)
            short_ref[low:high, :] = value
            end = min(high, head_ref.shape[0])
            if low < end:
                head_ref[low:end, :] = value[: end - low]


def nothing_kernel(short_ref, head_ref):
    head_ref[...] = jnp.zeros(head_ref.shape, BF16)


def pack_kernel(head_ref, other_ref, kappa_ref, pack_ref):
    _, half, width = pack_ref.shape
    parts = width // LANES

    @pl.when(lax.axis_index("sec") == 0)
    def _():
        head = head_ref[...].astype(F32)
        for f in range(SOLVED):
            pack_ref[f] = head[f * half : (f + 1) * half].astype(BF16)
            pack_ref[SOLVED + f] = get_rows(other_ref, f * half, (f + 1) * half, parts).astype(BF16)

    pack_ref[2 * SOLVED] = kappa_ref[...].astype(BF16)


def prepare_kernel(
    mine_ref, short_ref, nbr_ref, weight_ref, mask_ref, relax_ref, diff_ref, gather_ref, lagged_ref, rates_ref, keep_ref, take_ref, work,
    lagged,
):
    fields = rates_ref.shape[0]
    width = nbr_ref.shape[1]
    half = lagged_ref.shape[0] // fields
    base = up(fields * half, TILE)
    odd = lax.axis_index("dom") % 2
    sides = (2 * width * (1 - odd), 2 * width * odd, width)
    for side, start in enumerate(sides):
        for low, high in spans(0, width, 64):
            place = lax.broadcasted_iota(jnp.int32, (high - low, width), 0) + (low + start)
            total = jnp.zeros((high - low, width), F32)
            for edge in range(EDGES):
                total = total + jnp.where(place == nbr_ref[edge : edge + 1, :], weight_ref[edge : edge + 1, :], 0.0)
            first = total.astype(BF16)
            at = 2 * side * width + low
            gather_ref[at : at + high - low, :] = first
            gather_ref[at + width : at + width + high - low, :] = (total - first.astype(F32)).astype(BF16)
            if side == 2:
                gather_ref[at + 2 * width : at + 2 * width + high - low, :] = first
    total = weight_ref[0:1, :] + weight_ref[1:2, :] + weight_ref[2:3, :]
    keep_ref[...] = jnp.zeros(keep_ref.shape, F32)
    take_ref[...] = jnp.zeros(take_ref.shape, F32)
    for f in range(fields):
        rates_ref[f : f + 1, :] = jnp.full((1, width), relax_ref[f], F32)
    for f in range(fields + SOLVED):
        low = f * half if f < fields else base + (f - fields) * half
        scale = diff_ref[f % fields]
        keep_ref[low : low + half, :] = jnp.broadcast_to(1.0 - scale * total, (half, width))
        take_ref[low : low + half, :] = jnp.full((half, width), scale, F32)

    @pl.when(lax.axis_index("sec") == 0)
    def _():
        def emit(f, value):
            lagged[f * half : (f + 1) * half, :] = value

        for low, high in spans(0, fields * half, CHUNK):
            work[low:high, :] = short_ref[low:high, :].astype(F32)
        tendency(
            lambda f: work[f * half : (f + 1) * half, :], fields, mask_ref[0:1, :], lambda f: relax_ref[f], emit
        )
        for low, high in spans(0, fields * half, CHUNK):
            lagged_ref[low:high, :] = lagged[low:high, :].astype(BF16)

    @pl.when(lax.axis_index("sec") == 1)
    def _():
        for low, high in spans(0, fields * half, CHUNK):
            lagged_ref[low:high, :] = get_rows(mine_ref, low, high, width // LANES).astype(BF16)


def shift(values, by):
    return pltpu.roll(values, by % SUB, 0)


def put(ref, start, value):
    for h in range(ref.shape[0]):
        ref[h, start : start + value.shape[0], :] = value[:, h * LANES : (h + 1) * LANES]


def get(ref, start, count):
    return jnp.concatenate([ref[h, start : start + count, :] for h in range(ref.shape[0])], axis=1)


def get_strided(ref, start, steps):
    rows = pl.ds(start, SUB, stride=steps)
    return jnp.concatenate([ref[h, rows, :] for h in range(ref.shape[0])], axis=1)


def put_strided(ref, start, steps, value):
    for h in range(ref.shape[0]):
        ref[h, pl.ds(start, SUB, stride=steps), :] = value[:, h * LANES : (h + 1) * LANES]


def ready_first_kernel(kappa_ref, pack_ref, state_ref, lagged_ref, keep_ref, take_ref, gather_ref, *rest):
    factors, (start_ref, middle, *work) = rest[:6], rest[6:]
    _, half, width = pack_ref.shape
    own = lagged_ref.shape[0]
    base = up(own, TILE)

    @pl.when(lax.axis_index("sec") == 1)
    def _():
        factor(kappa_ref, pack_ref[2 * SOLVED].astype(F32), *factors, *work)
        middle[0:own, :] = get_rows(state_ref, 0, own, width // LANES)
        for f in range(SOLVED):
            middle[base + f * half : base + (f + 1) * half, :] = pack_ref[f].astype(F32)
        own_share(start_ref, middle, lagged_ref, keep_ref, take_ref, gather_ref, half)


def ready_last_kernel(at, kappa_ref, lagged_ref, keep_ref, take_ref, gather_ref, *rest):
    pieces, factors, (start_ref, middle, *work) = rest[:PIECES], rest[PIECES : PIECES + 6], rest[PIECES + 6 :]
    half = kappa_ref.shape[0]
    piece = pieces[0].shape[0]

    @pl.when(lax.axis_index("sec") == 0)
    def _():
        factor(kappa_ref, pieces[at // piece][at % piece : at % piece + half, :], *factors, *work)
        for i in range(PIECES):
            low, high = i * piece, min((i + 1) * piece, middle.shape[0])
            middle[low:high, :] = pieces[i][0 : high - low, :]
        own_share(start_ref, middle, lagged_ref, keep_ref, take_ref, gather_ref, half)


def own_share(start_ref, middle, lagged_ref, keep_ref, take_ref, gather_ref, half):
    width = middle.shape[1]
    solved, own = SOLVED * half, lagged_ref.shape[0]
    values = middle[...]
    high = values.astype(BF16)
    low = (values - high.astype(F32)).astype(BF16)
    share = jnp.dot(
        jnp.concatenate([high, high, low], axis=1), gather_ref[4 * width : 7 * width, :], preferred_element_type=F32
    )
    start_ref[...] = values * keep_ref[...] + take_ref[...] * share
    for low, high in spans(solved // CHUNK * CHUNK, own, CHUNK):
        lag = lagged_ref[low:high, :].astype(F32)
        if low < solved:
            lag = jnp.where(lax.broadcasted_iota(jnp.int32, lag.shape, 0) >= solved - low, lag, 0.0)
        start_ref[low:high, :] += lag


def side_share(rows, gather_ref, side):
    width = rows.shape[1]
    return jnp.dot(
        jnp.concatenate([rows, rows], axis=1),
        gather_ref[2 * side * width : 2 * (side + 1) * width, :],
        preferred_element_type=F32,
    )


def sides_share(near_rows, far_rows, gather_ref):
    width = near_rows.shape[1]
    rows = jnp.concatenate([near_rows, near_rows, far_rows, far_rows], axis=1)
    return jnp.dot(rows, gather_ref[0 : 4 * width, :], preferred_element_type=F32)


def factor(own_ref, other, low_ref, fore_ref, inv_ref, high_ref, back_ref, scan_ref, kappa, ratio, inverse):
    half, width = own_ref.shape
    depth = 2 * half
    steps = low_ref.shape[0]
    level = lax.axis_index("lev")
    ratio[...] = jnp.zeros(ratio.shape, F32)
    inverse[...] = jnp.zeros(inverse.shape, F32)

    @pl.when(level == 0)
    def _():
        kappa[0:half, :] = own_ref[...]
        kappa[half:depth, :] = other

    @pl.when(level == 1)
    def _():
        kappa[0:half, :] = other
        kappa[half:depth, :] = own_ref[...]

    excess = jnp.ones((1, width), F32)
    for k in range(depth):
        here = kappa[k : k + 1, :]
        inv = 1.0 / (excess + here)
        down = here * inv
        put(inverse, k, inv)
        if k < depth - 1:
            put(ratio, SUB + k, down)
        excess = 1.0 + down * excess

    index = lax.broadcasted_iota(jnp.int32, (SUB, width), 0)
    running = None
    for t in range(steps):
        low = get_strided(ratio, SUB - 1 + t, steps)
        low_ref[t] = low
        running = low if running is None else running * low
        fore_ref[t] = running
        inv_ref[t] = get_strided(inverse, t, steps)
    one = jnp.where(index >= 1, running, 0.0)
    two = jnp.where(index >= 2, running * shift(running, 1), 0.0)
    four = jnp.where(index >= 4, two * shift(two, 2), 0.0)
    scan_ref[0], scan_ref[1], scan_ref[2] = one, two, four
    running = None
    for t in range(steps - 1, -1, -1):
        high = get_strided(ratio, SUB + t, steps)
        high_ref[t] = high
        running = high if running is None else running * high
        back_ref[t] = running
    one = jnp.where(index < SUB - 1, running, 0.0)
    two = jnp.where(index < SUB - 2, running * shift(running, -1), 0.0)
    four = jnp.where(index < SUB - 4, two * shift(two, -2), 0.0)
    scan_ref[3], scan_ref[4], scan_ref[5] = one, two, four


def solve(right, factors):
    low_ref, fore_ref, inv_ref, high_ref, back_ref, scan_ref = factors
    steps, _, width = low_ref.shape
    index = lax.broadcasted_iota(jnp.int32, (SUB, width), 0)
    rows = []
    for t in range(steps):
        row = get_strided(right, t, steps)
        if t:
            row = row + low_ref[t] * rows[-1]
        rows.append(row)
    carry = rows[-1]
    for i, by in enumerate((1, 2, 4)):
        carry = carry + scan_ref[i] * shift(carry, by)
    carry = jnp.where(index >= 1, shift(carry, 1), 0.0)
    rows = [(rows[t] + fore_ref[t] * carry) * inv_ref[t] for t in range(steps)]
    for t in range(steps - 2, -1, -1):
        rows[t] = rows[t] + high_ref[t] * rows[t + 1]
    carry = rows[0]
    for i, by in enumerate((1, 2, 4)):
        carry = carry + scan_ref[3 + i] * shift(carry, -by)
    carry = jnp.where(index < SUB - 1, shift(carry, -1), 0.0)
    for t in range(steps):
        put_strided(right, t, steps, rows[t] + back_ref[t] * carry)


def solve_rows(own, other, columns, factors):
    upper = lax.axis_index("lev") == 0
    half, width = own[0].shape
    depth = 2 * half
    for f in range(SOLVED):
        put(columns.at[f], depth, jnp.zeros((columns.shape[2] - depth, width), F32))
        put(columns.at[f], 0, jnp.where(upper, own[f], other[f]))
        put(columns.at[f], half, jnp.where(upper, other[f], own[f]))
    for f in range(SOLVED):
        solve(columns.at[f], factors)
    halves = [(get(columns.at[f], 0, half), get(columns.at[f], half, half)) for f in range(SOLVED)]
    return [jnp.where(upper, a, b) for a, b in halves], [jnp.where(upper, b, a) for a, b in halves]


def near_kernel(core, near_ref, start_ref, take_ref, gather_ref, out_ref):
    rows = slice(0, near_ref.shape[0])

    @pl.when(lax.axis_index("sec") == core)
    def _():
        out_ref[rows, :] = start_ref[rows, :] + take_ref[rows, :] * side_share(near_ref[...], gather_ref, 0)
        if near_ref.shape[0] < out_ref.shape[0]:
            rest = slice(up(near_ref.shape[0], TILE), out_ref.shape[0])
            out_ref[rest, :] = start_ref[rest, :]


def first_kernel(
    dfar_ref, dnear_ref, far_ref, pack_ref, start_ref, lagged_ref, take_ref, gather_ref, *rest
):
    factors, (*full_refs, short_ref, smooth, columns) = rest[:6], rest[6:]
    _, half, width = pack_ref.shape
    own = lagged_ref.shape[0]
    total = short_ref.shape[0]
    base = up(own, TILE)
    first = up(SOLVED * half, CHUNK)
    piece = full_refs[0].shape[0]

    def store(low, value):
        for i, (start, stop) in enumerate(spans(0, piece * PIECES, piece)):
            a, b = max(low, start), min(low + value.shape[0], stop)
            if a < b:
                full_refs[i][a - start : b - start, :] = value[a - low : b - low]

    def emit(low, value):
        short_ref[low : low + value.shape[0], :] = value.astype(BF16)
        store(low, value)

    @pl.when(lax.axis_index("sec") == 1)
    def _():
        others = slice(base, base + SOLVED * half)
        smooth[others, :] = start_ref[others, :] + take_ref[others, :] * sides_share(
            dnear_ref[...], dfar_ref[...], gather_ref
        )
        rows = slice(0, first)
        smooth[rows, :] = start_ref[rows, :] + take_ref[rows, :] * side_share(far_ref[rows, :], gather_ref, 1)
        part = lambda low: [smooth[low + f * half : low + (f + 1) * half, :] for f in range(SOLVED)]
        mine, theirs = solve_rows(part(0), part(base), columns, factors)
        rows = slice(first, own)
        value = start_ref[rows, :] + take_ref[rows, :] * side_share(far_ref[rows, :], gather_ref, 1)
        for low, high in spans(first, own, CHUNK):
            emit(low, value[low - first : high - first])
        for f in range(SOLVED):
            smooth[f * half : (f + 1) * half, :] = mine[f]
            smooth[base + f * half : base + (f + 1) * half, :] = theirs[f] + pack_ref[SOLVED + f].astype(F32)
        for low, high in spans(0, first, CHUNK):
            lag = lagged_ref[low:high, :].astype(F32)
            if high > SOLVED * half:
                lag = jnp.where(lax.broadcasted_iota(jnp.int32, lag.shape, 0) < SOLVED * half - low, lag, 0.0)
            emit(low, smooth[low:high, :] + lag)
        for low, high in spans(base, total, CHUNK):
            emit(low, smooth[low:high, :])
        store(total, pack_ref[2 * SOLVED].astype(F32))


def last_kernel(far_ref, brief_ref, start_ref, lagged_ref, mask_ref, rates_ref, take_ref, gather_ref, *rest):
    factors, (out_ref, smooth, columns, held, sems) = rest[:6], rest[6:]
    own, width = lagged_ref.shape
    fields = rates_ref.shape[0]
    half = own // fields
    base = up(own, TILE)
    total = far_ref.shape[0]
    parts = width // LANES
    first = up(SOLVED * half, CHUNK)

    def send(low, high, sem):
        rows = pl.ds(low * parts, (high - low) * parts)
        return pltpu.make_async_copy(held.at[rows], out_ref.at[rows], sems.at[sem])

    @pl.when(lax.axis_index("sec") == 0)
    def _():
        def smoothed(low, high):
            rows = slice(low, high)
            return start_ref[rows, :] + take_ref[rows, :] * side_share(far_ref[rows, :], gather_ref, 1)

        smooth[0:first, :] = smoothed(0, first)
        smooth[base:total, :] = smoothed(base, total)
        part = lambda low: [smooth[low + f * half : low + (f + 1) * half, :] for f in range(SOLVED)]
        mine, _ = solve_rows(part(0), part(base), columns, factors)
        put_rows(held, first, parts, smoothed(first, own))
        send(first, own, 0).start()
        for f in range(SOLVED):
            smooth[f * half : (f + 1) * half, :] = mine[f]
        for low, high in spans(0, first, CHUNK):
            lag = lagged_ref[low:high, :].astype(F32)
            if high > SOLVED * half:
                lag = jnp.where(lax.broadcasted_iota(jnp.int32, lag.shape, 0) < SOLVED * half - low, lag, 0.0)
            put_rows(held, low, parts, smooth[low:high, :] + lag)

    @pl.when(lax.axis_index("sec") == 1)
    def _():
        for low, high in spans(0, base, CHUNK):
            smooth[low:high, :] = brief_ref[low:high, :].astype(F32)

        def keep(f, value):
            put_rows(held, f * half, parts, value)

        relax = lambda f: rates_ref[f : f + 1, :]
        tendency(lambda f: smooth[f * half : (f + 1) * half, :], fields, mask_ref[1:2, :], relax, keep)
        send(first, own, 0).start()

    send(0, first, 1).start()
    send(first, own, 0).wait()
    send(0, first, 1).wait()


def cost(us):
    return pl.CostEstimate(flops=int(us * 1e9), transcendentals=0, bytes_accessed=0)


def params(mib):
    return pltpu.CompilerParams(vmem_limit_bytes=mib << 20)


def shards(sections, neighbours, edge_weight, field_diff, vert_coef, relax_rate, precip_mask):
    _, fields, half, width = sections.shape
    shape = jax.ShapeDtypeStruct
    steps = up(up(2 * half, SUB) // SUB, 4)
    depth = steps * SUB
    own = fields * half
    total = up(own, TILE) + up(SOLVED * half, TILE)
    piece = up(-(-(total + half) // PIECES), SUB)

    mine = strips(sections)
    shorts = [shape((own, width), BF16), shape((SOLVED * half, width), BF16)]
    short, head = lax.cond(
        lax.axis_index("sec") == 0,
        pl.pallas_call(
            shorten_kernel,
            out_shape=shorts,
            in_specs=[ANY],
            out_specs=[VMEM] * 2,
            scratch_shapes=[pltpu.VMEM(mine.shape, F32), pltpu.SemaphoreType.DMA((2,))],
            compiler_params=params(4),
            cost_estimate=cost(3),
        ),
        lambda _: pl.pallas_call(
            nothing_kernel, out_shape=shorts, out_specs=[VMEM] * 2, compiler_params=params(4), cost_estimate=cost(3)
        )(),
        mine,
    )
    back = (1, 0, same, 0)
    state = route(mine, (0, 1, same, 0), back)
    near_rows = route(short, (0, 1, near, 0), back)
    far_rows = route(short, (0, 1, far, 0), back)
    dnear = route(head, (0, 1, near, 1), back)
    dfar = route(head, (0, 1, far, 1), back)

    pack = pl.pallas_call(
        pack_kernel,
        out_shape=shape((2 * SOLVED + 1, half, width), BF16),
        in_specs=[VMEM] * 3,
        out_specs=VMEM,
        compiler_params=params(4),
        cost_estimate=cost(0.01),
    )(head, state, vert_coef)
    pack = route(pack, (0, 1, same, 1), back)

    gather, lagged, rates, keep, take = pl.pallas_call(
        prepare_kernel,
        out_shape=[
            shape((7 * width, width), BF16),
            shape((own, width), BF16),
            shape((fields, width), F32),
            shape((total, width), F32),
            shape((total, width), F32),
        ],
        in_specs=[VMEM] * 5 + [SMEM] * 2,
        out_specs=[VMEM] * 5,
        scratch_shapes=[pltpu.VMEM((own, width), F32)] * 2,
        compiler_params=params(8),
        cost_estimate=cost(0.01),
    )(mine, short, neighbours, edge_weight, precip_mask, relax_rate, field_diff)

    chunk = shape((steps, SUB, width), F32)

    def ready(kernel, *operands):
        start, *factors = pl.pallas_call(
            kernel,
            out_shape=[chunk] * 5 + [shape((6, SUB, width), F32), shape((total, width), F32)],
            in_specs=[VMEM] * len(operands),
            out_specs=[VMEM] * 7,
            scratch_shapes=[
                pltpu.VMEM((total, width), F32),
                pltpu.VMEM((2 * half, width), F32),
                pltpu.VMEM((width // LANES, depth + 2 * SUB, LANES), F32),
                pltpu.VMEM((width // LANES, depth, LANES), F32),
            ],
            compiler_params=params(16),
            cost_estimate=cost(0),
        )(*operands)[::-1]
        return start, factors[::-1]

    def with_near(core, rows, start):
        return pl.pallas_call(
            functools.partial(near_kernel, core),
            out_shape=shape((total, width), F32),
            in_specs=[VMEM] * 4,
            out_specs=VMEM,
            compiler_params=params(8),
            cost_estimate=cost(0),
        )(rows, start, take, gather)

    start, factors = ready(ready_first_kernel, vert_coef, pack, state, lagged, keep, take, gather)

    start = with_near(1, near_rows, start)

    scratch = [pltpu.VMEM((total, width), F32), pltpu.VMEM((SOLVED, width // LANES, depth, LANES), F32)]
    *full, brief = pl.pallas_call(
        first_kernel,
        out_shape=[shape((piece, width), F32)] * PIECES + [shape((total, width), BF16)],
        in_specs=[VMEM] * 14,
        out_specs=[VMEM] * (PIECES + 1),
        scratch_shapes=scratch,
        compiler_params=params(24),
    )(dfar, dnear, far_rows, pack, start, lagged, take, gather, *factors)

    near_rows = route(brief, (1, 0, near, 0))
    far_rows = route(brief, (1, 0, far, 0), (0, 1, same, 0))
    pieces = [route(part, back, (0, 1, same, 0)) for part in full]
    start, factors = ready(
        functools.partial(ready_last_kernel, total), vert_coef, lagged, keep, take, gather, *pieces
    )
    start = with_near(0, near_rows, start)
    out = pl.pallas_call(
        last_kernel,
        out_shape=shape(mine.shape, F32),
        in_specs=[VMEM] * 14,
        out_specs=ANY,
        scratch_shapes=scratch + [pltpu.VMEM(mine.shape, F32), pltpu.SemaphoreType.DMA((2,))],
        compiler_params=params(24),
    )(far_rows, brief, start, lagged, precip_mask, rates, take, gather, *factors)
    return out.reshape(sections.shape)


def solution(mesh):
    return jax.shard_map(
        shards,
        mesh=mesh,
        in_specs=(
            P("sec", None, "lev", "dom"),
            P(None, "dom"),
            P(None, "dom"),
            P(),
            P("lev", "dom"),
            P(),
            P(None, "dom"),
        ),
        out_specs=P("sec", None, "lev", "dom"),
        check_vma=False,
    )
```

```python
import functools
import jax
import jax.numpy as jnp
from jax import lax
from jax.experimental import pallas as pl
from jax.experimental.pallas import tpu as pltpu
from jax.sharding import PartitionSpec as P

AXES = ("sec", "dom", "lev")
SOLVED = 2
EDGES = 3
SUB = 8
LANES = 128
TILE = 16
CHUNK = 32
PIECES = 3
VMEM = pl.BlockSpec(memory_space=pltpu.VMEM)
SMEM = pl.BlockSpec(memory_space=pltpu.SMEM)
ANY = pl.BlockSpec(memory_space=pl.ANY)
F32 = jnp.float32
BF16 = jnp.bfloat16


def up(count, unit):
    return -(-count // unit) * unit


def spans(low, high, size):
    return [(r, min(r + size, high)) for r in range(low, high, size)]


def route(array, *moves):
    doms, levs = lax.axis_size("dom"), lax.axis_size("lev")
    place = lambda s, d, v: (s * doms + d) * levs + v
    table = [
        (place(a, d, v), place(b, to_block(d) % doms, v ^ flip))
        for a, b, to_block, flip in moves
        for d in range(doms)
        for v in range(levs)
    ]
    return lax.ppermute(array, AXES, table)


def same(block):
    return block


def near(block):
    return block ^ 1


def far(block):
    return block - 1 if block % 2 == 0 else block + 1


def strips(array):
    return array.reshape(-1, LANES)


def get_rows(ref, low, high, parts):
    return jnp.concatenate([ref[pl.ds(low * parts + h, high - low, stride=parts), :] for h in range(parts)], axis=1)


def put_rows(ref, low, parts, value):
    for h in range(parts):
        ref[pl.ds(low * parts + h, value.shape[0], stride=parts), :] = value[:, h * LANES : (h + 1) * LANES]


def tendency(state, fields, mask, relax, emit):
    rounded = lambda f: state(f).astype(BF16).astype(F32)
    theta, vapour, cloud, rain = rounded(1), rounded(2), rounded(3), rounded(4)
    saturation = 0.6 * jnp.exp(0.25 * theta)
    condense = 0.5 * jnp.tanh(vapour - saturation)
    autoconv = 0.4 * cloud * cloud / (1.0 + cloud * cloud)
    evaporate = 0.3 * rain * rain / (1.0 + rain * rain) * jax.nn.sigmoid(saturation - vapour)
    micro = {
        1: 2.5 * (condense - evaporate),
        2: evaporate - condense,
        3: condense - autoconv,
        4: autoconv - evaporate,
    }
    for f in range(fields):
        clear = -relax(f) * rounded(f)
        if f in micro:
            clear = jnp.where(mask == 1, clear + micro[f], clear)
        emit(f, clear)


def shorten_kernel(mine_ref, short_ref, head_ref, wide, sems):
    own, width = short_ref.shape
    parts = width // LANES
    pieces = spans(0, own, up(-(-own // 2), TILE))
    copies = []
    for i, (low, high) in enumerate(pieces):
        rows = pl.ds(low * parts, (high - low) * parts)
        copies.append(pltpu.make_async_copy(mine_ref.at[rows], wide.at[rows], sems.at[i]))
        copies[-1].start()
    for copy, (start, stop) in zip(copies, pieces):
        copy.wait()
        for low, high in spans(start, stop, CHUNK):
            value = get_rows(wide, low, high, parts).astype(BF16)
            short_ref[low:high, :] = value
            end = min(high, head_ref.shape[0])
            if low < end:
                head_ref[low:end, :] = value[: end - low]


def nothing_kernel(short_ref, head_ref):
    head_ref[...] = jnp.zeros(head_ref.shape, BF16)


def pack_kernel(head_ref, other_ref, kappa_ref, pack_ref):
    _, half, width = pack_ref.shape
    parts = width // LANES

    @pl.when(lax.axis_index("sec") == 0)
    def _():
        head = head_ref[...].astype(F32)
        for f in range(SOLVED):
            pack_ref[f] = head[f * half : (f + 1) * half].astype(BF16)
            pack_ref[SOLVED + f] = get_rows(other_ref, f * half, (f + 1) * half, parts).astype(BF16)

    pack_ref[2 * SOLVED] = kappa_ref[...].astype(BF16)


def prepare_kernel(
    mine_ref, short_ref, nbr_ref, weight_ref, mask_ref, relax_ref, diff_ref, gather_ref, lagged_ref, rates_ref, keep_ref, take_ref, work,
    lagged,
):
    fields = rates_ref.shape[0]
    width = nbr_ref.shape[1]
    half = lagged_ref.shape[0] // fields
    base = up(fields * half, TILE)
    odd = lax.axis_index("dom") % 2
    sides = (2 * width * (1 - odd), 2 * width * odd, width)
    for side, start in enumerate(sides):
        for low, high in spans(0, width, 64):
            place = lax.broadcasted_iota(jnp.int32, (high - low, width), 0) + (low + start)
            total = jnp.zeros((high - low, width), F32)
            for edge in range(EDGES):
                total = total + jnp.where(place == nbr_ref[edge : edge + 1, :], weight_ref[edge : edge + 1, :], 0.0)
            first = total.astype(BF16)
            at = 2 * side * width + low
            gather_ref[at : at + high - low, :] = first
            gather_ref[at + width : at + width + high - low, :] = (total - first.astype(F32)).astype(BF16)
            if side == 2:
                gather_ref[at + 2 * width : at + 2 * width + high - low, :] = first
    total = weight_ref[0:1, :] + weight_ref[1:2, :] + weight_ref[2:3, :]
    keep_ref[...] = jnp.zeros(keep_ref.shape, F32)
    take_ref[...] = jnp.zeros(take_ref.shape, F32)
    for f in range(fields):
        rates_ref[f : f + 1, :] = jnp.full((1, width), relax_ref[f], F32)
    for f in range(fields + SOLVED):
        low = f * half if f < fields else base + (f - fields) * half
        scale = diff_ref[f % fields]
        keep_ref[low : low + half, :] = jnp.broadcast_to(1.0 - scale * total, (half, width))
        take_ref[low : low + half, :] = jnp.full((half, width), scale, F32)

    @pl.when(lax.axis_index("sec") == 0)
    def _():
        def emit(f, value):
            lagged[f * half : (f + 1) * half, :] = value

        for low, high in spans(0, fields * half, CHUNK):
            work[low:high, :] = short_ref[low:high, :].astype(F32)
        tendency(
            lambda f: work[f * half : (f + 1) * half, :], fields, mask_ref[0:1, :], lambda f: relax_ref[f], emit
        )
        for low, high in spans(0, fields * half, CHUNK):
            lagged_ref[low:high, :] = lagged[low:high, :].astype(BF16)

    @pl.when(lax.axis_index("sec") == 1)
    def _():
        for low, high in spans(0, fields * half, CHUNK):
            lagged_ref[low:high, :] = get_rows(mine_ref, low, high, width // LANES).astype(BF16)


def shift(values, by):
    return pltpu.roll(values, by % SUB, 0)


def put(ref, start, value):
    for h in range(ref.shape[0]):
        ref[h, start : start + value.shape[0], :] = value[:, h * LANES : (h + 1) * LANES]


def get(ref, start, count):
    return jnp.concatenate([ref[h, start : start + count, :] for h in range(ref.shape[0])], axis=1)


def get_strided(ref, start, steps):
    rows = pl.ds(start, SUB, stride=steps)
    return jnp.concatenate([ref[h, rows, :] for h in range(ref.shape[0])], axis=1)


def put_strided(ref, start, steps, value):
    for h in range(ref.shape[0]):
        ref[h, pl.ds(start, SUB, stride=steps), :] = value[:, h * LANES : (h + 1) * LANES]


def ready_first_kernel(kappa_ref, pack_ref, state_ref, lagged_ref, keep_ref, take_ref, gather_ref, *rest):
    factors, (start_ref, middle, *work) = rest[:6], rest[6:]
    _, half, width = pack_ref.shape
    own = lagged_ref.shape[0]
    base = up(own, TILE)

    @pl.when(lax.axis_index("sec") == 1)
    def _():
        factor(kappa_ref, pack_ref[2 * SOLVED].astype(F32), *factors, *work)
        middle[0:own, :] = get_rows(state_ref, 0, own, width // LANES)
        for f in range(SOLVED):
            middle[base + f * half : base + (f + 1) * half, :] = pack_ref[f].astype(F32)
        own_share(start_ref, middle, lagged_ref, keep_ref, take_ref, gather_ref, half)


def ready_last_kernel(at, kappa_ref, lagged_ref, keep_ref, take_ref, gather_ref, *rest):
    pieces, factors, (start_ref, middle, *work) = rest[:PIECES], rest[PIECES : PIECES + 6], rest[PIECES + 6 :]
    half = kappa_ref.shape[0]
    piece = pieces[0].shape[0]

    @pl.when(lax.axis_index("sec") == 0)
    def _():
        factor(kappa_ref, pieces[at // piece][at % piece : at % piece + half, :], *factors, *work)
        for i in range(PIECES):
            low, high = i * piece, min((i + 1) * piece, middle.shape[0])
            middle[low:high, :] = pieces[i][0 : high - low, :]
        own_share(start_ref, middle, lagged_ref, keep_ref, take_ref, gather_ref, half)


def own_share(start_ref, middle, lagged_ref, keep_ref, take_ref, gather_ref, half):
    width = middle.shape[1]
    solved, own = SOLVED * half, lagged_ref.shape[0]
    values = middle[...]
    high = values.astype(BF16)
    low = (values - high.astype(F32)).astype(BF16)
    share = jnp.dot(
        jnp.concatenate([high, high, low], axis=1), gather_ref[4 * width : 7 * width, :], preferred_element_type=F32
    )
    start_ref[...] = values * keep_ref[...] + take_ref[...] * share
    for low, high in spans(solved // CHUNK * CHUNK, own, CHUNK):
        lag = lagged_ref[low:high, :].astype(F32)
        if low < solved:
            lag = jnp.where(lax.broadcasted_iota(jnp.int32, lag.shape, 0) >= solved - low, lag, 0.0)
        start_ref[low:high, :] += lag


def side_share(rows, gather_ref, side):
    width = rows.shape[1]
    return jnp.dot(
        jnp.concatenate([rows, rows], axis=1),
        gather_ref[2 * side * width : 2 * (side + 1) * width, :],
        preferred_element_type=F32,
    )


def sides_share(near_rows, far_rows, gather_ref):
    width = near_rows.shape[1]
    rows = jnp.concatenate([near_rows, near_rows, far_rows, far_rows], axis=1)
    return jnp.dot(rows, gather_ref[0 : 4 * width, :], preferred_element_type=F32)


def factor(own_ref, other, low_ref, fore_ref, inv_ref, high_ref, back_ref, scan_ref, kappa, ratio, inverse):
    half, width = own_ref.shape
    depth = 2 * half
    steps = low_ref.shape[0]
    level = lax.axis_index("lev")
    ratio[...] = jnp.zeros(ratio.shape, F32)
    inverse[...] = jnp.zeros(inverse.shape, F32)

    @pl.when(level == 0)
    def _():
        kappa[0:half, :] = own_ref[...]
        kappa[half:depth, :] = other

    @pl.when(level == 1)
    def _():
        kappa[0:half, :] = other
        kappa[half:depth, :] = own_ref[...]

    excess = jnp.ones((1, width), F32)
    for k in range(depth):
        here = kappa[k : k + 1, :]
        inv = 1.0 / (excess + here)
        down = here * inv
        put(inverse, k, inv)
        if k < depth - 1:
            put(ratio, SUB + k, down)
        excess = 1.0 + down * excess

    index = lax.broadcasted_iota(jnp.int32, (SUB, width), 0)
    running = None
    for t in range(steps):
        low = get_strided(ratio, SUB - 1 + t, steps)
        low_ref[t] = low
        running = low if running is None else running * low
        fore_ref[t] = running
        inv_ref[t] = get_strided(inverse, t, steps)
    one = jnp.where(index >= 1, running, 0.0)
    two = jnp.where(index >= 2, running * shift(running, 1), 0.0)
    four = jnp.where(index >= 4, two * shift(two, 2), 0.0)
    scan_ref[0], scan_ref[1], scan_ref[2] = one, two, four
    running = None
    for t in range(steps - 1, -1, -1):
        high = get_strided(ratio, SUB + t, steps)
        high_ref[t] = high
        running = high if running is None else running * high
        back_ref[t] = running
    one = jnp.where(index < SUB - 1, running, 0.0)
    two = jnp.where(index < SUB - 2, running * shift(running, -1), 0.0)
    four = jnp.where(index < SUB - 4, two * shift(two, -2), 0.0)
    scan_ref[3], scan_ref[4], scan_ref[5] = one, two, four


def solve(right, factors):
    low_ref, fore_ref, inv_ref, high_ref, back_ref, scan_ref = factors
    steps, _, width = low_ref.shape
    index = lax.broadcasted_iota(jnp.int32, (SUB, width), 0)
    rows = []
    for t in range(steps):
        row = get_strided(right, t, steps)
        if t:
            row = row + low_ref[t] * rows[-1]
        rows.append(row)
    carry = rows[-1]
    for i, by in enumerate((1, 2, 4)):
        carry = carry + scan_ref[i] * shift(carry, by)
    carry = jnp.where(index >= 1, shift(carry, 1), 0.0)
    rows = [(rows[t] + fore_ref[t] * carry) * inv_ref[t] for t in range(steps)]
    for t in range(steps - 2, -1, -1):
        rows[t] = rows[t] + high_ref[t] * rows[t + 1]
    carry = rows[0]
    for i, by in enumerate((1, 2, 4)):
        carry = carry + scan_ref[3 + i] * shift(carry, -by)
    carry = jnp.where(index < SUB - 1, shift(carry, -1), 0.0)
    for t in range(steps):
        put_strided(right, t, steps, rows[t] + back_ref[t] * carry)


def solve_rows(own, other, columns, factors):
    upper = lax.axis_index("lev") == 0
    half, width = own[0].shape
    depth = 2 * half
    for f in range(SOLVED):
        put(columns.at[f], depth, jnp.zeros((columns.shape[2] - depth, width), F32))
        put(columns.at[f], 0, jnp.where(upper, own[f], other[f]))
        put(columns.at[f], half, jnp.where(upper, other[f], own[f]))
    for f in range(SOLVED):
        solve(columns.at[f], factors)
    halves = [(get(columns.at[f], 0, half), get(columns.at[f], half, half)) for f in range(SOLVED)]
    return [jnp.where(upper, a, b) for a, b in halves], [jnp.where(upper, b, a) for a, b in halves]


def near_kernel(core, near_ref, start_ref, take_ref, gather_ref, out_ref):
    rows = slice(0, near_ref.shape[0])

    @pl.when(lax.axis_index("sec") == core)
    def _():
        out_ref[rows, :] = start_ref[rows, :] + take_ref[rows, :] * side_share(near_ref[...], gather_ref, 0)
        if near_ref.shape[0] < out_ref.shape[0]:
            rest = slice(up(near_ref.shape[0], TILE), out_ref.shape[0])
            out_ref[rest, :] = start_ref[rest, :]


def early_kernel(far_ref, start_ref, take_ref, gather_ref, value_ref):
    own = far_ref.shape[0]
    rows = slice(own - value_ref.shape[0], own)

    @pl.when(lax.axis_index("sec") == 1)
    def _():
        value_ref[...] = start_ref[rows, :] + take_ref[rows, :] * side_share(far_ref[rows, :], gather_ref, 1)


def first_kernel(
    dfar_ref, dnear_ref, far_ref, early_ref, pack_ref, start_ref, lagged_ref, take_ref, gather_ref, *rest
):
    factors, (*full_refs, short_ref, smooth, columns) = rest[:6], rest[6:]
    _, half, width = pack_ref.shape
    own = lagged_ref.shape[0]
    total = short_ref.shape[0]
    base = up(own, TILE)
    first = up(SOLVED * half, CHUNK)
    piece = full_refs[0].shape[0]

    def store(low, value):
        for i, (start, stop) in enumerate(spans(0, piece * PIECES, piece)):
            a, b = max(low, start), min(low + value.shape[0], stop)
            if a < b:
                full_refs[i][a - start : b - start, :] = value[a - low : b - low]

    def emit(low, value):
        short_ref[low : low + value.shape[0], :] = value.astype(BF16)
        store(low, value)

    @pl.when(lax.axis_index("sec") == 1)
    def _():
        others = slice(base, base + SOLVED * half)
        smooth[others, :] = start_ref[others, :] + take_ref[others, :] * sides_share(
            dnear_ref[...], dfar_ref[...], gather_ref
        )
        rows = slice(0, first)
        smooth[rows, :] = start_ref[rows, :] + take_ref[rows, :] * side_share(far_ref[rows, :], gather_ref, 1)
        part = lambda low: [smooth[low + f * half : low + (f + 1) * half, :] for f in range(SOLVED)]
        mine, theirs = solve_rows(part(0), part(base), columns, factors)
        for low, high in spans(first, own, CHUNK):
            emit(low, early_ref[low - first : high - first, :])
        for f in range(SOLVED):
            smooth[f * half : (f + 1) * half, :] = mine[f]
            smooth[base + f * half : base + (f + 1) * half, :] = theirs[f] + pack_ref[SOLVED + f].astype(F32)
        for low, high in spans(0, first, CHUNK):
            lag = lagged_ref[low:high, :].astype(F32)
            if high > SOLVED * half:
                lag = jnp.where(lax.broadcasted_iota(jnp.int32, lag.shape, 0) < SOLVED * half - low, lag, 0.0)
            emit(low, smooth[low:high, :] + lag)
        for low, high in spans(base, total, CHUNK):
            emit(low, smooth[low:high, :])
        store(total, pack_ref[2 * SOLVED].astype(F32))


def last_kernel(far_ref, brief_ref, start_ref, lagged_ref, mask_ref, rates_ref, take_ref, gather_ref, *rest):
    factors, (out_ref, smooth, columns, held, sems) = rest[:6], rest[6:]
    own, width = lagged_ref.shape
    fields = rates_ref.shape[0]
    half = own // fields
    base = up(own, TILE)
    total = far_ref.shape[0]
    parts = width // LANES
    first = up(SOLVED * half, CHUNK)

    def send(low, high, sem):
        rows = pl.ds(low * parts, (high - low) * parts)
        return pltpu.make_async_copy(held.at[rows], out_ref.at[rows], sems.at[sem])

    @pl.when(lax.axis_index("sec") == 0)
    def _():
        def smoothed(low, high):
            rows = slice(low, high)
            return start_ref[rows, :] + take_ref[rows, :] * side_share(far_ref[rows, :], gather_ref, 1)

        smooth[0:first, :] = smoothed(0, first)
        smooth[base:total, :] = smoothed(base, total)
        part = lambda low: [smooth[low + f * half : low + (f + 1) * half, :] for f in range(SOLVED)]
        mine, _ = solve_rows(part(0), part(base), columns, factors)
        put_rows(held, first, parts, smoothed(first, own))
        send(first, own, 0).start()
        for f in range(SOLVED):
            smooth[f * half : (f + 1) * half, :] = mine[f]
        for low, high in spans(0, first, CHUNK):
            lag = lagged_ref[low:high, :].astype(F32)
            if high > SOLVED * half:
                lag = jnp.where(lax.broadcasted_iota(jnp.int32, lag.shape, 0) < SOLVED * half - low, lag, 0.0)
            put_rows(held, low, parts, smooth[low:high, :] + lag)

    @pl.when(lax.axis_index("sec") == 1)
    def _():
        for low, high in spans(0, base, CHUNK):
            smooth[low:high, :] = brief_ref[low:high, :].astype(F32)

        def keep(f, value):
            put_rows(held, f * half, parts, value)

        relax = lambda f: rates_ref[f : f + 1, :]
        tendency(lambda f: smooth[f * half : (f + 1) * half, :], fields, mask_ref[1:2, :], relax, keep)
        send(first, own, 0).start()

    send(0, first, 1).start()
    send(first, own, 0).wait()
    send(0, first, 1).wait()


def cost(us):
    return pl.CostEstimate(flops=int(us * 1e9), transcendentals=0, bytes_accessed=0)


def params(mib):
    return pltpu.CompilerParams(vmem_limit_bytes=mib << 20)


def shards(sections, neighbours, edge_weight, field_diff, vert_coef, relax_rate, precip_mask):
    _, fields, half, width = sections.shape
    shape = jax.ShapeDtypeStruct
    steps = up(up(2 * half, SUB) // SUB, 4)
    depth = steps * SUB
    own = fields * half
    total = up(own, TILE) + up(SOLVED * half, TILE)
    piece = up(-(-(total + half) // PIECES), SUB)

    mine = strips(sections)
    shorts = [shape((own, width), BF16), shape((SOLVED * half, width), BF16)]
    short, head = lax.cond(
        lax.axis_index("sec") == 0,
        pl.pallas_call(
            shorten_kernel,
            out_shape=shorts,
            in_specs=[ANY],
            out_specs=[VMEM] * 2,
            scratch_shapes=[pltpu.VMEM(mine.shape, F32), pltpu.SemaphoreType.DMA((2,))],
            compiler_params=params(4),
            cost_estimate=cost(3),
        ),
        lambda _: pl.pallas_call(
            nothing_kernel, out_shape=shorts, out_specs=[VMEM] * 2, compiler_params=params(4), cost_estimate=cost(3)
        )(),
        mine,
    )
    back = (1, 0, same, 0)
    state = route(mine, (0, 1, same, 0), back)
    near_rows = route(short, (0, 1, near, 0), back)
    far_rows = route(short, (0, 1, far, 0), back)
    dnear = route(head, (0, 1, near, 1), back)
    dfar = route(head, (0, 1, far, 1), back)

    pack = pl.pallas_call(
        pack_kernel,
        out_shape=shape((2 * SOLVED + 1, half, width), BF16),
        in_specs=[VMEM] * 3,
        out_specs=VMEM,
        compiler_params=params(4),
        cost_estimate=cost(0.01),
    )(head, state, vert_coef)
    pack = route(pack, (0, 1, same, 1), back)

    gather, lagged, rates, keep, take = pl.pallas_call(
        prepare_kernel,
        out_shape=[
            shape((7 * width, width), BF16),
            shape((own, width), BF16),
            shape((fields, width), F32),
            shape((total, width), F32),
            shape((total, width), F32),
        ],
        in_specs=[VMEM] * 5 + [SMEM] * 2,
        out_specs=[VMEM] * 5,
        scratch_shapes=[pltpu.VMEM((own, width), F32)] * 2,
        compiler_params=params(8),
        cost_estimate=cost(0.01),
    )(mine, short, neighbours, edge_weight, precip_mask, relax_rate, field_diff)

    chunk = shape((steps, SUB, width), F32)

    def ready(kernel, *operands):
        start, *factors = pl.pallas_call(
            kernel,
            out_shape=[chunk] * 5 + [shape((6, SUB, width), F32), shape((total, width), F32)],
            in_specs=[VMEM] * len(operands),
            out_specs=[VMEM] * 7,
            scratch_shapes=[
                pltpu.VMEM((total, width), F32),
                pltpu.VMEM((2 * half, width), F32),
                pltpu.VMEM((width // LANES, depth + 2 * SUB, LANES), F32),
                pltpu.VMEM((width // LANES, depth, LANES), F32),
            ],
            compiler_params=params(16),
            cost_estimate=cost(0),
        )(*operands)[::-1]
        return start, factors[::-1]

    def with_near(core, rows, start):
        return pl.pallas_call(
            functools.partial(near_kernel, core),
            out_shape=shape((total, width), F32),
            in_specs=[VMEM] * 4,
            out_specs=VMEM,
            compiler_params=params(8),
            cost_estimate=cost(0),
        )(rows, start, take, gather)

    start, factors = ready(ready_first_kernel, vert_coef, pack, state, lagged, keep, take, gather)

    start = with_near(1, near_rows, start)

    scratch = [pltpu.VMEM((total, width), F32), pltpu.VMEM((SOLVED, width // LANES, depth, LANES), F32)]
    first = up(SOLVED * half, CHUNK)
    early = pl.pallas_call(
        early_kernel,
        out_shape=shape((own - first, width), F32),
        in_specs=[VMEM] * 4,
        out_specs=VMEM,
        compiler_params=params(8),
        cost_estimate=cost(0),
    )(far_rows, start, take, gather)
    *full, brief = pl.pallas_call(
        first_kernel,
        out_shape=[shape((piece, width), F32)] * PIECES + [shape((total, width), BF16)],
        in_specs=[VMEM] * 15,
        out_specs=[VMEM] * (PIECES + 1),
        scratch_shapes=scratch,
        compiler_params=params(24),
    )(dfar, dnear, far_rows, early, pack, start, lagged, take, gather, *factors)

    near_rows = route(brief, (1, 0, near, 0))
    far_rows = route(brief, (1, 0, far, 0), (0, 1, same, 0))
    pieces = [route(part, back, (0, 1, same, 0)) for part in full]
    start, factors = ready(
        functools.partial(ready_last_kernel, total), vert_coef, lagged, keep, take, gather, *pieces
    )
    start = with_near(0, near_rows, start)
    out = pl.pallas_call(
        last_kernel,
        out_shape=shape(mine.shape, F32),
        in_specs=[VMEM] * 14,
        out_specs=ANY,
        scratch_shapes=scratch + [pltpu.VMEM(mine.shape, F32), pltpu.SemaphoreType.DMA((2,))],
        compiler_params=params(24),
    )(far_rows, brief, start, lagged, precip_mask, rates, take, gather, *factors)
    return out.reshape(sections.shape)


def solution(mesh):
    return jax.shard_map(
        shards,
        mesh=mesh,
        in_specs=(
            P("sec", None, "lev", "dom"),
            P(None, "dom"),
            P(None, "dom"),
            P(),
            P("lev", "dom"),
            P(),
            P(None, "dom"),
        ),
        out_specs=P("sec", None, "lev", "dom"),
        check_vma=False,
    )
```

```python
import functools
import jax
import jax.numpy as jnp
from jax import lax
from jax.experimental import pallas as pl
from jax.experimental.pallas import tpu as pltpu
from jax.sharding import PartitionSpec as P

AXES = ("sec", "dom", "lev")
SOLVED = 2
EDGES = 3
SUB = 8
LANES = 128
TILE = 16
CHUNK = 32
PIECES = 3
VMEM = pl.BlockSpec(memory_space=pltpu.VMEM)
SMEM = pl.BlockSpec(memory_space=pltpu.SMEM)
ANY = pl.BlockSpec(memory_space=pl.ANY)
F32 = jnp.float32
BF16 = jnp.bfloat16


def up(count, unit):
    return -(-count // unit) * unit


def spans(low, high, size):
    return [(r, min(r + size, high)) for r in range(low, high, size)]


def route(array, *moves):
    doms, levs = lax.axis_size("dom"), lax.axis_size("lev")
    place = lambda s, d, v: (s * doms + d) * levs + v
    table = [
        (place(a, d, v), place(b, to_block(d) % doms, v ^ flip))
        for a, b, to_block, flip in moves
        for d in range(doms)
        for v in range(levs)
    ]
    return lax.ppermute(array, AXES, table)


def same(block):
    return block


def near(block):
    return block ^ 1


def far(block):
    return block - 1 if block % 2 == 0 else block + 1


def strips(array):
    return array.reshape(-1, LANES)


def get_rows(ref, low, high, parts):
    return jnp.concatenate([ref[pl.ds(low * parts + h, high - low, stride=parts), :] for h in range(parts)], axis=1)


def put_rows(ref, low, parts, value):
    for h in range(parts):
        ref[pl.ds(low * parts + h, value.shape[0], stride=parts), :] = value[:, h * LANES : (h + 1) * LANES]


def tendency(state, fields, mask, relax, emit):
    rounded = lambda f: state(f).astype(BF16).astype(F32)
    theta, vapour, cloud, rain = rounded(1), rounded(2), rounded(3), rounded(4)
    saturation = 0.6 * jnp.exp(0.25 * theta)
    condense = 0.5 * jnp.tanh(vapour - saturation)
    autoconv = 0.4 * cloud * cloud / (1.0 + cloud * cloud)
    evaporate = 0.3 * rain * rain / (1.0 + rain * rain) * jax.nn.sigmoid(saturation - vapour)
    micro = {
        1: 2.5 * (condense - evaporate),
        2: evaporate - condense,
        3: condense - autoconv,
        4: autoconv - evaporate,
    }
    for f in range(fields):
        clear = -relax(f) * rounded(f)
        if f in micro:
            clear = jnp.where(mask == 1, clear + micro[f], clear)
        emit(f, clear)


def shorten_kernel(mine_ref, short_ref, head_ref, wide, sems):
    own, width = short_ref.shape
    parts = width // LANES
    pieces = spans(0, own, up(-(-own // 2), TILE))
    copies = []
    for i, (low, high) in enumerate(pieces):
        rows = pl.ds(low * parts, (high - low) * parts)
        copies.append(pltpu.make_async_copy(mine_ref.at[rows], wide.at[rows], sems.at[i]))
        copies[-1].start()
    for copy, (start, stop) in zip(copies, pieces):
        copy.wait()
        for low, high in spans(start, stop, CHUNK):
            value = get_rows(wide, low, high, parts).astype(BF16)
            short_ref[low:high, :] = value
            end = min(high, head_ref.shape[0])
            if low < end:
                head_ref[low:end, :] = value[: end - low]


def nothing_kernel(short_ref, head_ref):
    head_ref[...] = jnp.zeros(head_ref.shape, BF16)


def pack_kernel(head_ref, other_ref, kappa_ref, pack_ref):
    _, half, width = pack_ref.shape
    parts = width // LANES

    @pl.when(lax.axis_index("sec") == 0)
    def _():
        head = head_ref[...].astype(F32)
        for f in range(SOLVED):
            pack_ref[f] = head[f * half : (f + 1) * half].astype(BF16)
            pack_ref[SOLVED + f] = get_rows(other_ref, f * half, (f + 1) * half, parts).astype(BF16)

    pack_ref[2 * SOLVED] = kappa_ref[...].astype(BF16)


def prepare_kernel(
    mine_ref, short_ref, nbr_ref, weight_ref, mask_ref, relax_ref, diff_ref, gather_ref, lagged_ref, rates_ref, keep_ref, take_ref, work,
    lagged,
):
    fields = rates_ref.shape[0]
    width = nbr_ref.shape[1]
    half = lagged_ref.shape[0] // fields
    base = up(fields * half, TILE)
    odd = lax.axis_index("dom") % 2
    sides = (2 * width * (1 - odd), 2 * width * odd, width)
    for side, start in enumerate(sides):
        for low, high in spans(0, width, 64):
            place = lax.broadcasted_iota(jnp.int32, (high - low, width), 0) + (low + start)
            total = jnp.zeros((high - low, width), F32)
            for edge in range(EDGES):
                total = total + jnp.where(place == nbr_ref[edge : edge + 1, :], weight_ref[edge : edge + 1, :], 0.0)
            first = total.astype(BF16)
            at = 2 * side * width + low
            gather_ref[at : at + high - low, :] = first
            gather_ref[at + width : at + width + high - low, :] = (total - first.astype(F32)).astype(BF16)
            if side == 2:
                gather_ref[at + 2 * width : at + 2 * width + high - low, :] = first
    total = weight_ref[0:1, :] + weight_ref[1:2, :] + weight_ref[2:3, :]
    keep_ref[...] = jnp.zeros(keep_ref.shape, F32)
    take_ref[...] = jnp.zeros(take_ref.shape, F32)
    for f in range(fields):
        rates_ref[f : f + 1, :] = jnp.full((1, width), relax_ref[f], F32)
    for f in range(fields + SOLVED):
        low = f * half if f < fields else base + (f - fields) * half
        scale = diff_ref[f % fields]
        keep_ref[low : low + half, :] = jnp.broadcast_to(1.0 - scale * total, (half, width))
        take_ref[low : low + half, :] = jnp.full((half, width), scale, F32)

    @pl.when(lax.axis_index("sec") == 0)
    def _():
        def emit(f, value):
            lagged[f * half : (f + 1) * half, :] = value

        for low, high in spans(0, fields * half, CHUNK):
            work[low:high, :] = short_ref[low:high, :].astype(F32)
        tendency(
            lambda f: work[f * half : (f + 1) * half, :], fields, mask_ref[0:1, :], lambda f: relax_ref[f], emit
        )
        for low, high in spans(0, fields * half, CHUNK):
            lagged_ref[low:high, :] = lagged[low:high, :].astype(BF16)

    @pl.when(lax.axis_index("sec") == 1)
    def _():
        for low, high in spans(0, fields * half, CHUNK):
            lagged_ref[low:high, :] = get_rows(mine_ref, low, high, width // LANES).astype(BF16)


def shift(values, by):
    return pltpu.roll(values, by % SUB, 0)


def put(ref, start, value):
    for h in range(ref.shape[0]):
        ref[h, start : start + value.shape[0], :] = value[:, h * LANES : (h + 1) * LANES]


def get(ref, start, count):
    return jnp.concatenate([ref[h, start : start + count, :] for h in range(ref.shape[0])], axis=1)


def get_strided(ref, start, steps):
    rows = pl.ds(start, SUB, stride=steps)
    return jnp.concatenate([ref[h, rows, :] for h in range(ref.shape[0])], axis=1)


def put_strided(ref, start, steps, value):
    for h in range(ref.shape[0]):
        ref[h, pl.ds(start, SUB, stride=steps), :] = value[:, h * LANES : (h + 1) * LANES]


def ready_first_kernel(kappa_ref, pack_ref, state_ref, lagged_ref, keep_ref, take_ref, gather_ref, *rest):
    factors, (start_ref, middle, *work) = rest[:6], rest[6:]
    _, half, width = pack_ref.shape
    own = lagged_ref.shape[0]
    base = up(own, TILE)

    @pl.when(lax.axis_index("sec") == 1)
    def _():
        factor(kappa_ref, pack_ref[2 * SOLVED].astype(F32), *factors, *work)
        middle[0:own, :] = get_rows(state_ref, 0, own, width // LANES)
        for f in range(SOLVED):
            middle[base + f * half : base + (f + 1) * half, :] = pack_ref[f].astype(F32)
        own_share(start_ref, middle, lagged_ref, keep_ref, take_ref, gather_ref, half)


def ready_last_kernel(at, kappa_ref, lagged_ref, keep_ref, take_ref, gather_ref, *rest):
    pieces, factors, (start_ref, middle, *work) = rest[:PIECES], rest[PIECES : PIECES + 6], rest[PIECES + 6 :]
    half = kappa_ref.shape[0]
    piece = pieces[0].shape[0]

    @pl.when(lax.axis_index("sec") == 0)
    def _():
        factor(kappa_ref, pieces[at // piece][at % piece : at % piece + half, :], *factors, *work)
        for i in range(PIECES):
            low, high = i * piece, min((i + 1) * piece, middle.shape[0])
            middle[low:high, :] = pieces[i][0 : high - low, :]
        own_share(start_ref, middle, lagged_ref, keep_ref, take_ref, gather_ref, half)


def own_share(start_ref, middle, lagged_ref, keep_ref, take_ref, gather_ref, half):
    width = middle.shape[1]
    solved, own = SOLVED * half, lagged_ref.shape[0]
    values = middle[...]
    high = values.astype(BF16)
    low = (values - high.astype(F32)).astype(BF16)
    share = jnp.dot(
        jnp.concatenate([high, high, low], axis=1), gather_ref[4 * width : 7 * width, :], preferred_element_type=F32
    )
    start_ref[...] = values * keep_ref[...] + take_ref[...] * share
    for low, high in spans(solved // CHUNK * CHUNK, own, CHUNK):
        lag = lagged_ref[low:high, :].astype(F32)
        if low < solved:
            lag = jnp.where(lax.broadcasted_iota(jnp.int32, lag.shape, 0) >= solved - low, lag, 0.0)
        start_ref[low:high, :] += lag


def side_share(rows, gather_ref, side):
    width = rows.shape[1]
    return jnp.dot(
        jnp.concatenate([rows, rows], axis=1),
        gather_ref[2 * side * width : 2 * (side + 1) * width, :],
        preferred_element_type=F32,
    )


def sides_share(near_rows, far_rows, gather_ref):
    width = near_rows.shape[1]
    rows = jnp.concatenate([near_rows, near_rows, far_rows, far_rows], axis=1)
    return jnp.dot(rows, gather_ref[0 : 4 * width, :], preferred_element_type=F32)


def factor(own_ref, other, low_ref, fore_ref, inv_ref, high_ref, back_ref, scan_ref, kappa, ratio, inverse):
    half, width = own_ref.shape
    depth = 2 * half
    steps = low_ref.shape[0]
    level = lax.axis_index("lev")
    ratio[...] = jnp.zeros(ratio.shape, F32)
    inverse[...] = jnp.zeros(inverse.shape, F32)

    @pl.when(level == 0)
    def _():
        kappa[0:half, :] = own_ref[...]
        kappa[half:depth, :] = other

    @pl.when(level == 1)
    def _():
        kappa[0:half, :] = other
        kappa[half:depth, :] = own_ref[...]

    excess = jnp.ones((1, width), F32)
    for k in range(depth):
        here = kappa[k : k + 1, :]
        inv = 1.0 / (excess + here)
        down = here * inv
        put(inverse, k, inv)
        if k < depth - 1:
            put(ratio, SUB + k, down)
        excess = 1.0 + down * excess

    index = lax.broadcasted_iota(jnp.int32, (SUB, width), 0)
    running = None
    for t in range(steps):
        low = get_strided(ratio, SUB - 1 + t, steps)
        low_ref[t] = low
        running = low if running is None else running * low
        fore_ref[t] = running
        inv_ref[t] = get_strided(inverse, t, steps)
    one = jnp.where(index >= 1, running, 0.0)
    two = jnp.where(index >= 2, running * shift(running, 1), 0.0)
    four = jnp.where(index >= 4, two * shift(two, 2), 0.0)
    scan_ref[0], scan_ref[1], scan_ref[2] = one, two, four
    running = None
    for t in range(steps - 1, -1, -1):
        high = get_strided(ratio, SUB + t, steps)
        high_ref[t] = high
        running = high if running is None else running * high
        back_ref[t] = running
    one = jnp.where(index < SUB - 1, running, 0.0)
    two = jnp.where(index < SUB - 2, running * shift(running, -1), 0.0)
    four = jnp.where(index < SUB - 4, two * shift(two, -2), 0.0)
    scan_ref[3], scan_ref[4], scan_ref[5] = one, two, four


def solve(right, factors):
    low_ref, fore_ref, inv_ref, high_ref, back_ref, scan_ref = factors
    steps, _, width = low_ref.shape
    index = lax.broadcasted_iota(jnp.int32, (SUB, width), 0)
    rows = []
    for t in range(steps):
        row = get_strided(right, t, steps)
        if t:
            row = row + low_ref[t] * rows[-1]
        rows.append(row)
    carry = rows[-1]
    for i, by in enumerate((1, 2, 4)):
        carry = carry + scan_ref[i] * shift(carry, by)
    carry = jnp.where(index >= 1, shift(carry, 1), 0.0)
    rows = [(rows[t] + fore_ref[t] * carry) * inv_ref[t] for t in range(steps)]
    for t in range(steps - 2, -1, -1):
        rows[t] = rows[t] + high_ref[t] * rows[t + 1]
    carry = rows[0]
    for i, by in enumerate((1, 2, 4)):
        carry = carry + scan_ref[3 + i] * shift(carry, -by)
    carry = jnp.where(index < SUB - 1, shift(carry, -1), 0.0)
    for t in range(steps):
        put_strided(right, t, steps, rows[t] + back_ref[t] * carry)


def solve_rows(own, other, columns, factors):
    upper = lax.axis_index("lev") == 0
    half, width = own[0].shape
    depth = 2 * half
    for f in range(SOLVED):
        put(columns.at[f], depth, jnp.zeros((columns.shape[2] - depth, width), F32))
        put(columns.at[f], 0, jnp.where(upper, own[f], other[f]))
        put(columns.at[f], half, jnp.where(upper, other[f], own[f]))
    for f in range(SOLVED):
        solve(columns.at[f], factors)
    halves = [(get(columns.at[f], 0, half), get(columns.at[f], half, half)) for f in range(SOLVED)]
    return [jnp.where(upper, a, b) for a, b in halves], [jnp.where(upper, b, a) for a, b in halves]


def near_kernel(core, near_ref, start_ref, take_ref, gather_ref, out_ref):
    rows = slice(0, near_ref.shape[0])

    @pl.when(lax.axis_index("sec") == core)
    def _():
        out_ref[rows, :] = start_ref[rows, :] + take_ref[rows, :] * side_share(near_ref[...], gather_ref, 0)
        if near_ref.shape[0] < out_ref.shape[0]:
            rest = slice(up(near_ref.shape[0], TILE), out_ref.shape[0])
            out_ref[rest, :] = start_ref[rest, :]


def early_kernel(far_ref, start_ref, take_ref, gather_ref, value_ref):
    rows = slice(0, far_ref.shape[0])

    @pl.when(lax.axis_index("sec") == 1)
    def _():
        value_ref[...] = start_ref[rows, :] + take_ref[rows, :] * side_share(far_ref[...], gather_ref, 1)


def first_kernel(
    dfar_ref, dnear_ref, early_ref, pack_ref, start_ref, lagged_ref, take_ref, gather_ref, *rest
):
    factors, (*full_refs, short_ref, smooth, columns) = rest[:6], rest[6:]
    _, half, width = pack_ref.shape
    own = lagged_ref.shape[0]
    total = short_ref.shape[0]
    base = up(own, TILE)
    first = up(SOLVED * half, CHUNK)
    piece = full_refs[0].shape[0]

    def store(low, value):
        for i, (start, stop) in enumerate(spans(0, piece * PIECES, piece)):
            a, b = max(low, start), min(low + value.shape[0], stop)
            if a < b:
                full_refs[i][a - start : b - start, :] = value[a - low : b - low]

    def emit(low, value):
        short_ref[low : low + value.shape[0], :] = value.astype(BF16)
        store(low, value)

    @pl.when(lax.axis_index("sec") == 1)
    def _():
        others = slice(base, base + SOLVED * half)
        smooth[others, :] = start_ref[others, :] + take_ref[others, :] * sides_share(
            dnear_ref[...], dfar_ref[...], gather_ref
        )
        smooth[0:first, :] = early_ref[0:first, :]
        part = lambda low: [smooth[low + f * half : low + (f + 1) * half, :] for f in range(SOLVED)]
        mine, theirs = solve_rows(part(0), part(base), columns, factors)
        for low, high in spans(first, own, CHUNK):
            emit(low, early_ref[low:high, :])
        for f in range(SOLVED):
            smooth[f * half : (f + 1) * half, :] = mine[f]
            smooth[base + f * half : base + (f + 1) * half, :] = theirs[f] + pack_ref[SOLVED + f].astype(F32)
        for low, high in spans(0, first, CHUNK):
            lag = lagged_ref[low:high, :].astype(F32)
            if high > SOLVED * half:
                lag = jnp.where(lax.broadcasted_iota(jnp.int32, lag.shape, 0) < SOLVED * half - low, lag, 0.0)
            emit(low, smooth[low:high, :] + lag)
        for low, high in spans(base, total, CHUNK):
            emit(low, smooth[low:high, :])
        store(total, pack_ref[2 * SOLVED].astype(F32))


def last_kernel(far_ref, brief_ref, start_ref, lagged_ref, mask_ref, rates_ref, take_ref, gather_ref, *rest):
    factors, (out_ref, smooth, columns, held, sems) = rest[:6], rest[6:]
    own, width = lagged_ref.shape
    fields = rates_ref.shape[0]
    half = own // fields
    base = up(own, TILE)
    total = far_ref.shape[0]
    parts = width // LANES
    first = up(SOLVED * half, CHUNK)

    def send(low, high, sem):
        rows = pl.ds(low * parts, (high - low) * parts)
        return pltpu.make_async_copy(held.at[rows], out_ref.at[rows], sems.at[sem])

    @pl.when(lax.axis_index("sec") == 0)
    def _():
        def smoothed(low, high):
            rows = slice(low, high)
            return start_ref[rows, :] + take_ref[rows, :] * side_share(far_ref[rows, :], gather_ref, 1)

        smooth[0:first, :] = smoothed(0, first)
        smooth[base:total, :] = smoothed(base, total)
        part = lambda low: [smooth[low + f * half : low + (f + 1) * half, :] for f in range(SOLVED)]
        mine, _ = solve_rows(part(0), part(base), columns, factors)
        put_rows(held, first, parts, smoothed(first, own))
        send(first, own, 0).start()
        for f in range(SOLVED):
            smooth[f * half : (f + 1) * half, :] = mine[f]
        for low, high in spans(0, first, CHUNK):
            lag = lagged_ref[low:high, :].astype(F32)
            if high > SOLVED * half:
                lag = jnp.where(lax.broadcasted_iota(jnp.int32, lag.shape, 0) < SOLVED * half - low, lag, 0.0)
            put_rows(held, low, parts, smooth[low:high, :] + lag)

    @pl.when(lax.axis_index("sec") == 1)
    def _():
        for low, high in spans(0, base, CHUNK):
            smooth[low:high, :] = brief_ref[low:high, :].astype(F32)

        def keep(f, value):
            put_rows(held, f * half, parts, value)

        relax = lambda f: rates_ref[f : f + 1, :]
        tendency(lambda f: smooth[f * half : (f + 1) * half, :], fields, mask_ref[1:2, :], relax, keep)
        send(first, own, 0).start()

    send(0, first, 1).start()
    send(first, own, 0).wait()
    send(0, first, 1).wait()


def cost(us):
    return pl.CostEstimate(flops=int(us * 1e9), transcendentals=0, bytes_accessed=0)


def params(mib):
    return pltpu.CompilerParams(vmem_limit_bytes=mib << 20)


def shards(sections, neighbours, edge_weight, field_diff, vert_coef, relax_rate, precip_mask):
    _, fields, half, width = sections.shape
    shape = jax.ShapeDtypeStruct
    steps = up(up(2 * half, SUB) // SUB, 4)
    depth = steps * SUB
    own = fields * half
    total = up(own, TILE) + up(SOLVED * half, TILE)
    piece = up(-(-(total + half) // PIECES), SUB)

    mine = strips(sections)
    shorts = [shape((own, width), BF16), shape((SOLVED * half, width), BF16)]
    short, head = lax.cond(
        lax.axis_index("sec") == 0,
        pl.pallas_call(
            shorten_kernel,
            out_shape=shorts,
            in_specs=[ANY],
            out_specs=[VMEM] * 2,
            scratch_shapes=[pltpu.VMEM(mine.shape, F32), pltpu.SemaphoreType.DMA((2,))],
            compiler_params=params(4),
            cost_estimate=cost(3),
        ),
        lambda _: pl.pallas_call(
            nothing_kernel, out_shape=shorts, out_specs=[VMEM] * 2, compiler_params=params(4), cost_estimate=cost(3)
        )(),
        mine,
    )
    back = (1, 0, same, 0)
    state = route(mine, (0, 1, same, 0), back)
    near_rows = route(short, (0, 1, near, 0), back)
    far_rows = route(short, (0, 1, far, 0), back)
    dnear = route(head, (0, 1, near, 1), back)
    dfar = route(head, (0, 1, far, 1), back)

    pack = pl.pallas_call(
        pack_kernel,
        out_shape=shape((2 * SOLVED + 1, half, width), BF16),
        in_specs=[VMEM] * 3,
        out_specs=VMEM,
        compiler_params=params(4),
        cost_estimate=cost(0.01),
    )(head, state, vert_coef)
    pack = route(pack, (0, 1, same, 1), back)

    gather, lagged, rates, keep, take = pl.pallas_call(
        prepare_kernel,
        out_shape=[
            shape((7 * width, width), BF16),
            shape((own, width), BF16),
            shape((fields, width), F32),
            shape((total, width), F32),
            shape((total, width), F32),
        ],
        in_specs=[VMEM] * 5 + [SMEM] * 2,
        out_specs=[VMEM] * 5,
        scratch_shapes=[pltpu.VMEM((own, width), F32)] * 2,
        compiler_params=params(8),
        cost_estimate=cost(0.01),
    )(mine, short, neighbours, edge_weight, precip_mask, relax_rate, field_diff)

    chunk = shape((steps, SUB, width), F32)

    def ready(kernel, *operands):
        start, *factors = pl.pallas_call(
            kernel,
            out_shape=[chunk] * 5 + [shape((6, SUB, width), F32), shape((total, width), F32)],
            in_specs=[VMEM] * len(operands),
            out_specs=[VMEM] * 7,
            scratch_shapes=[
                pltpu.VMEM((total, width), F32),
                pltpu.VMEM((2 * half, width), F32),
                pltpu.VMEM((width // LANES, depth + 2 * SUB, LANES), F32),
                pltpu.VMEM((width // LANES, depth, LANES), F32),
            ],
            compiler_params=params(16),
            cost_estimate=cost(0),
        )(*operands)[::-1]
        return start, factors[::-1]

    def with_near(core, rows, start):
        return pl.pallas_call(
            functools.partial(near_kernel, core),
            out_shape=shape((total, width), F32),
            in_specs=[VMEM] * 4,
            out_specs=VMEM,
            compiler_params=params(8),
            cost_estimate=cost(0),
        )(rows, start, take, gather)

    start, factors = ready(ready_first_kernel, vert_coef, pack, state, lagged, keep, take, gather)

    start = with_near(1, near_rows, start)

    scratch = [pltpu.VMEM((total, width), F32), pltpu.VMEM((SOLVED, width // LANES, depth, LANES), F32)]
    early = pl.pallas_call(
        early_kernel,
        out_shape=shape((own, width), F32),
        in_specs=[VMEM] * 4,
        out_specs=VMEM,
        compiler_params=params(8),
        cost_estimate=cost(0),
    )(far_rows, start, take, gather)
    *full, brief = pl.pallas_call(
        first_kernel,
        out_shape=[shape((piece, width), F32)] * PIECES + [shape((total, width), BF16)],
        in_specs=[VMEM] * 14,
        out_specs=[VMEM] * (PIECES + 1),
        scratch_shapes=scratch,
        compiler_params=params(24),
    )(dfar, dnear, early, pack, start, lagged, take, gather, *factors)

    near_rows = route(brief, (1, 0, near, 0))
    far_rows = route(brief, (1, 0, far, 0), (0, 1, same, 0))
    pieces = [route(part, back, (0, 1, same, 0)) for part in full]
    start, factors = ready(
        functools.partial(ready_last_kernel, total), vert_coef, lagged, keep, take, gather, *pieces
    )
    start = with_near(0, near_rows, start)
    out = pl.pallas_call(
        last_kernel,
        out_shape=shape(mine.shape, F32),
        in_specs=[VMEM] * 14,
        out_specs=ANY,
        scratch_shapes=scratch + [pltpu.VMEM(mine.shape, F32), pltpu.SemaphoreType.DMA((2,))],
        compiler_params=params(24),
    )(far_rows, brief, start, lagged, precip_mask, rates, take, gather, *factors)
    return out.reshape(sections.shape)


def solution(mesh):
    return jax.shard_map(
        shards,
        mesh=mesh,
        in_specs=(
            P("sec", None, "lev", "dom"),
            P(None, "dom"),
            P(None, "dom"),
            P(),
            P("lev", "dom"),
            P(),
            P(None, "dom"),
        ),
        out_specs=P("sec", None, "lev", "dom"),
        check_vma=False,
    )
```

```python
import functools
import jax
import jax.numpy as jnp
from jax import lax
from jax.experimental import pallas as pl
from jax.experimental.pallas import tpu as pltpu
from jax.sharding import PartitionSpec as P

AXES = ("sec", "dom", "lev")
SOLVED = 2
EDGES = 3
SUB = 8
LANES = 128
TILE = 16
CHUNK = 32
PIECES = 3
VMEM = pl.BlockSpec(memory_space=pltpu.VMEM)
SMEM = pl.BlockSpec(memory_space=pltpu.SMEM)
ANY = pl.BlockSpec(memory_space=pl.ANY)
F32 = jnp.float32
BF16 = jnp.bfloat16


def up(count, unit):
    return -(-count // unit) * unit


def spans(low, high, size):
    return [(r, min(r + size, high)) for r in range(low, high, size)]


def route(array, *moves):
    doms, levs = lax.axis_size("dom"), lax.axis_size("lev")
    place = lambda s, d, v: (s * doms + d) * levs + v
    table = [
        (place(a, d, v), place(b, to_block(d) % doms, v ^ flip))
        for a, b, to_block, flip in moves
        for d in range(doms)
        for v in range(levs)
    ]
    return lax.ppermute(array, AXES, table)


def same(block):
    return block


def near(block):
    return block ^ 1


def far(block):
    return block - 1 if block % 2 == 0 else block + 1


def strips(array):
    return array.reshape(-1, LANES)


def get_rows(ref, low, high, parts):
    return jnp.concatenate([ref[pl.ds(low * parts + h, high - low, stride=parts), :] for h in range(parts)], axis=1)


def put_rows(ref, low, parts, value):
    for h in range(parts):
        ref[pl.ds(low * parts + h, value.shape[0], stride=parts), :] = value[:, h * LANES : (h + 1) * LANES]


def tendency(state, fields, mask, relax, emit):
    rounded = lambda f: state(f).astype(BF16).astype(F32)
    theta, vapour, cloud, rain = rounded(1), rounded(2), rounded(3), rounded(4)
    saturation = 0.6 * jnp.exp(0.25 * theta)
    condense = 0.5 * jnp.tanh(vapour - saturation)
    autoconv = 0.4 * cloud * cloud / (1.0 + cloud * cloud)
    evaporate = 0.3 * rain * rain / (1.0 + rain * rain) * jax.nn.sigmoid(saturation - vapour)
    micro = {
        1: 2.5 * (condense - evaporate),
        2: evaporate - condense,
        3: condense - autoconv,
        4: autoconv - evaporate,
    }
    for f in range(fields):
        clear = -relax(f) * rounded(f)
        if f in micro:
            clear = jnp.where(mask == 1, clear + micro[f], clear)
        emit(f, clear)


def shorten_kernel(mine_ref, short_ref, head_ref, wide, sems):
    own, width = short_ref.shape
    parts = width // LANES
    pieces = spans(0, own, up(own, TILE))
    copies = []
    for i, (low, high) in enumerate(pieces):
        rows = pl.ds(low * parts, (high - low) * parts)
        copies.append(pltpu.make_async_copy(mine_ref.at[rows], wide.at[rows], sems.at[i]))
        copies[-1].start()
    for copy, (start, stop) in zip(copies, pieces):
        copy.wait()
        for low, high in spans(start, stop, CHUNK):
            value = get_rows(wide, low, high, parts).astype(BF16)
            short_ref[low:high, :] = value
            end = min(high, head_ref.shape[0])
            if low < end:
                head_ref[low:end, :] = value[: end - low]


def nothing_kernel(short_ref, head_ref):
    head_ref[...] = jnp.zeros(head_ref.shape, BF16)


def pack_kernel(head_ref, other_ref, kappa_ref, pack_ref):
    _, half, width = pack_ref.shape
    parts = width // LANES

    @pl.when(lax.axis_index("sec") == 0)
    def _():
        head = head_ref[...].astype(F32)
        for f in range(SOLVED):
            pack_ref[f] = head[f * half : (f + 1) * half].astype(BF16)
            pack_ref[SOLVED + f] = get_rows(other_ref, f * half, (f + 1) * half, parts).astype(BF16)

    pack_ref[2 * SOLVED] = kappa_ref[...].astype(BF16)


def prepare_kernel(
    mine_ref, short_ref, nbr_ref, weight_ref, mask_ref, relax_ref, diff_ref, gather_ref, lagged_ref, rates_ref, keep_ref, take_ref, work,
    lagged,
):
    fields = rates_ref.shape[0]
    width = nbr_ref.shape[1]
    half = lagged_ref.shape[0] // fields
    base = up(fields * half, TILE)
    odd = lax.axis_index("dom") % 2
    sides = (2 * width * (1 - odd), 2 * width * odd, width)
    for side, start in enumerate(sides):
        for low, high in spans(0, width, 64):
            place = lax.broadcasted_iota(jnp.int32, (high - low, width), 0) + (low + start)
            total = jnp.zeros((high - low, width), F32)
            for edge in range(EDGES):
                total = total + jnp.where(place == nbr_ref[edge : edge + 1, :], weight_ref[edge : edge + 1, :], 0.0)
            first = total.astype(BF16)
            at = 2 * side * width + low
            gather_ref[at : at + high - low, :] = first
            gather_ref[at + width : at + width + high - low, :] = (total - first.astype(F32)).astype(BF16)
            if side == 2:
                gather_ref[at + 2 * width : at + 2 * width + high - low, :] = first
    total = weight_ref[0:1, :] + weight_ref[1:2, :] + weight_ref[2:3, :]
    keep_ref[...] = jnp.zeros(keep_ref.shape, F32)
    take_ref[...] = jnp.zeros(take_ref.shape, F32)
    for f in range(fields):
        rates_ref[f : f + 1, :] = jnp.full((1, width), relax_ref[f], F32)
    for f in range(fields + SOLVED):
        low = f * half if f < fields else base + (f - fields) * half
        scale = diff_ref[f % fields]
        keep_ref[low : low + half, :] = jnp.broadcast_to(1.0 - scale * total, (half, width))
        take_ref[low : low + half, :] = jnp.full((half, width), scale, F32)

    @pl.when(lax.axis_index("sec") == 0)
    def _():
        def emit(f, value):
            lagged[f * half : (f + 1) * half, :] = value

        for low, high in spans(0, fields * half, CHUNK):
            work[low:high, :] = short_ref[low:high, :].astype(F32)
        tendency(
            lambda f: work[f * half : (f + 1) * half, :], fields, mask_ref[0:1, :], lambda f: relax_ref[f], emit
        )
        for low, high in spans(0, fields * half, CHUNK):
            lagged_ref[low:high, :] = lagged[low:high, :].astype(BF16)

    @pl.when(lax.axis_index("sec") == 1)
    def _():
        for low, high in spans(0, fields * half, CHUNK):
            lagged_ref[low:high, :] = get_rows(mine_ref, low, high, width // LANES).astype(BF16)


def shift(values, by):
    return pltpu.roll(values, by % SUB, 0)


def put(ref, start, value):
    for h in range(ref.shape[0]):
        ref[h, start : start + value.shape[0], :] = value[:, h * LANES : (h + 1) * LANES]


def get(ref, start, count):
    return jnp.concatenate([ref[h, start : start + count, :] for h in range(ref.shape[0])], axis=1)


def get_strided(ref, start, steps):
    rows = pl.ds(start, SUB, stride=steps)
    return jnp.concatenate([ref[h, rows, :] for h in range(ref.shape[0])], axis=1)


def put_strided(ref, start, steps, value):
    for h in range(ref.shape[0]):
        ref[h, pl.ds(start, SUB, stride=steps), :] = value[:, h * LANES : (h + 1) * LANES]


def ready_first_kernel(kappa_ref, pack_ref, state_ref, lagged_ref, keep_ref, take_ref, gather_ref, *rest):
    factors, (start_ref, middle, *work) = rest[:6], rest[6:]
    _, half, width = pack_ref.shape
    own = lagged_ref.shape[0]
    base = up(own, TILE)

    @pl.when(lax.axis_index("sec") == 1)
    def _():
        factor(kappa_ref, pack_ref[2 * SOLVED].astype(F32), *factors, *work)
        middle[0:own, :] = get_rows(state_ref, 0, own, width // LANES)
        for f in range(SOLVED):
            middle[base + f * half : base + (f + 1) * half, :] = pack_ref[f].astype(F32)
        own_share(start_ref, middle, lagged_ref, keep_ref, take_ref, gather_ref, half)


def ready_last_kernel(at, kappa_ref, lagged_ref, keep_ref, take_ref, gather_ref, *rest):
    pieces, factors, (start_ref, middle, *work) = rest[:PIECES], rest[PIECES : PIECES + 6], rest[PIECES + 6 :]
    half = kappa_ref.shape[0]
    piece = pieces[0].shape[0]

    @pl.when(lax.axis_index("sec") == 0)
    def _():
        factor(kappa_ref, pieces[at // piece][at % piece : at % piece + half, :], *factors, *work)
        for i in range(PIECES):
            low, high = i * piece, min((i + 1) * piece, middle.shape[0])
            middle[low:high, :] = pieces[i][0 : high - low, :]
        own_share(start_ref, middle, lagged_ref, keep_ref, take_ref, gather_ref, half)


def own_share(start_ref, middle, lagged_ref, keep_ref, take_ref, gather_ref, half):
    width = middle.shape[1]
    solved, own = SOLVED * half, lagged_ref.shape[0]
    values = middle[...]
    high = values.astype(BF16)
    low = (values - high.astype(F32)).astype(BF16)
    share = jnp.dot(
        jnp.concatenate([high, high, low], axis=1), gather_ref[4 * width : 7 * width, :], preferred_element_type=F32
    )
    start_ref[...] = values * keep_ref[...] + take_ref[...] * share
    for low, high in spans(solved // CHUNK * CHUNK, own, CHUNK):
        lag = lagged_ref[low:high, :].astype(F32)
        if low < solved:
            lag = jnp.where(lax.broadcasted_iota(jnp.int32, lag.shape, 0) >= solved - low, lag, 0.0)
        start_ref[low:high, :] += lag


def side_share(rows, gather_ref, side):
    width = rows.shape[1]
    return jnp.dot(
        jnp.concatenate([rows, rows], axis=1),
        gather_ref[2 * side * width : 2 * (side + 1) * width, :],
        preferred_element_type=F32,
    )


def sides_share(near_rows, far_rows, gather_ref):
    width = near_rows.shape[1]
    rows = jnp.concatenate([near_rows, near_rows, far_rows, far_rows], axis=1)
    return jnp.dot(rows, gather_ref[0 : 4 * width, :], preferred_element_type=F32)


def factor(own_ref, other, low_ref, fore_ref, inv_ref, high_ref, back_ref, scan_ref, kappa, ratio, inverse):
    half, width = own_ref.shape
    depth = 2 * half
    steps = low_ref.shape[0]
    level = lax.axis_index("lev")
    ratio[...] = jnp.zeros(ratio.shape, F32)
    inverse[...] = jnp.zeros(inverse.shape, F32)

    @pl.when(level == 0)
    def _():
        kappa[0:half, :] = own_ref[...]
        kappa[half:depth, :] = other

    @pl.when(level == 1)
    def _():
        kappa[0:half, :] = other
        kappa[half:depth, :] = own_ref[...]

    excess = jnp.ones((1, width), F32)
    for k in range(depth):
        here = kappa[k : k + 1, :]
        inv = 1.0 / (excess + here)
        down = here * inv
        put(inverse, k, inv)
        if k < depth - 1:
            put(ratio, SUB + k, down)
        excess = 1.0 + down * excess

    index = lax.broadcasted_iota(jnp.int32, (SUB, width), 0)
    running = None
    for t in range(steps):
        low = get_strided(ratio, SUB - 1 + t, steps)
        low_ref[t] = low
        running = low if running is None else running * low
        fore_ref[t] = running
        inv_ref[t] = get_strided(inverse, t, steps)
    one = jnp.where(index >= 1, running, 0.0)
    two = jnp.where(index >= 2, running * shift(running, 1), 0.0)
    four = jnp.where(index >= 4, two * shift(two, 2), 0.0)
    scan_ref[0], scan_ref[1], scan_ref[2] = one, two, four
    running = None
    for t in range(steps - 1, -1, -1):
        high = get_strided(ratio, SUB + t, steps)
        high_ref[t] = high
        running = high if running is None else running * high
        back_ref[t] = running
    one = jnp.where(index < SUB - 1, running, 0.0)
    two = jnp.where(index < SUB - 2, running * shift(running, -1), 0.0)
    four = jnp.where(index < SUB - 4, two * shift(two, -2), 0.0)
    scan_ref[3], scan_ref[4], scan_ref[5] = one, two, four


def solve(right, factors):
    low_ref, fore_ref, inv_ref, high_ref, back_ref, scan_ref = factors
    steps, _, width = low_ref.shape
    index = lax.broadcasted_iota(jnp.int32, (SUB, width), 0)
    rows = []
    for t in range(steps):
        row = get_strided(right, t, steps)
        if t:
            row = row + low_ref[t] * rows[-1]
        rows.append(row)
    carry = rows[-1]
    for i, by in enumerate((1, 2, 4)):
        carry = carry + scan_ref[i] * shift(carry, by)
    carry = jnp.where(index >= 1, shift(carry, 1), 0.0)
    rows = [(rows[t] + fore_ref[t] * carry) * inv_ref[t] for t in range(steps)]
    for t in range(steps - 2, -1, -1):
        rows[t] = rows[t] + high_ref[t] * rows[t + 1]
    carry = rows[0]
    for i, by in enumerate((1, 2, 4)):
        carry = carry + scan_ref[3 + i] * shift(carry, -by)
    carry = jnp.where(index < SUB - 1, shift(carry, -1), 0.0)
    for t in range(steps):
        put_strided(right, t, steps, rows[t] + back_ref[t] * carry)


def solve_rows(own, other, columns, factors):
    upper = lax.axis_index("lev") == 0
    half, width = own[0].shape
    depth = 2 * half
    for f in range(SOLVED):
        put(columns.at[f], depth, jnp.zeros((columns.shape[2] - depth, width), F32))
        put(columns.at[f], 0, jnp.where(upper, own[f], other[f]))
        put(columns.at[f], half, jnp.where(upper, other[f], own[f]))
    for f in range(SOLVED):
        solve(columns.at[f], factors)
    halves = [(get(columns.at[f], 0, half), get(columns.at[f], half, half)) for f in range(SOLVED)]
    return [jnp.where(upper, a, b) for a, b in halves], [jnp.where(upper, b, a) for a, b in halves]


def near_kernel(core, near_ref, start_ref, take_ref, gather_ref, out_ref):
    rows = slice(0, near_ref.shape[0])

    @pl.when(lax.axis_index("sec") == core)
    def _():
        out_ref[rows, :] = start_ref[rows, :] + take_ref[rows, :] * side_share(near_ref[...], gather_ref, 0)
        if near_ref.shape[0] < out_ref.shape[0]:
            rest = slice(up(near_ref.shape[0], TILE), out_ref.shape[0])
            out_ref[rest, :] = start_ref[rest, :]


def early_kernel(far_ref, start_ref, take_ref, gather_ref, value_ref):
    rows = slice(0, far_ref.shape[0])

    @pl.when(lax.axis_index("sec") == 1)
    def _():
        value_ref[...] = start_ref[rows, :] + take_ref[rows, :] * side_share(far_ref[...], gather_ref, 1)


def first_kernel(
    dfar_ref, dnear_ref, early_ref, pack_ref, start_ref, lagged_ref, take_ref, gather_ref, *rest
):
    factors, (*full_refs, short_ref, smooth, columns) = rest[:6], rest[6:]
    _, half, width = pack_ref.shape
    own = lagged_ref.shape[0]
    total = short_ref.shape[0]
    base = up(own, TILE)
    first = up(SOLVED * half, CHUNK)
    piece = full_refs[0].shape[0]

    def store(low, value):
        for i, (start, stop) in enumerate(spans(0, piece * PIECES, piece)):
            a, b = max(low, start), min(low + value.shape[0], stop)
            if a < b:
                full_refs[i][a - start : b - start, :] = value[a - low : b - low]

    def emit(low, value):
        short_ref[low : low + value.shape[0], :] = value.astype(BF16)
        store(low, value)

    @pl.when(lax.axis_index("sec") == 1)
    def _():
        others = slice(base, base + SOLVED * half)
        smooth[others, :] = start_ref[others, :] + take_ref[others, :] * sides_share(
            dnear_ref[...], dfar_ref[...], gather_ref
        )
        smooth[0:first, :] = early_ref[0:first, :]
        part = lambda low: [smooth[low + f * half : low + (f + 1) * half, :] for f in range(SOLVED)]
        mine, theirs = solve_rows(part(0), part(base), columns, factors)
        for low, high in spans(first, own, CHUNK):
            emit(low, early_ref[low:high, :])
        for f in range(SOLVED):
            smooth[f * half : (f + 1) * half, :] = mine[f]
            smooth[base + f * half : base + (f + 1) * half, :] = theirs[f] + pack_ref[SOLVED + f].astype(F32)
        for low, high in spans(0, first, CHUNK):
            lag = lagged_ref[low:high, :].astype(F32)
            if high > SOLVED * half:
                lag = jnp.where(lax.broadcasted_iota(jnp.int32, lag.shape, 0) < SOLVED * half - low, lag, 0.0)
            emit(low, smooth[low:high, :] + lag)
        for low, high in spans(base, total, CHUNK):
            emit(low, smooth[low:high, :])
        store(total, pack_ref[2 * SOLVED].astype(F32))


def last_kernel(far_ref, brief_ref, start_ref, lagged_ref, mask_ref, rates_ref, take_ref, gather_ref, *rest):
    factors, (out_ref, smooth, columns, held, sems) = rest[:6], rest[6:]
    own, width = lagged_ref.shape
    fields = rates_ref.shape[0]
    half = own // fields
    base = up(own, TILE)
    total = far_ref.shape[0]
    parts = width // LANES
    first = up(SOLVED * half, CHUNK)

    def send(low, high, sem):
        rows = pl.ds(low * parts, (high - low) * parts)
        return pltpu.make_async_copy(held.at[rows], out_ref.at[rows], sems.at[sem])

    @pl.when(lax.axis_index("sec") == 0)
    def _():
        def smoothed(low, high):
            rows = slice(low, high)
            return start_ref[rows, :] + take_ref[rows, :] * side_share(far_ref[rows, :], gather_ref, 1)

        smooth[0:first, :] = smoothed(0, first)
        smooth[base:total, :] = smoothed(base, total)
        part = lambda low: [smooth[low + f * half : low + (f + 1) * half, :] for f in range(SOLVED)]
        mine, _ = solve_rows(part(0), part(base), columns, factors)
        put_rows(held, first, parts, smoothed(first, own))
        send(first, own, 0).start()
        for f in range(SOLVED):
            smooth[f * half : (f + 1) * half, :] = mine[f]
        for low, high in spans(0, first, CHUNK):
            lag = lagged_ref[low:high, :].astype(F32)
            if high > SOLVED * half:
                lag = jnp.where(lax.broadcasted_iota(jnp.int32, lag.shape, 0) < SOLVED * half - low, lag, 0.0)
            put_rows(held, low, parts, smooth[low:high, :] + lag)

    @pl.when(lax.axis_index("sec") == 1)
    def _():
        for low, high in spans(0, base, CHUNK):
            smooth[low:high, :] = brief_ref[low:high, :].astype(F32)

        def keep(f, value):
            put_rows(held, f * half, parts, value)

        relax = lambda f: rates_ref[f : f + 1, :]
        tendency(lambda f: smooth[f * half : (f + 1) * half, :], fields, mask_ref[1:2, :], relax, keep)
        send(first, own, 0).start()

    send(0, first, 1).start()
    send(first, own, 0).wait()
    send(0, first, 1).wait()


def cost(us):
    return pl.CostEstimate(flops=int(us * 1e9), transcendentals=0, bytes_accessed=0)


def params(mib):
    return pltpu.CompilerParams(vmem_limit_bytes=mib << 20)


def shards(sections, neighbours, edge_weight, field_diff, vert_coef, relax_rate, precip_mask):
    _, fields, half, width = sections.shape
    shape = jax.ShapeDtypeStruct
    steps = up(up(2 * half, SUB) // SUB, 4)
    depth = steps * SUB
    own = fields * half
    total = up(own, TILE) + up(SOLVED * half, TILE)
    piece = up(-(-(total + half) // PIECES), SUB)

    mine = strips(sections)
    shorts = [shape((own, width), BF16), shape((SOLVED * half, width), BF16)]
    short, head = lax.cond(
        lax.axis_index("sec") == 0,
        pl.pallas_call(
            shorten_kernel,
            out_shape=shorts,
            in_specs=[ANY],
            out_specs=[VMEM] * 2,
            scratch_shapes=[pltpu.VMEM(mine.shape, F32), pltpu.SemaphoreType.DMA((2,))],
            compiler_params=params(4),
            cost_estimate=cost(3),
        ),
        lambda _: pl.pallas_call(
            nothing_kernel, out_shape=shorts, out_specs=[VMEM] * 2, compiler_params=params(4), cost_estimate=cost(3)
        )(),
        mine,
    )
    back = (1, 0, same, 0)
    state = route(mine, (0, 1, same, 0), back)
    near_rows = route(short, (0, 1, near, 0), back)
    far_rows = route(short, (0, 1, far, 0), back)
    dnear = route(head, (0, 1, near, 1), back)
    dfar = route(head, (0, 1, far, 1), back)

    pack = pl.pallas_call(
        pack_kernel,
        out_shape=shape((2 * SOLVED + 1, half, width), BF16),
        in_specs=[VMEM] * 3,
        out_specs=VMEM,
        compiler_params=params(4),
        cost_estimate=cost(0.01),
    )(head, state, vert_coef)
    pack = route(pack, (0, 1, same, 1), back)

    gather, lagged, rates, keep, take = pl.pallas_call(
        prepare_kernel,
        out_shape=[
            shape((7 * width, width), BF16),
            shape((own, width), BF16),
            shape((fields, width), F32),
            shape((total, width), F32),
            shape((total, width), F32),
        ],
        in_specs=[VMEM] * 5 + [SMEM] * 2,
        out_specs=[VMEM] * 5,
        scratch_shapes=[pltpu.VMEM((own, width), F32)] * 2,
        compiler_params=params(8),
        cost_estimate=cost(0.01),
    )(mine, short, neighbours, edge_weight, precip_mask, relax_rate, field_diff)

    chunk = shape((steps, SUB, width), F32)

    def ready(kernel, *operands):
        start, *factors = pl.pallas_call(
            kernel,
            out_shape=[chunk] * 5 + [shape((6, SUB, width), F32), shape((total, width), F32)],
            in_specs=[VMEM] * len(operands),
            out_specs=[VMEM] * 7,
            scratch_shapes=[
                pltpu.VMEM((total, width), F32),
                pltpu.VMEM((2 * half, width), F32),
                pltpu.VMEM((width // LANES, depth + 2 * SUB, LANES), F32),
                pltpu.VMEM((width // LANES, depth, LANES), F32),
            ],
            compiler_params=params(16),
            cost_estimate=cost(0),
        )(*operands)[::-1]
        return start, factors[::-1]

    def with_near(core, rows, start):
        return pl.pallas_call(
            functools.partial(near_kernel, core),
            out_shape=shape((total, width), F32),
            in_specs=[VMEM] * 4,
            out_specs=VMEM,
            compiler_params=params(8),
            cost_estimate=cost(0),
        )(rows, start, take, gather)

    start, factors = ready(ready_first_kernel, vert_coef, pack, state, lagged, keep, take, gather)

    start = with_near(1, near_rows, start)

    scratch = [pltpu.VMEM((total, width), F32), pltpu.VMEM((SOLVED, width // LANES, depth, LANES), F32)]
    early = pl.pallas_call(
        early_kernel,
        out_shape=shape((own, width), F32),
        in_specs=[VMEM] * 4,
        out_specs=VMEM,
        compiler_params=params(8),
        cost_estimate=cost(0),
    )(far_rows, start, take, gather)
    *full, brief = pl.pallas_call(
        first_kernel,
        out_shape=[shape((piece, width), F32)] * PIECES + [shape((total, width), BF16)],
        in_specs=[VMEM] * 14,
        out_specs=[VMEM] * (PIECES + 1),
        scratch_shapes=scratch,
        compiler_params=params(24),
    )(dfar, dnear, early, pack, start, lagged, take, gather, *factors)

    near_rows = route(brief, (1, 0, near, 0))
    far_rows = route(brief, (1, 0, far, 0), (0, 1, same, 0))
    pieces = [route(part, back, (0, 1, same, 0)) for part in full]
    start, factors = ready(
        functools.partial(ready_last_kernel, total), vert_coef, lagged, keep, take, gather, *pieces
    )
    start = with_near(0, near_rows, start)
    out = pl.pallas_call(
        last_kernel,
        out_shape=shape(mine.shape, F32),
        in_specs=[VMEM] * 14,
        out_specs=ANY,
        scratch_shapes=scratch + [pltpu.VMEM(mine.shape, F32), pltpu.SemaphoreType.DMA((2,))],
        compiler_params=params(24),
    )(far_rows, brief, start, lagged, precip_mask, rates, take, gather, *factors)
    return out.reshape(sections.shape)


def solution(mesh):
    return jax.shard_map(
        shards,
        mesh=mesh,
        in_specs=(
            P("sec", None, "lev", "dom"),
            P(None, "dom"),
            P(None, "dom"),
            P(),
            P("lev", "dom"),
            P(),
            P(None, "dom"),
        ),
        out_specs=P("sec", None, "lev", "dom"),
        check_vma=False,
    )
```
